32 devices in a mesh: tile: 2 (over x), expert: 16 (over z, y, core).
Axes of the slice: x: 2, y: 2, z: 4, core: 2. Of those that a mesh axis runs over, the one named last changes fastest.
Arguments:
- patches: bfloat16 [16, 8, 32, 1152], P('expert', 'tile'), may hold values from -6 to 6
- norm1_gain: float32 [1152], replicated, may hold values from 0.1 to 1.9
- qkv_weight: bfloat16 [1152, 3, 1152], P(None, None, 'tile'), may hold values from -8 to 8
- qkv_bias: float32 [3, 1152], P(None, 'tile'), may hold values from -3 to 3
- out_weight: bfloat16 [1152, 1152], P('tile'), may hold values from -0.1875 to 0.1875
- out_bias: float32 [1152], replicated, may hold values from -3 to 3
- norm2_gain: float32 [1152], replicated, may hold values from 0.1 to 1.9
- proj_weight: bfloat16 [4608, 2048], P('expert', 'tile'), may hold values from -0.09375 to 0.09375
- moe_gain: float32 [2048], replicated, may hold values from 0.1 to 1.9
- expert_in: bfloat16 [16, 2048, 2, 1408], P('expert', None, None, 'tile'), may hold values from -0.125 to 0.125
- expert_out: bfloat16 [16, 1408, 2048], P('expert', 'tile'), may hold values from -0.15625 to 0.15625
- shared_in: bfloat16 [2048, 2, 1408], P(None, None, 'tile'), may hold values from -0.125 to 0.125
- shared_out: bfloat16 [1408, 2048], P('tile'), may hold values from -0.15625 to 0.15625
- routes: int32 [16, 4, 16, 6], P('expert'), may hold values from 0 to 15, all different within a row; in each aligned block of 32 rows (0 to 31, 32 to 63, ..., all dimensions but the last counted through in order) at most 24 rows name the same one
- gates: float32 [16, 4, 16, 6], P('expert', 'tile'), may hold values from 0.1 to 1
Outputs:
- moe_tokens: bfloat16 [16, 4, 16, 2048], P('expert', 'tile')
The draws below stay inside these ranges and needn't reach their ends.
Inputs may be any that keep to these rules, and one draw needn't show every extreme that they name: `routes`: each merged token names 6 different experts. Flattening the merged tokens in the order page, row, column into aligned blocks of 32 (the merged tokens of one device), no expert is named more than 24 times in a block, a bound that some block reaches.
All inputs are finite; a program needn't handle non-finite values.
Results may differ from the reference program's by a relative error of at most 0.02.
Values may be sent and summed in bfloat16 or wider, within the bound.
No kernel may reach another device: no remote copies, remote signals or barrier semaphores. Data moves between devices by JAX's collectives and lax.ppermute only.
A program may use at most 128 MiB of HBM per device.

```python
import math
from functools import partial
import jax
import jax.numpy as jnp
import numpy as np
from jax import lax

HEADS = 16
HD = 72
DV = 1152
D = 2048
FF = 1408
SFF = 1408
TOP = 6
PCOLS = 32
PROWS = 8
PAGES = 16
MROWS = 4
MCOLS = 16
MTOK_DEV = 32
EXPERTS = 16
CAP = 24
SHARES = 2


def draw_qkv_weight(key, part):
    entries = jnp.clip(jax.random.normal(key, (DV, 3, DV), jnp.float32), -6.0, 6.0) * DV ** (-0.5)
    return entries.astype(jnp.bfloat16)


def block_scale(rng, dims, pieces, low, largest):
    def one(dim, blocks):
        steps = jax.random.uniform(jax.random.fold_in(jax.random.fold_in(rng, 6), dim), (blocks,), jnp.float32, low / len(pieces), largest / len(pieces))
        return jnp.repeat(jnp.exp(steps), dims[dim] // blocks).reshape((-1,) + (1,) * (len(dims) - dim - 1))

    level = one(*pieces[0])
    for cut in pieces[1:]:
        level = level * one(*cut)
    return level


def routed_block(rng, own, number, rows, number_of, top, reach, slope):
    sequence = jax.random.permutation(rng, number_of)
    crowded, usual = load_shares(number_of, rows * top, reach, slope, True), load_shares(number_of, rows * top, reach, slope, False)
    places = jnp.arange(number_of)

    def named(tallies, turn):
        used = int((tallies > 0).sum())
        fixed = max(1, used // 4)
        shifted = fixed + (places - fixed + turn * (used - fixed)) % max(1, number_of - fixed)
        return jnp.zeros((number_of,), jnp.int32).at[sequence[jnp.where(places < fixed, places, shifted)]].set(jnp.asarray(tallies, jnp.int32))

    tallies = jnp.where(number % 4 == 0, named(crowded, number // 4), named(usual, number - number // 4 - 1))
    mixed = jax.random.permutation(jax.random.fold_in(own, 3), number_of)
    donor, taker = mixed[0:number_of // 2 * 2:2], mixed[1:number_of // 2 * 2:2]
    slack = jnp.minimum(tallies[donor] - 1, reach - tallies[taker]) // 2
    slack = jnp.where((donor == sequence[0]) | (taker == sequence[0]) | (tallies[taker] == 0), 0, jnp.maximum(slack, 0))
    shifted = jax.random.randint(jax.random.fold_in(own, 4), (number_of // 2,), 0, 1 << 20) % (slack + 1)
    tallies = tallies.at[donor].add(-shifted).at[taker].add(shifted)
    members = jnp.searchsorted(jnp.cumsum(tallies), jnp.arange(rows * top), side="right").astype(jnp.int32)
    table = members.reshape(top, rows).T
    table = table[jax.random.permutation(jax.random.fold_in(own, 1), rows)]
    turn = jax.random.randint(jax.random.fold_in(own, 2), (rows, 1), 0, top)
    return jnp.take_along_axis(table, (jnp.arange(top)[None, :] + turn) % top, axis=1)


def load_shares(amount, total, bound, slope, full):
    weights = [(1 << 20) // math.isqrt(grade ** slope) + 1 for grade in range(1, amount + 1)]
    largest = bound if full else min(bound, max(-(-total // amount), total * weights[0] // sum(weights)))
    least = 1 if total - largest >= amount - 1 else 0
    counts, spare = [largest] + [least] * (amount - 1), total - largest - least * (amount - 1)
    while spare > 0:
        candidates = [i for i in range(1, amount) if counts[i] < largest] or [i for i in range(1, amount) if counts[i] < bound]
        pool, remaining = sum([weights[i] for i in candidates]), spare
        for i in candidates:
            extra = min(bound - counts[i], max(1, remaining * weights[i] // pool), spare)
            counts[i] = counts[i] + extra
            spare = spare - extra
    return np.array(counts)


def normal_values(stream_key, extent, deviation, bound, cuts=(), kind=jnp.bfloat16):
    gain = block_scale(stream_key, extent, cuts, -0.22, 0.18) if cuts else 1.0
    values = jax.random.normal(stream_key, extent, jnp.float32) * deviation * gain
    return jnp.minimum(jnp.maximum(values, -bound), bound).astype(kind)


def setup_inputs(seed: int = 0) -> dict:
    keys = jax.random.split(jax.random.key(seed), 16)
    patches = normal_values(keys[0], (PAGES, PROWS, PCOLS, DV), 1.0, 6.0, ((0, 16), (1, 2)))
    norm1_gain = jnp.clip(1.0 + 0.18 * jax.random.normal(keys[1], (DV,), jnp.float32), 0.1, 1.9)
    qkv_weight = draw_qkv_weight(jax.random.fold_in(keys[15], 71), 0)
    qkv_bias = normal_values(keys[3], (3, DV), 0.5, 3.0, ((1, 2),), jnp.float32)
    out_weight = normal_values(keys[4], (DV, DV), DV ** -0.5, 0.1875, ((0, 2),))
    out_bias = normal_values(keys[5], (DV,), 0.5, 3.0, (), jnp.float32)
    norm2_gain = jnp.clip(1.0 + 0.18 * jax.random.normal(keys[6], (DV,), jnp.float32), 0.1, 1.9)
    proj_weight = normal_values(keys[7], (4 * DV, D), (4 * DV) ** -0.5, 0.09375, ((0, 16), (1, 2)))
    moe_gain = jnp.clip(1.0 + 0.18 * jax.random.normal(keys[8], (D,), jnp.float32), 0.1, 1.9)
    expert_in = normal_values(keys[9], (EXPERTS, D, 2, FF), D ** -0.5, 0.125, ((0, 16), (3, 2)))
    expert_out = normal_values(keys[10], (EXPERTS, FF, D), FF ** -0.5, 0.15625, ((0, 16), (1, 2)))
    shared_in = normal_values(keys[11], (D, 2, SFF), D ** -0.5, 0.125, ((2, 2),))
    shared_out = normal_values(keys[12], (SFF, D), SFF ** -0.5, 0.15625, ((0, 2),))
    routes_keys = jax.random.split(jax.random.fold_in(keys[13], 1), PAGES * MROWS * MCOLS // MTOK_DEV)
    routes_turns = jax.random.permutation(jax.random.fold_in(keys[13], 3), PAGES * MROWS * MCOLS // MTOK_DEV)
    routes = jax.vmap(lambda own, number: routed_block(jax.random.fold_in(keys[13], 2), own, number, MTOK_DEV, EXPERTS, TOP, CAP, 2))(routes_keys, routes_turns).reshape((PAGES, MROWS, MCOLS, TOP))
    gates = jnp.clip(jnp.exp(math.log(1.0) - 2.3025851 * jax.random.uniform(keys[14], (PAGES, MROWS, MCOLS, TOP), jnp.float32) ** block_scale(keys[14], (PAGES, MROWS, MCOLS, TOP), ((0, 16), (1, 2)), -0.2, 0.2)), 0.1, 1.0)
    return {"patches": patches, "norm1_gain": norm1_gain, "qkv_weight": qkv_weight, "qkv_bias": qkv_bias, "out_weight": out_weight, "out_bias": out_bias, "norm2_gain": norm2_gain, "proj_weight": proj_weight, "moe_gain": moe_gain, "expert_in": expert_in, "expert_out": expert_out, "shared_in": shared_in, "shared_out": shared_out, "routes": routes, "gates": gates}


norm_eps = 1e-06
rope_base = 10000.0

def layer_norm(values, gain_vec):
    centre = values - lax.optimization_barrier(jnp.mean(values, axis=-1, keepdims=True))
    spread = lax.optimization_barrier(jnp.mean(centre * centre, axis=-1, keepdims=True))
    return centre * lax.rsqrt(spread + norm_eps) * gain_vec

def rms_norm(values, gain_vec):
    return values * lax.rsqrt(lax.optimization_barrier(jnp.mean(values * values, axis=-1, keepdims=True)) + norm_eps) * gain_vec

def rope_tables(positions, columns, head_size):
    quarter = head_size // 4
    inverse = jnp.exp(jnp.arange(quarter).astype(jnp.float32) * (-math.log(rope_base) / quarter))
    row_angle = (positions // columns).astype(jnp.float32)[:, None] * inverse[None, :]
    col_angle = (positions % columns).astype(jnp.float32)[:, None] * inverse[None, :]
    return (jnp.cos(row_angle), jnp.sin(row_angle), jnp.cos(col_angle), jnp.sin(col_angle))

def rotate(values, tables):
    cos_row, sin_row, cos_col, sin_col = tables
    quarter = values.shape[-1] // 4
    row_a = values[..., :quarter]
    row_b = values[..., quarter:2 * quarter]
    col_a = values[..., 2 * quarter:3 * quarter]
    col_b = values[..., 3 * quarter:]
    return jnp.concatenate([row_a * cos_row[:, None] - row_b * sin_row[:, None], row_b * cos_row[:, None] + row_a * sin_row[:, None], col_a * cos_col[:, None] - col_b * sin_col[:, None], col_b * cos_col[:, None] + col_a * sin_col[:, None]], axis=-1)

def attend(query_rows, key_rows, value_rows, divisor):
    count = query_rows.shape[0]
    width = min(count, 512)
    blocks = query_rows.reshape(count // width, width, query_rows.shape[1], query_rows.shape[2])

    def one_block(block):
        scores = jnp.einsum('qhd,khd->hqk', block.astype(jnp.float32), key_rows.astype(jnp.float32)) / divisor
        weights = jax.nn.softmax(scores, axis=-1).astype(jnp.bfloat16)
        return jnp.einsum('hqk,khd->qhd', weights.astype(jnp.float32), value_rows.astype(jnp.float32)).astype(jnp.bfloat16)
    return lax.map(one_block, blocks).reshape(count, -1)

def block_slots(block_routes, experts_count, capacity):
    picks = block_routes.reshape(-1)
    onehot = (picks[:, None] == jnp.arange(experts_count).astype(jnp.int32)[None, :]).astype(jnp.int32)
    earlier = jnp.cumsum(onehot, axis=0).astype(jnp.int32) - onehot
    ranks = lax.optimization_barrier(jnp.sum(earlier * onehot, axis=1)).astype(jnp.int32)
    owners_flat = (jnp.arange(picks.shape[0]) // block_routes.shape[1]).astype(jnp.int32)
    table = jnp.full((experts_count * capacity,), -1, dtype=jnp.int32).at[picks * capacity + ranks].set(owners_flat)
    return (ranks.reshape(block_routes.shape), table.reshape(experts_count, capacity))

def reference(patches, norm1_gain, qkv_weight, qkv_bias, out_weight, out_bias, norm2_gain, proj_weight, moe_gain, expert_in, expert_out, shared_in, shared_out, routes, gates):
    count = PROWS * PCOLS

    def page_merge(single_page):
        inputs = single_page.reshape(count, DV).astype(jnp.float32)
        normed = layer_norm(inputs, norm1_gain).astype(jnp.bfloat16)
        mixed = jnp.dot(normed, qkv_weight.reshape(DV, 3 * DV), preferred_element_type=jnp.float32).reshape(count, 3, HEADS, HD)
        mixed = mixed + qkv_bias.reshape(1, 3, HEADS, HD)
        tables = rope_tables(jnp.arange(count).astype(jnp.int32), PCOLS, HD)
        query_rows = rotate(mixed[:, 0], tables).astype(jnp.bfloat16)
        key_rows = rotate(mixed[:, 1], tables).astype(jnp.bfloat16)
        value_rows = mixed[:, 2].astype(jnp.bfloat16)
        attended = attend(query_rows, key_rows, value_rows, math.sqrt(HD))
        hidden = inputs + jnp.dot(attended, out_weight, preferred_element_type=jnp.float32) + out_bias
        normed_out = layer_norm(hidden, norm2_gain).astype(jnp.bfloat16)
        windows = normed_out.reshape(PROWS // 2, 2, PCOLS // 2, 2, DV).transpose(0, 2, 1, 3, 4)
        return windows.reshape(PROWS // 2 * (PCOLS // 2), 4 * DV)
    merged = lax.map(page_merge, patches).reshape(-1, 4 * DV)
    tokens_moe = jnp.dot(merged, proj_weight, preferred_element_type=jnp.float32).astype(jnp.bfloat16)
    moe_in = rms_norm(tokens_moe.astype(jnp.float32), moe_gain).astype(jnp.bfloat16)
    total = tokens_moe.shape[0]
    blocks = total // MTOK_DEV
    block_routes = routes.reshape(blocks, MTOK_DEV, TOP)
    ranks, owners = jax.vmap(partial(block_slots, experts_count=EXPERTS, capacity=CAP))(block_routes)
    base_rows = (jnp.arange(blocks) * MTOK_DEV).astype(jnp.int32)[:, None]
    share = FF // SHARES

    def run_expert(expert_id):
        table = owners[:, expert_id, :]
        used = table >= 0
        rows_index = jnp.where(used, base_rows + table, 0)
        inputs = jnp.where(used[..., None], moe_in[rows_index], jnp.zeros((), moe_in.dtype)).reshape(-1, D)
        gated = jnp.dot(inputs, expert_in[expert_id].reshape(D, 2 * FF), preferred_element_type=jnp.float32).reshape(-1, 2, FF)
        hidden = (jax.nn.silu(gated[:, 0]) * gated[:, 1]).astype(jnp.bfloat16)
        total_out = jnp.zeros((hidden.shape[0], D), jnp.float32)
        for portion in range(SHARES):
            partial_out = jnp.dot(hidden[:, portion * share:(portion + 1) * share], expert_out[expert_id, portion * share:(portion + 1) * share], preferred_element_type=jnp.float32)
            total_out = total_out + lax.optimization_barrier(partial_out.astype(jnp.bfloat16)).astype(jnp.float32)
        return total_out.astype(jnp.bfloat16).reshape(blocks, CAP, D)
    results = lax.map(run_expert, jnp.arange(EXPERTS).astype(jnp.int32))
    flat_results = results.reshape(EXPERTS * blocks * CAP, D)
    block_ids = jnp.arange(blocks).astype(jnp.int32)[:, None, None]
    flat_index = ((block_routes * blocks + block_ids) * CAP + ranks).reshape(total, TOP)
    gate_rows = gates.reshape(total, TOP)
    routed = jnp.zeros((total, D), jnp.float32)
    for position in range(TOP):
        routed = routed + gate_rows[:, position:position + 1] * flat_results[flat_index[:, position]].astype(jnp.float32)
    shared_gated = jnp.dot(moe_in, shared_in.reshape(D, 2 * SFF), preferred_element_type=jnp.float32).reshape(total, 2, SFF)
    shared_hidden = (jax.nn.silu(shared_gated[:, 0]) * shared_gated[:, 1]).astype(jnp.bfloat16)
    shared_part = jnp.dot(shared_hidden, shared_out, preferred_element_type=jnp.float32)
    output = tokens_moe.astype(jnp.float32) + shared_part + routed
    return output.astype(jnp.bfloat16).reshape(PAGES, MROWS, MCOLS, D)
```

```python
from functools import partial
import math

import jax
import jax.numpy as jnp
from jax import lax
from jax.sharding import PartitionSpec as P

HD = 72


norm_eps = 1e-06
rope_base = 10000.0


def layer_norm(values, gain_vec):
    centre = values - jnp.mean(values, axis=-1, keepdims=True)
    spread = jnp.mean(centre * centre, axis=-1, keepdims=True)
    return centre * lax.rsqrt(spread + norm_eps) * gain_vec


def rms_norm(values, gain_vec):
    return (
        values * lax.rsqrt(jnp.mean(values * values, axis=-1, keepdims=True) + norm_eps) * gain_vec
    )


def rope_tables(positions, columns, head_size):
    quarter = head_size // 4
    inverse = jnp.exp(jnp.arange(quarter).astype(jnp.float32) * (-math.log(rope_base) / quarter))
    row_angle = (positions // columns).astype(jnp.float32)[:, None] * inverse[None, :]
    col_angle = (positions % columns).astype(jnp.float32)[:, None] * inverse[None, :]
    return (jnp.cos(row_angle), jnp.sin(row_angle), jnp.cos(col_angle), jnp.sin(col_angle))


def rotate(values, tables):
    cos_row, sin_row, cos_col, sin_col = tables
    quarter = values.shape[-1] // 4
    row_a = values[..., :quarter]
    row_b = values[..., quarter : 2 * quarter]
    col_a = values[..., 2 * quarter : 3 * quarter]
    col_b = values[..., 3 * quarter :]
    return jnp.concatenate(
        [
            row_a * cos_row[:, None] - row_b * sin_row[:, None],
            row_b * cos_row[:, None] + row_a * sin_row[:, None],
            col_a * cos_col[:, None] - col_b * sin_col[:, None],
            col_b * cos_col[:, None] + col_a * sin_col[:, None],
        ],
        axis=-1,
    )


def attend(query_rows, key_rows, value_rows, divisor):
    count = query_rows.shape[0]
    width = min(count, 512)
    blocks = query_rows.reshape(count // width, width, query_rows.shape[1], query_rows.shape[2])

    def one_block(block):
        scores = (
            jnp.einsum("qhd,khd->hqk", block, key_rows, preferred_element_type=jnp.float32)
            / divisor
        )
        weights = jax.nn.softmax(scores, axis=-1).astype(jnp.bfloat16)
        return jnp.einsum(
            "hqk,khd->qhd", weights, value_rows, preferred_element_type=jnp.float32
        ).astype(jnp.bfloat16)

    return lax.map(one_block, blocks).reshape(count, -1)


def block_slots(block_routes, experts_count, capacity):
    picks = block_routes.reshape(-1)
    onehot = (picks[:, None] == jnp.arange(experts_count)[None, :]).astype(jnp.int32)
    earlier = jnp.cumsum(onehot, axis=0) - onehot
    ranks = jnp.sum(earlier * onehot, axis=1)
    owners_flat = jnp.arange(picks.shape[0]) // block_routes.shape[1]
    table = (
        jnp.full((experts_count * capacity,), -1, dtype=jnp.int32)
        .at[picks * capacity + ranks]
        .set(owners_flat)
    )
    return (ranks.reshape(block_routes.shape), table.reshape(experts_count, capacity))


def per_device_slots(
    patches,
    norm1_gain,
    qkv_weight,
    qkv_bias,
    out_weight,
    out_bias,
    norm2_gain,
    proj_weight,
    moe_gain,
    expert_in,
    expert_out,
    shared_in,
    shared_out,
    routes,
    gates,
):
    tiles = lax.axis_size("tile")
    experts_count = lax.axis_size("expert")
    tile_id = lax.axis_index("tile")
    row_count = patches.shape[1]
    columns = patches.shape[2]
    width_vit = patches.shape[3]
    local_rows = row_count * columns
    inputs = patches.reshape(local_rows, width_vit).astype(jnp.float32)
    normed = layer_norm(inputs, norm1_gain).astype(jnp.bfloat16)
    heads_here = qkv_weight.shape[2] // HD
    qkv_flat = qkv_weight.reshape(width_vit, -1)
    bias_rows = qkv_bias.reshape(1, 3, heads_here, HD)
    piece = lax.all_gather(normed, "tile", axis=0, tiled=True)
    mixed = (
        jnp.dot(piece, qkv_flat, preferred_element_type=jnp.float32).reshape(
            piece.shape[0], 3, heads_here, HD
        )
        + bias_rows
    )
    tables = rope_tables(jnp.arange(piece.shape[0]), columns, HD)
    page_qkv = jnp.stack(
        [rotate(mixed[:, 0], tables), rotate(mixed[:, 1], tables), mixed[:, 2]], axis=1
    ).astype(jnp.bfloat16)
    attended = attend(page_qkv[:, 0], page_qkv[:, 1], page_qkv[:, 2], math.sqrt(HD))
    mixed_heads = lax.psum_scatter(
        jnp.dot(attended, out_weight, preferred_element_type=jnp.float32).astype(jnp.bfloat16),
        "tile",
        scatter_dimension=0,
        tiled=True,
    ).astype(jnp.float32)
    hidden = inputs + mixed_heads + out_bias
    normed_out = layer_norm(hidden, norm2_gain).astype(jnp.bfloat16)
    merged = (
        normed_out.reshape(row_count // 2, 2, columns // 2, 2, width_vit)
        .transpose(0, 2, 1, 3, 4)
        .reshape(-1, 4 * width_vit)
    )
    merged_count = merged.shape[0]
    group_merged = lax.all_gather(merged, "tile", axis=0, tiled=True)
    projected = jnp.dot(
        group_merged,
        lax.all_gather(proj_weight, "expert", axis=0, tiled=True),
        preferred_element_type=jnp.float32,
    ).astype(jnp.bfloat16)
    tokens_moe = lax.all_to_all(projected, "tile", split_axis=0, concat_axis=1, tiled=True)
    width_moe = tokens_moe.shape[1]
    moe_in = rms_norm(tokens_moe.astype(jnp.float32), moe_gain).astype(jnp.bfloat16)
    group_in = lax.all_gather(moe_in, "tile", axis=0, tiled=True)
    shared_gated = jnp.dot(
        group_in, shared_in.reshape(width_moe, -1), preferred_element_type=jnp.float32
    ).reshape(group_in.shape[0], 2, -1)
    shared_hidden = (jax.nn.silu(shared_gated[:, 0]) * shared_gated[:, 1]).astype(jnp.bfloat16)
    shared_part = lax.psum_scatter(
        jnp.dot(shared_hidden, shared_out, preferred_element_type=jnp.float32).astype(jnp.bfloat16),
        "tile",
        scatter_dimension=0,
        tiled=True,
    ).astype(jnp.float32)
    top_count = routes.shape[-1]
    capacity = max(2, min(merged_count, 2 * merged_count * top_count // experts_count))
    group_routes = routes.reshape(tiles, merged_count, top_count)
    group_ranks, group_owners = jax.vmap(
        partial(block_slots, experts_count=experts_count, capacity=capacity)
    )(group_routes)
    own_routes = lax.dynamic_index_in_dim(group_routes, tile_id, 0, keepdims=False)
    own_ranks = lax.dynamic_index_in_dim(group_ranks, tile_id, 0, keepdims=False)
    empty_value = jnp.zeros((), jnp.bfloat16)
    table = lax.dynamic_index_in_dim(group_owners, tile_id, 0, keepdims=False)
    used = table >= 0
    outgoing = jnp.where(used[..., None], moe_in[jnp.where(used, table, 0)], empty_value)
    received = lax.all_to_all(outgoing, "expert", split_axis=0, concat_axis=0, tiled=True)
    arrived = lax.all_gather(received[:, None], "tile", axis=1, tiled=True)
    slot_rows = arrived.reshape(-1, width_moe)
    gated = jnp.dot(
        slot_rows, expert_in.reshape(width_moe, -1), preferred_element_type=jnp.float32
    ).reshape(slot_rows.shape[0], 2, -1)
    expert_hidden = (jax.nn.silu(gated[:, 0]) * gated[:, 1]).astype(jnp.bfloat16)
    partial_out = (
        jnp.dot(
            expert_hidden,
            expert_out.reshape(expert_hidden.shape[1], width_moe),
            preferred_element_type=jnp.float32,
        )
        .astype(jnp.bfloat16)
        .reshape(arrived.shape)
    )
    came_back = lax.all_to_all(partial_out, "expert", split_axis=0, concat_axis=0, tiled=True)
    returned = lax.psum_scatter(
        came_back.astype(jnp.float32).astype(jnp.bfloat16), "tile", scatter_dimension=1, tiled=True
    )
    results_flat = returned.reshape(experts_count * capacity, width_moe)
    pick_index = own_routes * capacity + own_ranks
    gate_rows = gates.reshape(merged_count, top_count)
    routed = jnp.zeros((merged_count, width_moe), jnp.float32)
    for position in range(top_count):
        routed = routed + gate_rows[:, position : position + 1] * results_flat[
            pick_index[:, position]
        ].astype(jnp.float32)
    output = tokens_moe.astype(jnp.float32) + shared_part + routed
    return output.astype(jnp.bfloat16).reshape(1, row_count // 2, columns // 2, width_moe)


def near_shift(values, grid, moved):
    tiles, outer, inner, cores = grid
    pairs = []
    for source in range(tiles * outer * inner * cores):
        place, rest = [], source
        for size in reversed(grid):
            place.append(rest % size)
            rest //= size
        target = 0
        for spot, size, step in zip(reversed(place), grid, moved):
            target = target * size + (spot + step) % size
        pairs.append((source, target))
    return lax.ppermute(values, ("tile", "expert"), pairs)


def rope_tables_at(rows, columns, head_size):
    quarter = head_size // 4
    inverse = jnp.exp(jnp.arange(quarter).astype(jnp.float32) * (-math.log(rope_base) / quarter))
    row_angle = rows.astype(jnp.float32)[:, None] * inverse[None, :]
    col_angle = columns.astype(jnp.float32)[:, None] * inverse[None, :]
    return (jnp.cos(row_angle), jnp.sin(row_angle), jnp.cos(col_angle), jnp.sin(col_angle))


def attend_rows(query_rows, key_rows, value_rows, divisor):
    scores = (
        jnp.einsum("qhd,khd->hqk", query_rows, key_rows, preferred_element_type=jnp.float32)
        / divisor
    )
    weights = jax.nn.softmax(scores, axis=-1).astype(jnp.bfloat16)
    return (
        jnp.einsum("hqk,khd->qhd", weights, value_rows, preferred_element_type=jnp.float32)
        .astype(jnp.bfloat16)
        .reshape(query_rows.shape[0], -1)
    )


def per_device_near(
    patches,
    norm1_gain,
    qkv_weight,
    qkv_bias,
    out_weight,
    out_bias,
    norm2_gain,
    proj_weight,
    moe_gain,
    expert_in,
    expert_out,
    shared_in,
    shared_out,
    routes,
    gates,
):
    experts_count = lax.axis_size("expert")
    outer = experts_count // 4
    grid = (2, outer, 2, 2)
    shift = partial(near_shift, grid=grid)
    tile_id = lax.axis_index("tile")
    expert_id = lax.axis_index("expert")
    outer_id, inner_id, core_id = expert_id // 4, (expert_id // 2) % 2, expert_id % 2
    row_count, columns, width_vit = patches.shape[1:]
    local_rows = row_count * columns
    token_count = local_rows // 4
    heads_here = qkv_weight.shape[2] // HD

    def by_tile(mine, other):
        first = tile_id == 0
        return jnp.where(first, mine, other), jnp.where(first, other, mine)

    own_patches = (
        patches.reshape(row_count // 2, 2, columns // 2, 2, width_vit)
        .transpose(1, 3, 0, 2, 4)
        .reshape(local_rows, width_vit)
    )
    other_patches = shift(own_patches, moved=(1, 0, 0, 0))

    proj_rows = [proj_weight] + [
        shift(proj_weight, moved=(0, step, 0, 0)) for step in range(1, outer)
    ]
    proj_pairs = [(rows, shift(rows, moved=(0, 0, 0, 1))) for rows in proj_rows]

    top_count = routes.shape[-1]
    page_routes = routes.reshape(2, token_count, top_count)
    own_routes = lax.dynamic_index_in_dim(page_routes, tile_id, 0, keepdims=False)
    own_gates = gates.reshape(token_count, top_count)
    dense_gates = jnp.sum(
        jnp.where(
            own_routes[:, :, None] == jnp.arange(experts_count)[None, None, :],
            own_gates[:, :, None],
            0.0,
        ),
        axis=1,
    )
    all_gates = lax.all_gather(dense_gates, ("expert", "tile"), axis=0, tiled=True)
    expert_gates = jnp.sum(
        jnp.where(jnp.arange(experts_count)[None, :] == expert_id, all_gates, 0.0), axis=1
    ).reshape(experts_count, 2 * token_count)

    place = jnp.arange(local_rows)
    pair_size = token_count
    parity, within = place // pair_size, place % pair_size
    patch_rows = 2 * (within // (columns // 2)) + parity // 2
    patch_cols = 2 * (within % (columns // 2)) + parity % 2

    def project_qkv(rows, tile):
        normed = layer_norm(rows.astype(jnp.float32), norm1_gain).astype(jnp.bfloat16)
        mixed = jnp.dot(
            normed, qkv_weight.reshape(width_vit, -1), preferred_element_type=jnp.float32
        ).reshape(rows.shape[0], 3, heads_here, HD) + qkv_bias.reshape(1, 3, heads_here, HD)
        tables = rope_tables_at(tile * row_count + patch_rows, patch_cols, HD)
        return (
            rotate(mixed[:, 0], tables).astype(jnp.bfloat16),
            rotate(mixed[:, 1], tables).astype(jnp.bfloat16),
            mixed[:, 2].astype(jnp.bfloat16),
        )

    own_query, own_key, own_value = project_qkv(own_patches, tile_id)
    other_query, other_key, other_value = project_qkv(other_patches, 1 - tile_id)
    keys = jnp.concatenate([own_key, other_key], axis=0)
    values = jnp.concatenate([own_value, other_value], axis=0)
    other_part = jnp.dot(
        attend_rows(other_query, keys, values, math.sqrt(HD)),
        out_weight,
        preferred_element_type=jnp.float32,
    ).astype(jnp.bfloat16)
    arrived_part = shift(other_part, moved=(1, 0, 0, 0))
    own_part = jnp.dot(
        attend_rows(own_query, keys, values, math.sqrt(HD)),
        out_weight,
        preferred_element_type=jnp.float32,
    )
    hidden = (
        own_patches.astype(jnp.float32) + own_part + arrived_part.astype(jnp.float32) + out_bias
    )
    normed_out = layer_norm(hidden, norm2_gain).astype(jnp.bfloat16)

    half = width_vit // 2
    low_half, high_half = normed_out[:, :half], normed_out[:, half:]
    kept = jnp.where(inner_id == 0, low_half, high_half).reshape(4, token_count, half)
    given = jnp.where(inner_id == 0, high_half, low_half).reshape(4, token_count, half)
    from_tile = shift(kept, moved=(1, 0, 0, 0))
    from_inner = shift(given, moved=(0, 0, 1, 0))
    from_both = shift(given, moved=(1, 0, 1, 0))
    features = jnp.concatenate(
        [*by_tile(kept, from_tile), *by_tile(from_inner, from_both)], axis=1
    )
    quarter = half // 2
    low_quarter, high_quarter = features[:, :, :quarter], features[:, :, quarter:]
    own_quarter = jnp.where(core_id == 0, low_quarter, high_quarter)
    other_quarter = jnp.where(core_id == 0, high_quarter, low_quarter)
    projected = 0.0
    for step, (own_rows, core_rows) in enumerate(proj_pairs):
        window = (outer_id - step) % outer
        for side, weight in ((own_quarter, own_rows), (other_quarter, core_rows)):
            projected = projected + jnp.dot(
                lax.dynamic_index_in_dim(side, window, 0, keepdims=False),
                weight,
                preferred_element_type=jnp.float32,
            )
    page_tokens = 2 * token_count
    inner_part = shift(projected[page_tokens:].astype(jnp.bfloat16), moved=(0, 0, 1, 0))
    tokens_half = (projected[:page_tokens] + inner_part.astype(jnp.float32)).astype(jnp.bfloat16)

    width_moe = 2 * tokens_half.shape[1]
    shared_flat = shared_in.reshape(width_moe, -1)
    expert_flat = expert_in.reshape(width_moe, -1)
    expert_back = expert_out.reshape(-1, width_moe)
    contributions = []
    residual = None
    halves_by_step = [tokens_half] + [
        shift(tokens_half, moved=(0, step, 0, 0)) for step in range(1, outer)
    ]
    for step, held in enumerate(halves_by_step):
        over_tile = shift(held, moved=(1, 0, 0, 0))
        over_inner = shift(held, moved=(0, 0, 1, 0))
        over_both = shift(held, moved=(1, 0, 1, 0))
        block = jnp.stack([held, over_tile, over_inner, over_both])
        core_block = shift(block, moved=(0, 0, 0, 1))
        mine = jnp.concatenate([block[0], block[2], core_block[0], core_block[2]], axis=0)
        tiles_other = jnp.concatenate([block[1], block[3], core_block[1], core_block[3]], axis=0)
        tokens = jnp.concatenate(by_tile(mine, tiles_other), axis=1)
        moe_in = rms_norm(tokens.astype(jnp.float32), moe_gain).astype(jnp.bfloat16)
        gated = jnp.dot(moe_in, expert_flat, preferred_element_type=jnp.float32)
        units = gated.shape[1] // 2
        hidden_units = (jax.nn.silu(gated[:, :units]) * gated[:, units:]).astype(jnp.bfloat16)
        result = jnp.dot(hidden_units, expert_back, preferred_element_type=jnp.float32)
        outer_page = (outer_id - step) % outer
        step_gates = jnp.concatenate(
            [
                lax.dynamic_index_in_dim(
                    expert_gates,
                    outer_page * 4 + (inner_id ^ other_inner) * 2 + (core_id ^ other_core),
                    0,
                    keepdims=False,
                )
                for other_core in range(2)
                for other_inner in range(2)
            ]
        )
        result = result * step_gates[:, None]
        if step == 0:
            residual = lax.dynamic_slice_in_dim(
                tokens[:page_tokens], tile_id * token_count, token_count, 0
            )
            shared_gated = jnp.dot(
                moe_in[:page_tokens], shared_flat, preferred_element_type=jnp.float32
            )
            shared_units = shared_gated.shape[1] // 2
            shared_hidden = (
                jax.nn.silu(shared_gated[:, :shared_units]) * shared_gated[:, shared_units:]
            ).astype(jnp.bfloat16)
            shared_part = jnp.dot(shared_hidden, shared_out, preferred_element_type=jnp.float32)
            result = jnp.concatenate(
                [result[:page_tokens] + shared_part, result[page_tokens:]], axis=0
            )
        contributions.append(result.astype(jnp.bfloat16))

    total = residual.astype(jnp.float32)
    for step, result in enumerate(contributions):
        across = shift(result[2 * page_tokens :], moved=(0, 0, 0, 1))
        summed = (
            (result[: 2 * page_tokens].astype(jnp.float32) + across.astype(jnp.float32))
            .astype(jnp.bfloat16)
            .reshape(2, 2, token_count, width_moe)
        )
        here, there = summed[:, 0], summed[:, 1]
        stays = jnp.where(tile_id == 0, here, there)
        leaves = jnp.where(tile_id == 0, there, here)
        step_total = (
            stays[0].astype(jnp.float32)
            + shift(leaves[0], moved=(1, 0, 0, 0)).astype(jnp.float32)
            + shift(stays[1], moved=(0, 0, 1, 0)).astype(jnp.float32)
            + shift(leaves[1], moved=(1, 0, 1, 0)).astype(jnp.float32)
        )
        if step:
            step_total = shift(
                step_total.astype(jnp.bfloat16), moved=(0, outer - step, 0, 0)
            ).astype(jnp.float32)
        total = total + step_total
    return total.astype(jnp.bfloat16).reshape(1, row_count // 2, columns // 2, width_moe)


def per_device(*arguments):
    experts_count = lax.axis_size("expert")
    if lax.axis_size("tile") == 2 and experts_count % 4 == 0 and experts_count == 16:
        return per_device_near(*arguments)
    return per_device_slots(*arguments)


def solution(mesh):
    placed = (
        P("expert", "tile", None, None),
        P(),
        P(None, None, "tile"),
        P(None, "tile"),
        P("tile", None),
        P(),
        P(),
        P("expert", "tile"),
        P(),
        P("expert", None, None, "tile"),
        P("expert", "tile", None),
        P(None, None, "tile"),
        P("tile", None),
        P("expert", None, None, None),
        P("expert", "tile", None, None),
    )
    return jax.shard_map(
        per_device,
        mesh=mesh,
        in_specs=placed,
        out_specs=P("expert", "tile", None, None),
        check_vma=False,
    )
```

```python
from functools import partial
import math

import jax
import jax.numpy as jnp
from jax import lax
from jax.experimental import pallas as pl
from jax.experimental.pallas import tpu as pltpu
from jax.sharding import PartitionSpec as P

HD = 72


norm_eps = 1e-06
rope_base = 10000.0


def layer_norm(values, gain_vec):
    centre = values - jnp.mean(values, axis=-1, keepdims=True)
    spread = jnp.mean(centre * centre, axis=-1, keepdims=True)
    return centre * lax.rsqrt(spread + norm_eps) * gain_vec


def rms_norm(values, gain_vec):
    return (
        values * lax.rsqrt(jnp.mean(values * values, axis=-1, keepdims=True) + norm_eps) * gain_vec
    )


def rope_tables(positions, columns, head_size):
    quarter = head_size // 4
    inverse = jnp.exp(jnp.arange(quarter).astype(jnp.float32) * (-math.log(rope_base) / quarter))
    row_angle = (positions // columns).astype(jnp.float32)[:, None] * inverse[None, :]
    col_angle = (positions % columns).astype(jnp.float32)[:, None] * inverse[None, :]
    return (jnp.cos(row_angle), jnp.sin(row_angle), jnp.cos(col_angle), jnp.sin(col_angle))


def rotate(values, tables):
    cos_row, sin_row, cos_col, sin_col = tables
    quarter = values.shape[-1] // 4
    row_a = values[..., :quarter]
    row_b = values[..., quarter : 2 * quarter]
    col_a = values[..., 2 * quarter : 3 * quarter]
    col_b = values[..., 3 * quarter :]
    return jnp.concatenate(
        [
            row_a * cos_row[:, None] - row_b * sin_row[:, None],
            row_b * cos_row[:, None] + row_a * sin_row[:, None],
            col_a * cos_col[:, None] - col_b * sin_col[:, None],
            col_b * cos_col[:, None] + col_a * sin_col[:, None],
        ],
        axis=-1,
    )


def attend(query_rows, key_rows, value_rows, divisor):
    count = query_rows.shape[0]
    width = min(count, 512)
    blocks = query_rows.reshape(count // width, width, query_rows.shape[1], query_rows.shape[2])

    def one_block(block):
        scores = (
            jnp.einsum("qhd,khd->hqk", block, key_rows, preferred_element_type=jnp.float32)
            / divisor
        )
        weights = jax.nn.softmax(scores, axis=-1).astype(jnp.bfloat16)
        return jnp.einsum(
            "hqk,khd->qhd", weights, value_rows, preferred_element_type=jnp.float32
        ).astype(jnp.bfloat16)

    return lax.map(one_block, blocks).reshape(count, -1)


def block_slots(block_routes, experts_count, capacity):
    picks = block_routes.reshape(-1)
    onehot = (picks[:, None] == jnp.arange(experts_count)[None, :]).astype(jnp.int32)
    earlier = jnp.cumsum(onehot, axis=0) - onehot
    ranks = jnp.sum(earlier * onehot, axis=1)
    owners_flat = jnp.arange(picks.shape[0]) // block_routes.shape[1]
    table = (
        jnp.full((experts_count * capacity,), -1, dtype=jnp.int32)
        .at[picks * capacity + ranks]
        .set(owners_flat)
    )
    return (ranks.reshape(block_routes.shape), table.reshape(experts_count, capacity))


def per_device_slots(
    patches,
    norm1_gain,
    qkv_weight,
    qkv_bias,
    out_weight,
    out_bias,
    norm2_gain,
    proj_weight,
    moe_gain,
    expert_in,
    expert_out,
    shared_in,
    shared_out,
    routes,
    gates,
):
    tiles = lax.axis_size("tile")
    experts_count = lax.axis_size("expert")
    tile_id = lax.axis_index("tile")
    row_count = patches.shape[1]
    columns = patches.shape[2]
    width_vit = patches.shape[3]
    local_rows = row_count * columns
    inputs = patches.reshape(local_rows, width_vit).astype(jnp.float32)
    normed = layer_norm(inputs, norm1_gain).astype(jnp.bfloat16)
    heads_here = qkv_weight.shape[2] // HD
    qkv_flat = qkv_weight.reshape(width_vit, -1)
    bias_rows = qkv_bias.reshape(1, 3, heads_here, HD)
    piece = lax.all_gather(normed, "tile", axis=0, tiled=True)
    mixed = (
        jnp.dot(piece, qkv_flat, preferred_element_type=jnp.float32).reshape(
            piece.shape[0], 3, heads_here, HD
        )
        + bias_rows
    )
    tables = rope_tables(jnp.arange(piece.shape[0]), columns, HD)
    page_qkv = jnp.stack(
        [rotate(mixed[:, 0], tables), rotate(mixed[:, 1], tables), mixed[:, 2]], axis=1
    ).astype(jnp.bfloat16)
    attended = attend(page_qkv[:, 0], page_qkv[:, 1], page_qkv[:, 2], math.sqrt(HD))
    mixed_heads = lax.psum_scatter(
        jnp.dot(attended, out_weight, preferred_element_type=jnp.float32).astype(jnp.bfloat16),
        "tile",
        scatter_dimension=0,
        tiled=True,
    ).astype(jnp.float32)
    hidden = inputs + mixed_heads + out_bias
    normed_out = layer_norm(hidden, norm2_gain).astype(jnp.bfloat16)
    merged = (
        normed_out.reshape(row_count // 2, 2, columns // 2, 2, width_vit)
        .transpose(0, 2, 1, 3, 4)
        .reshape(-1, 4 * width_vit)
    )
    merged_count = merged.shape[0]
    group_merged = lax.all_gather(merged, "tile", axis=0, tiled=True)
    projected = jnp.dot(
        group_merged,
        lax.all_gather(proj_weight, "expert", axis=0, tiled=True),
        preferred_element_type=jnp.float32,
    ).astype(jnp.bfloat16)
    tokens_moe = lax.all_to_all(projected, "tile", split_axis=0, concat_axis=1, tiled=True)
    width_moe = tokens_moe.shape[1]
    moe_in = rms_norm(tokens_moe.astype(jnp.float32), moe_gain).astype(jnp.bfloat16)
    group_in = lax.all_gather(moe_in, "tile", axis=0, tiled=True)
    shared_gated = jnp.dot(
        group_in, shared_in.reshape(width_moe, -1), preferred_element_type=jnp.float32
    ).reshape(group_in.shape[0], 2, -1)
    shared_hidden = (jax.nn.silu(shared_gated[:, 0]) * shared_gated[:, 1]).astype(jnp.bfloat16)
    shared_part = lax.psum_scatter(
        jnp.dot(shared_hidden, shared_out, preferred_element_type=jnp.float32).astype(jnp.bfloat16),
        "tile",
        scatter_dimension=0,
        tiled=True,
    ).astype(jnp.float32)
    top_count = routes.shape[-1]
    capacity = max(2, min(merged_count, 2 * merged_count * top_count // experts_count))
    group_routes = routes.reshape(tiles, merged_count, top_count)
    group_ranks, group_owners = jax.vmap(
        partial(block_slots, experts_count=experts_count, capacity=capacity)
    )(group_routes)
    own_routes = lax.dynamic_index_in_dim(group_routes, tile_id, 0, keepdims=False)
    own_ranks = lax.dynamic_index_in_dim(group_ranks, tile_id, 0, keepdims=False)
    empty_value = jnp.zeros((), jnp.bfloat16)
    table = lax.dynamic_index_in_dim(group_owners, tile_id, 0, keepdims=False)
    used = table >= 0
    outgoing = jnp.where(used[..., None], moe_in[jnp.where(used, table, 0)], empty_value)
    received = lax.all_to_all(outgoing, "expert", split_axis=0, concat_axis=0, tiled=True)
    arrived = lax.all_gather(received[:, None], "tile", axis=1, tiled=True)
    slot_rows = arrived.reshape(-1, width_moe)
    gated = jnp.dot(
        slot_rows, expert_in.reshape(width_moe, -1), preferred_element_type=jnp.float32
    ).reshape(slot_rows.shape[0], 2, -1)
    expert_hidden = (jax.nn.silu(gated[:, 0]) * gated[:, 1]).astype(jnp.bfloat16)
    partial_out = (
        jnp.dot(
            expert_hidden,
            expert_out.reshape(expert_hidden.shape[1], width_moe),
            preferred_element_type=jnp.float32,
        )
        .astype(jnp.bfloat16)
        .reshape(arrived.shape)
    )
    came_back = lax.all_to_all(partial_out, "expert", split_axis=0, concat_axis=0, tiled=True)
    returned = lax.psum_scatter(
        came_back.astype(jnp.float32).astype(jnp.bfloat16), "tile", scatter_dimension=1, tiled=True
    )
    results_flat = returned.reshape(experts_count * capacity, width_moe)
    pick_index = own_routes * capacity + own_ranks
    gate_rows = gates.reshape(merged_count, top_count)
    routed = jnp.zeros((merged_count, width_moe), jnp.float32)
    for position in range(top_count):
        routed = routed + gate_rows[:, position : position + 1] * results_flat[
            pick_index[:, position]
        ].astype(jnp.float32)
    output = tokens_moe.astype(jnp.float32) + shared_part + routed
    return output.astype(jnp.bfloat16).reshape(1, row_count // 2, columns // 2, width_moe)


def near_swap(values, grid, flips):
    pairs = []
    for source in range(math.prod(grid)):
        place, rest = [], source
        for size in reversed(grid):
            place.append(rest % size)
            rest //= size
        target = 0
        for spot, size, flip in zip(reversed(place), grid, flips):
            target = target * size + (spot ^ flip)
        pairs.append((source, target))
    return lax.ppermute(values, ("tile", "expert"), pairs)


def rope_tables_at(rows, columns, head_size):
    quarter = head_size // 4
    inverse = jnp.exp(jnp.arange(quarter).astype(jnp.float32) * (-math.log(rope_base) / quarter))
    row_angle = rows.astype(jnp.float32)[:, None] * inverse[None, :]
    col_angle = columns.astype(jnp.float32)[:, None] * inverse[None, :]
    return (jnp.cos(row_angle), jnp.sin(row_angle), jnp.cos(col_angle), jnp.sin(col_angle))


def attend_rows(query_rows, key_rows, value_rows, divisor):
    scores = (
        jnp.einsum("qhd,khd->hqk", query_rows, key_rows, preferred_element_type=jnp.float32)
        / divisor
    )
    weights = jax.nn.softmax(scores, axis=-1).astype(jnp.bfloat16)
    return (
        jnp.einsum("hqk,khd->qhd", weights, value_rows, preferred_element_type=jnp.float32)
        .astype(jnp.bfloat16)
        .reshape(query_rows.shape[0], -1)
    )


def unit_pieces(units):
    cuts = list(range(0, units, 256)) + [units]
    return list(zip(cuts[:-1], cuts[1:]))


def fetch_units(pieces, sources, targets, arrivals):
    copies = []
    for number, (begin, end) in enumerate(pieces):
        rows = pl.ds(begin, end - begin)
        copies.append(
            [
                pltpu.make_async_copy(
                    source.at[rows], target.at[rows], arrivals.at[number, which]
                )
                for which, (source, target) in enumerate(zip(sources, targets))
            ]
        )
    for piece in copies:
        for copy in piece:
            copy.start()
    return copies


def expert_sums(pieces, copies, normed, gate_rows, up_rows, back_rows):
    total = None
    for (begin, end), piece in zip(pieces, copies):
        for copy in piece:
            copy.wait()
        rows = pl.ds(begin, end - begin)
        wide = (((1,), (1,)), ((), ()))
        gate = lax.dot_general(normed, gate_rows[rows], wide, preferred_element_type=jnp.float32)
        up = lax.dot_general(normed, up_rows[rows], wide, preferred_element_type=jnp.float32)
        hidden = (gate / (1.0 + jnp.exp(-gate)) * up).astype(jnp.bfloat16)
        part = jnp.dot(hidden, back_rows[rows], preferred_element_type=jnp.float32)
        total = part if total is None else total + part
    return total


def norm_pages(place_ref, page_refs, gain_ref, lanes_ref, normed, weights):
    half = normed.shape[1] // 2
    first = pl.multiple_of(place_ref[0] * half, half)
    second = pl.multiple_of((1 - place_ref[0]) * half, half)
    for number, (mine_ref, other_ref) in enumerate(page_refs):
        mine = mine_ref[:, :half].astype(jnp.float32)
        other = other_ref[:, :half].astype(jnp.float32)
        squares = jnp.sum(mine * mine, axis=1, keepdims=True) + jnp.sum(
            other * other, axis=1, keepdims=True
        )
        scale = lax.rsqrt(squares / (2 * half) + norm_eps)
        count = mine.shape[0]
        rows = pl.ds(number * count, count)
        normed[rows, pl.ds(first, half)] = (mine * scale * gain_ref[:, pl.ds(first, half)]).astype(
            jnp.bfloat16
        )
        normed[rows, pl.ds(second, half)] = (
            other * scale * gain_ref[:, pl.ds(second, half)]
        ).astype(jnp.bfloat16)
        if weights is not None:
            lanes = mine_ref[:, half:].astype(jnp.float32) + other_ref[:, half:].astype(jnp.float32)
            weights[rows] = jnp.sum(lanes * lanes_ref[...], axis=1, keepdims=True)


def expert_kernel(pieces, extra, *refs):
    place_ref, near_ref, across_ref, gain_ref, lanes_ref, gate_hbm, up_hbm, back_hbm = refs[:8]
    extra_ref = refs[8] if extra else None
    own_out, across_out, normed, weights, gate_rows, up_rows, back_rows, arrivals = refs[8 + extra :]
    copies = fetch_units(
        pieces, (gate_hbm, up_hbm, back_hbm), (gate_rows, up_rows, back_rows), arrivals
    )
    page_refs = [
        (ref.at[inner, 0], ref.at[inner, 1]) for ref in (near_ref, across_ref) for inner in range(2)
    ]
    norm_pages(place_ref, page_refs, gain_ref, lanes_ref, normed, weights)
    total = expert_sums(pieces, copies, normed[...], gate_rows, up_rows, back_rows)
    total = total * weights[...]
    count = total.shape[0] // 4
    for page in range(4):
        rows = total[page * count : (page + 1) * count]
        if extra and page == 0:
            rows = rows + extra_ref[...]
        target = own_out if page < 2 else across_out
        target[page % 2] = rows.astype(jnp.bfloat16)


def shared_kernel(pieces, *refs):
    place_ref, mine_ref, other_ref, gain_ref, gate_hbm, up_hbm, back_hbm = refs[:7]
    out_ref, normed, gate_rows, up_rows, back_rows, arrivals = refs[7:]
    copies = fetch_units(
        pieces, (gate_hbm, up_hbm, back_hbm), (gate_rows, up_rows, back_rows), arrivals
    )
    norm_pages(place_ref, [(mine_ref, other_ref)], gain_ref, None, normed, None)
    out_ref[...] = expert_sums(pieces, copies, normed[...], gate_rows, up_rows, back_rows)


vmem_spec = pl.BlockSpec(memory_space=pltpu.VMEM)
smem_spec = pl.BlockSpec(memory_space=pltpu.SMEM)
any_spec = pl.BlockSpec(memory_space=pl.ANY)


def expert_cost(rows, units, width):
    return pl.CostEstimate(
        flops=6 * rows * units * width,
        bytes_accessed=6 * units * width + 4 * rows * width,
        transcendentals=rows * units,
    )


def run_expert(tile_place, near, across, gain, lanes, gate_rows, up_rows, back_rows, extra):
    units, width = back_rows.shape
    page_rows = near.shape[2]
    rows = 4 * page_rows
    pieces = unit_pieces(units)
    out = jax.ShapeDtypeStruct((2, page_rows, width), jnp.bfloat16)
    return pl.pallas_call(
        partial(expert_kernel, pieces, extra is not None),
        out_shape=(out, out),
        in_specs=[smem_spec] + [vmem_spec] * 4 + [any_spec] * 3 + [vmem_spec] * (extra is not None),
        out_specs=(vmem_spec, vmem_spec),
        scratch_shapes=[
            pltpu.VMEM((rows, width), jnp.bfloat16),
            pltpu.VMEM((rows, 1), jnp.float32),
            pltpu.VMEM((units, width), jnp.bfloat16),
            pltpu.VMEM((units, width), jnp.bfloat16),
            pltpu.VMEM((units, width), jnp.bfloat16),
            pltpu.SemaphoreType.DMA((len(pieces), 3)),
        ],
        compiler_params=pltpu.CompilerParams(vmem_limit_bytes=40 * 2**20),
        cost_estimate=expert_cost(rows, units, width),
        name="expert_units",
    )(
        tile_place,
        near,
        across,
        gain,
        lanes,
        gate_rows,
        up_rows,
        back_rows,
        *(() if extra is None else (extra,)),
    )


def run_shared(tile_place, mine, other, gain, gate_rows, up_rows, back_rows):
    units, width = back_rows.shape
    rows = mine.shape[0]
    pieces = unit_pieces(units)
    return pl.pallas_call(
        partial(shared_kernel, pieces),
        out_shape=jax.ShapeDtypeStruct((rows, width), jnp.float32),
        in_specs=[smem_spec] + [vmem_spec] * 3 + [any_spec] * 3,
        out_specs=vmem_spec,
        scratch_shapes=[
            pltpu.VMEM((rows, width), jnp.bfloat16),
            pltpu.VMEM((units, width), jnp.bfloat16),
            pltpu.VMEM((units, width), jnp.bfloat16),
            pltpu.VMEM((units, width), jnp.bfloat16),
            pltpu.SemaphoreType.DMA((len(pieces), 3)),
        ],
        compiler_params=pltpu.CompilerParams(vmem_limit_bytes=40 * 2**20),
        cost_estimate=expert_cost(rows, units, width),
        name="shared_units",
    )(tile_place, mine, other, gain, gate_rows, up_rows, back_rows)


def per_device_near(
    patches,
    norm1_gain,
    qkv_weight,
    qkv_bias,
    out_weight,
    out_bias,
    norm2_gain,
    proj_weight,
    moe_gain,
    expert_in,
    expert_out,
    shared_in,
    shared_out,
    routes,
    gates,
):
    experts_count = lax.axis_size("expert")
    outer = experts_count // 4
    swap = partial(near_swap, grid=(2, outer, 2, 2))
    tile_id = lax.axis_index("tile")
    expert_id = lax.axis_index("expert")
    outer_id, inner_id, core_id = expert_id // 4, (expert_id // 2) % 2, expert_id % 2
    row_count, columns, width_vit = patches.shape[1:]
    local_rows = row_count * columns
    token_count = local_rows // 4
    heads_here = qkv_weight.shape[2] // HD

    def by_place(place, mine, other):
        first = place == 0
        return jnp.where(first, mine, other), jnp.where(first, other, mine)

    own_patches = (
        patches.reshape(row_count // 2, 2, columns // 2, 2, width_vit)
        .transpose(1, 3, 0, 2, 4)
        .reshape(local_rows, width_vit)
    )
    other_patches = swap(own_patches, flips=(1, 0, 0, 0))

    shard_rows = proj_weight.shape[0]
    proj_half = jnp.zeros((outer * 2 * shard_rows, proj_weight.shape[1]), proj_weight.dtype)
    for low in range(outer // 2):
        for inner in range(2):
            rows = swap(proj_weight, flips=(0, low, inner, 0)) if low or inner else proj_weight
            for core, block in enumerate((rows, swap(rows, flips=(0, 0, 0, 1)))):
                spot = (
                    ((outer_id ^ low) % (outer // 2)) * 4
                    + (inner_id ^ inner) * 2
                    + (core_id ^ core)
                )
                proj_half = lax.dynamic_update_slice_in_dim(
                    proj_half, block, spot * shard_rows, axis=0
                )

    top_count = routes.shape[-1]
    page_routes = routes.reshape(2, token_count, top_count)
    own_routes = lax.dynamic_index_in_dim(page_routes, tile_id, 0, keepdims=False)
    own_gates = gates.reshape(token_count, top_count)
    dense_gates = jnp.sum(
        jnp.where(
            own_routes[:, :, None] == jnp.arange(experts_count)[None, None, :],
            own_gates[:, :, None],
            0.0,
        ),
        axis=1,
    )
    gates_high = lax.reduce_precision(dense_gates, 8, 7)
    gate_lanes = jnp.concatenate([gates_high, dense_gates - gates_high], axis=1)
    gate_width = gate_lanes.shape[1]
    gate_lanes = jnp.pad(gate_lanes, ((0, 0), (0, 128 - gate_width))).astype(jnp.bfloat16)
    gate_rows = jnp.concatenate(
        by_place(tile_id, gate_lanes, jnp.zeros_like(gate_lanes)), axis=0
    )
    expert_lanes = jnp.arange(128) % experts_count == expert_id
    expert_lanes = (expert_lanes & (jnp.arange(128) < gate_width)).astype(jnp.float32)

    place = jnp.arange(local_rows)
    pair_size = token_count
    parity, within = place // pair_size, place % pair_size
    patch_rows = 2 * (within // (columns // 2)) + parity // 2
    patch_cols = 2 * (within % (columns // 2)) + parity % 2

    def project_qkv(rows, tile):
        normed = layer_norm(rows.astype(jnp.float32), norm1_gain).astype(jnp.bfloat16)
        mixed = jnp.dot(
            normed, qkv_weight.reshape(width_vit, -1), preferred_element_type=jnp.float32
        ).reshape(rows.shape[0], 3, heads_here, HD) + qkv_bias.reshape(1, 3, heads_here, HD)
        tables = rope_tables_at(tile * row_count + patch_rows, patch_cols, HD)
        return (
            rotate(mixed[:, 0], tables).astype(jnp.bfloat16),
            rotate(mixed[:, 1], tables).astype(jnp.bfloat16),
            mixed[:, 2].astype(jnp.bfloat16),
        )

    own_query, own_key, own_value = project_qkv(own_patches, tile_id)
    other_query, other_key, other_value = project_qkv(other_patches, 1 - tile_id)
    keys = jnp.concatenate([own_key, other_key], axis=0)
    values = jnp.concatenate([own_value, other_value], axis=0)
    other_part = jnp.dot(
        attend_rows(other_query, keys, values, math.sqrt(HD)),
        out_weight,
        preferred_element_type=jnp.float32,
    ).astype(jnp.bfloat16)
    arrived_part = swap(other_part, flips=(1, 0, 0, 0))
    own_part = jnp.dot(
        attend_rows(own_query, keys, values, math.sqrt(HD)),
        out_weight,
        preferred_element_type=jnp.float32,
    )
    hidden = (
        own_patches.astype(jnp.float32) + own_part + arrived_part.astype(jnp.float32) + out_bias
    )
    normed_out = layer_norm(hidden, norm2_gain).astype(jnp.bfloat16)

    far = outer // 2
    parity_half = local_rows // 2
    first, second = normed_out[:parity_half], normed_out[parity_half:]
    upper = outer_id // far
    kept, given = by_place(upper, first, second)
    from_far = swap(given, flips=(0, far, 0, 0))
    from_both = swap(given, flips=(1, far, 0, 0))
    from_tile = swap(kept, flips=(1, 0, 0, 0))
    page_tokens = 2 * token_count

    def project(mine, other):
        features = jnp.concatenate(by_place(tile_id, mine, other), axis=0).reshape(
            2, 2, token_count, width_vit
        )
        features = jnp.concatenate([features[:, 0], features[:, 1]], axis=-1)
        return jnp.dot(
            features.reshape(page_tokens, 2 * width_vit),
            proj_half,
            preferred_element_type=jnp.float32,
        )

    far_part = swap(project(from_far, from_both).astype(jnp.bfloat16), flips=(0, far, 0, 0))
    tokens_half = (project(kept, from_tile) + far_part.astype(jnp.float32)).astype(jnp.bfloat16)

    width_moe = 2 * tokens_half.shape[1]
    expert_gate, expert_up = expert_in[0, :, 0].T, expert_in[0, :, 1].T
    shared_gate, shared_up = shared_in[:, 0].T, shared_in[:, 1].T
    tile_place = tile_id.astype(jnp.int32).reshape(1)
    gain_row, lane_row = moe_gain[None], expert_lanes[None]
    half_moe = tokens_half.shape[1]
    held = jnp.concatenate([tokens_half, gate_rows], axis=1)
    held_by_step = [held] + [swap(held, flips=(0, step, 0, 0)) for step in range(1, outer)]
    tile_flip, inner_flip, core_flip = (1, 0, 0, 0), (0, 0, 1, 0), (0, 0, 0, 1)
    contributions = []
    for step, held in enumerate(held_by_step):
        extra = None
        for flip in (inner_flip, tile_flip) if step % 2 else (tile_flip, inner_flip):
            arrived = swap(held, flips=flip)
            if step == 0 and flip == tile_flip:
                extra = run_shared(
                    tile_place, held, arrived, gain_row, shared_gate, shared_up, shared_out
                )
                residual = jnp.concatenate(
                    by_place(
                        tile_id,
                        *(
                            lax.dynamic_slice_in_dim(
                                rows[:, :half_moe], tile_id * token_count, token_count, 0
                            )
                            for rows in (held, arrived)
                        ),
                    ),
                    axis=1,
                )
            held = jnp.stack([held, arrived])
        if step % 2:
            held = held.transpose(1, 0, 2, 3)
        contributions.append(
            run_expert(
                tile_place,
                held,
                swap(held, flips=core_flip),
                gain_row,
                lane_row,
                expert_gate,
                expert_up,
                expert_out[0],
                extra,
            )
        )

    def add(mine, other):
        return (mine.astype(jnp.float32) + other.astype(jnp.float32)).astype(jnp.bfloat16)

    total = residual.astype(jnp.float32)
    for step, (own_sums, across_sums) in enumerate(contributions):
        summed = add(own_sums, swap(across_sums, flips=core_flip)).reshape(
            2, 2, token_count, width_moe
        )
        if step % 2:
            summed = add(summed[0], swap(summed[1], flips=inner_flip))
            stays, leaves = by_place(tile_id, summed[0], summed[1])
            summed = add(stays, swap(leaves, flips=tile_flip))
        else:
            stays, leaves = by_place(tile_id, summed[:, 0], summed[:, 1])
            summed = add(stays, swap(leaves, flips=tile_flip))
            summed = add(summed[0], swap(summed[1], flips=inner_flip))
        if step:
            summed = swap(summed, flips=(0, step, 0, 0))
        total = total + summed.astype(jnp.float32)
    return total.astype(jnp.bfloat16).reshape(1, row_count // 2, columns // 2, width_moe)


def per_device(*arguments):
    experts_count = lax.axis_size("expert")
    if lax.axis_size("tile") == 2 and experts_count % 4 == 0 and experts_count == 16:
        return per_device_near(*arguments)
    return per_device_slots(*arguments)


def solution(mesh):
    placed = (
        P("expert", "tile", None, None),
        P(),
        P(None, None, "tile"),
        P(None, "tile"),
        P("tile", None),
        P(),
        P(),
        P("expert", "tile"),
        P(),
        P("expert", None, None, "tile"),
        P("expert", "tile", None),
        P(None, None, "tile"),
        P("tile", None),
        P("expert", None, None, None),
        P("expert", "tile", None, None),
    )
    return jax.shard_map(
        per_device,
        mesh=mesh,
        in_specs=placed,
        out_specs=P("expert", "tile", None, None),
        check_vma=False,
    )
```

```python
from functools import partial
import math

import jax
import jax.numpy as jnp
from jax import lax
from jax.experimental import pallas as pl
from jax.experimental.pallas import tpu as pltpu
from jax.sharding import PartitionSpec as P

HD = 72


norm_eps = 1e-06
rope_base = 10000.0


def layer_norm(values, gain_vec):
    centre = values - jnp.mean(values, axis=-1, keepdims=True)
    spread = jnp.mean(centre * centre, axis=-1, keepdims=True)
    return centre * lax.rsqrt(spread + norm_eps) * gain_vec


def rms_norm(values, gain_vec):
    return (
        values * lax.rsqrt(jnp.mean(values * values, axis=-1, keepdims=True) + norm_eps) * gain_vec
    )


def rope_tables(positions, columns, head_size):
    quarter = head_size // 4
    inverse = jnp.exp(jnp.arange(quarter).astype(jnp.float32) * (-math.log(rope_base) / quarter))
    row_angle = (positions // columns).astype(jnp.float32)[:, None] * inverse[None, :]
    col_angle = (positions % columns).astype(jnp.float32)[:, None] * inverse[None, :]
    return (jnp.cos(row_angle), jnp.sin(row_angle), jnp.cos(col_angle), jnp.sin(col_angle))


def rotate(values, tables):
    cos_row, sin_row, cos_col, sin_col = tables
    quarter = values.shape[-1] // 4
    row_a = values[..., :quarter]
    row_b = values[..., quarter : 2 * quarter]
    col_a = values[..., 2 * quarter : 3 * quarter]
    col_b = values[..., 3 * quarter :]
    return jnp.concatenate(
        [
            row_a * cos_row[:, None] - row_b * sin_row[:, None],
            row_b * cos_row[:, None] + row_a * sin_row[:, None],
            col_a * cos_col[:, None] - col_b * sin_col[:, None],
            col_b * cos_col[:, None] + col_a * sin_col[:, None],
        ],
        axis=-1,
    )


def attend(query_rows, key_rows, value_rows, divisor):
    count = query_rows.shape[0]
    width = min(count, 512)
    blocks = query_rows.reshape(count // width, width, query_rows.shape[1], query_rows.shape[2])

    def one_block(block):
        scores = (
            jnp.einsum("qhd,khd->hqk", block, key_rows, preferred_element_type=jnp.float32)
            / divisor
        )
        weights = jax.nn.softmax(scores, axis=-1).astype(jnp.bfloat16)
        return jnp.einsum(
            "hqk,khd->qhd", weights, value_rows, preferred_element_type=jnp.float32
        ).astype(jnp.bfloat16)

    return lax.map(one_block, blocks).reshape(count, -1)


def block_slots(block_routes, experts_count, capacity):
    picks = block_routes.reshape(-1)
    onehot = (picks[:, None] == jnp.arange(experts_count)[None, :]).astype(jnp.int32)
    earlier = jnp.cumsum(onehot, axis=0) - onehot
    ranks = jnp.sum(earlier * onehot, axis=1)
    owners_flat = jnp.arange(picks.shape[0]) // block_routes.shape[1]
    table = (
        jnp.full((experts_count * capacity,), -1, dtype=jnp.int32)
        .at[picks * capacity + ranks]
        .set(owners_flat)
    )
    return (ranks.reshape(block_routes.shape), table.reshape(experts_count, capacity))


def per_device_slots(
    patches,
    norm1_gain,
    qkv_weight,
    qkv_bias,
    out_weight,
    out_bias,
    norm2_gain,
    proj_weight,
    moe_gain,
    expert_in,
    expert_out,
    shared_in,
    shared_out,
    routes,
    gates,
):
    tiles = lax.axis_size("tile")
    experts_count = lax.axis_size("expert")
    tile_id = lax.axis_index("tile")
    row_count = patches.shape[1]
    columns = patches.shape[2]
    width_vit = patches.shape[3]
    local_rows = row_count * columns
    inputs = patches.reshape(local_rows, width_vit).astype(jnp.float32)
    normed = layer_norm(inputs, norm1_gain).astype(jnp.bfloat16)
    heads_here = qkv_weight.shape[2] // HD
    qkv_flat = qkv_weight.reshape(width_vit, -1)
    bias_rows = qkv_bias.reshape(1, 3, heads_here, HD)
    piece = lax.all_gather(normed, "tile", axis=0, tiled=True)
    mixed = (
        jnp.dot(piece, qkv_flat, preferred_element_type=jnp.float32).reshape(
            piece.shape[0], 3, heads_here, HD
        )
        + bias_rows
    )
    tables = rope_tables(jnp.arange(piece.shape[0]), columns, HD)
    page_qkv = jnp.stack(
        [rotate(mixed[:, 0], tables), rotate(mixed[:, 1], tables), mixed[:, 2]], axis=1
    ).astype(jnp.bfloat16)
    attended = attend(page_qkv[:, 0], page_qkv[:, 1], page_qkv[:, 2], math.sqrt(HD))
    mixed_heads = lax.psum_scatter(
        jnp.dot(attended, out_weight, preferred_element_type=jnp.float32).astype(jnp.bfloat16),
        "tile",
        scatter_dimension=0,
        tiled=True,
    ).astype(jnp.float32)
    hidden = inputs + mixed_heads + out_bias
    normed_out = layer_norm(hidden, norm2_gain).astype(jnp.bfloat16)
    merged = (
        normed_out.reshape(row_count // 2, 2, columns // 2, 2, width_vit)
        .transpose(0, 2, 1, 3, 4)
        .reshape(-1, 4 * width_vit)
    )
    merged_count = merged.shape[0]
    group_merged = lax.all_gather(merged, "tile", axis=0, tiled=True)
    projected = jnp.dot(
        group_merged,
        lax.all_gather(proj_weight, "expert", axis=0, tiled=True),
        preferred_element_type=jnp.float32,
    ).astype(jnp.bfloat16)
    tokens_moe = lax.all_to_all(projected, "tile", split_axis=0, concat_axis=1, tiled=True)
    width_moe = tokens_moe.shape[1]
    moe_in = rms_norm(tokens_moe.astype(jnp.float32), moe_gain).astype(jnp.bfloat16)
    group_in = lax.all_gather(moe_in, "tile", axis=0, tiled=True)
    shared_gated = jnp.dot(
        group_in, shared_in.reshape(width_moe, -1), preferred_element_type=jnp.float32
    ).reshape(group_in.shape[0], 2, -1)
    shared_hidden = (jax.nn.silu(shared_gated[:, 0]) * shared_gated[:, 1]).astype(jnp.bfloat16)
    shared_part = lax.psum_scatter(
        jnp.dot(shared_hidden, shared_out, preferred_element_type=jnp.float32).astype(jnp.bfloat16),
        "tile",
        scatter_dimension=0,
        tiled=True,
    ).astype(jnp.float32)
    top_count = routes.shape[-1]
    capacity = max(2, min(merged_count, 2 * merged_count * top_count // experts_count))
    group_routes = routes.reshape(tiles, merged_count, top_count)
    group_ranks, group_owners = jax.vmap(
        partial(block_slots, experts_count=experts_count, capacity=capacity)
    )(group_routes)
    own_routes = lax.dynamic_index_in_dim(group_routes, tile_id, 0, keepdims=False)
    own_ranks = lax.dynamic_index_in_dim(group_ranks, tile_id, 0, keepdims=False)
    empty_value = jnp.zeros((), jnp.bfloat16)
    table = lax.dynamic_index_in_dim(group_owners, tile_id, 0, keepdims=False)
    used = table >= 0
    outgoing = jnp.where(used[..., None], moe_in[jnp.where(used, table, 0)], empty_value)
    received = lax.all_to_all(outgoing, "expert", split_axis=0, concat_axis=0, tiled=True)
    arrived = lax.all_gather(received[:, None], "tile", axis=1, tiled=True)
    slot_rows = arrived.reshape(-1, width_moe)
    gated = jnp.dot(
        slot_rows, expert_in.reshape(width_moe, -1), preferred_element_type=jnp.float32
    ).reshape(slot_rows.shape[0], 2, -1)
    expert_hidden = (jax.nn.silu(gated[:, 0]) * gated[:, 1]).astype(jnp.bfloat16)
    partial_out = (
        jnp.dot(
            expert_hidden,
            expert_out.reshape(expert_hidden.shape[1], width_moe),
            preferred_element_type=jnp.float32,
        )
        .astype(jnp.bfloat16)
        .reshape(arrived.shape)
    )
    came_back = lax.all_to_all(partial_out, "expert", split_axis=0, concat_axis=0, tiled=True)
    returned = lax.psum_scatter(
        came_back.astype(jnp.float32).astype(jnp.bfloat16), "tile", scatter_dimension=1, tiled=True
    )
    results_flat = returned.reshape(experts_count * capacity, width_moe)
    pick_index = own_routes * capacity + own_ranks
    gate_rows = gates.reshape(merged_count, top_count)
    routed = jnp.zeros((merged_count, width_moe), jnp.float32)
    for position in range(top_count):
        routed = routed + gate_rows[:, position : position + 1] * results_flat[
            pick_index[:, position]
        ].astype(jnp.float32)
    output = tokens_moe.astype(jnp.float32) + shared_part + routed
    return output.astype(jnp.bfloat16).reshape(1, row_count // 2, columns // 2, width_moe)


def near_swap(values, grid, flips):
    pairs = []
    for source in range(math.prod(grid)):
        place, rest = [], source
        for size in reversed(grid):
            place.append(rest % size)
            rest //= size
        target = 0
        for spot, size, flip in zip(reversed(place), grid, flips):
            target = target * size + (spot ^ flip)
        pairs.append((source, target))
    return lax.ppermute(values, ("tile", "expert"), pairs)


def unit_pieces(units):
    cuts = list(range(0, units, 256)) + [units]
    return list(zip(cuts[:-1], cuts[1:]))


def fetch_units(pieces, sources, targets, arrivals):
    copies = []
    for number, (begin, end) in enumerate(pieces):
        rows = pl.ds(begin, end - begin)
        copies.append(
            [
                pltpu.make_async_copy(
                    source.at[rows], target.at[rows], arrivals.at[number, which]
                )
                for which, (source, target) in enumerate(zip(sources, targets))
            ]
        )
    for piece in copies:
        for copy in piece:
            copy.start()
    return copies


def expert_sums(pieces, copies, normed, gate_rows, up_rows, back_rows):
    total = None
    for (begin, end), piece in zip(pieces, copies):
        for copy in piece:
            copy.wait()
        rows = pl.ds(begin, end - begin)
        wide = (((1,), (1,)), ((), ()))
        gate = lax.dot_general(normed, gate_rows[rows], wide, preferred_element_type=jnp.float32)
        up = lax.dot_general(normed, up_rows[rows], wide, preferred_element_type=jnp.float32)
        hidden = (gate / (1.0 + jnp.exp(-gate)) * up).astype(jnp.bfloat16)
        part = jnp.dot(hidden, back_rows[rows], preferred_element_type=jnp.float32)
        total = part if total is None else total + part
    return total


def norm_pages(place_ref, page_refs, gain_ref, lanes_ref, normed, weights):
    half = normed.shape[1] // 2
    first = pl.multiple_of(place_ref[0] * half, half)
    second = pl.multiple_of((1 - place_ref[0]) * half, half)
    for number, (mine_ref, other_ref) in enumerate(page_refs):
        mine = mine_ref[:, :half].astype(jnp.float32)
        other = other_ref[:, :half].astype(jnp.float32)
        squares = jnp.sum(mine * mine, axis=1, keepdims=True) + jnp.sum(
            other * other, axis=1, keepdims=True
        )
        scale = lax.rsqrt(squares / (2 * half) + norm_eps)
        count = mine.shape[0]
        rows = pl.ds(number * count, count)
        normed[rows, pl.ds(first, half)] = (mine * scale * gain_ref[:, pl.ds(first, half)]).astype(
            jnp.bfloat16
        )
        normed[rows, pl.ds(second, half)] = (
            other * scale * gain_ref[:, pl.ds(second, half)]
        ).astype(jnp.bfloat16)
        if weights is not None:
            lanes = mine_ref[:, half:].astype(jnp.float32) + other_ref[:, half:].astype(jnp.float32)
            weights[rows] = jnp.sum(lanes * lanes_ref[...], axis=1, keepdims=True)


def expert_kernel(pieces, extra, *refs):
    place_ref, near_ref, across_ref, gain_ref, lanes_ref, in_hbm, back_hbm = refs[:7]
    extra_ref = refs[7] if extra else None
    own_out, across_out, normed, weights, gate_rows, up_rows, back_rows, arrivals = refs[7 + extra :]
    copies = fetch_units(
        pieces, (in_hbm.at[0], in_hbm.at[1], back_hbm), (gate_rows, up_rows, back_rows), arrivals
    )
    page_refs = [
        (ref.at[inner, 0], ref.at[inner, 1]) for ref in (near_ref, across_ref) for inner in range(2)
    ]
    norm_pages(place_ref, page_refs, gain_ref, lanes_ref, normed, weights)
    total = expert_sums(pieces, copies, normed[...], gate_rows, up_rows, back_rows)
    total = total * weights[...]
    count = total.shape[0] // 4
    for page in range(4):
        rows = total[page * count : (page + 1) * count]
        if extra and page == 0:
            rows = rows + extra_ref[...]
        target = own_out if page < 2 else across_out
        target[page % 2] = rows.astype(jnp.bfloat16)


def shared_kernel(pieces, *refs):
    place_ref, mine_ref, other_ref, gain_ref, in_hbm, back_hbm = refs[:6]
    out_ref, normed, gate_rows, up_rows, back_rows, arrivals = refs[6:]
    copies = fetch_units(
        pieces, (in_hbm.at[0], in_hbm.at[1], back_hbm), (gate_rows, up_rows, back_rows), arrivals
    )
    norm_pages(place_ref, [(mine_ref, other_ref)], gain_ref, None, normed, None)
    out_ref[...] = expert_sums(pieces, copies, normed[...], gate_rows, up_rows, back_rows)


vmem_spec = pl.BlockSpec(memory_space=pltpu.VMEM)
smem_spec = pl.BlockSpec(memory_space=pltpu.SMEM)
any_spec = pl.BlockSpec(memory_space=pl.ANY)


def expert_cost(rows, units, width):
    return pl.CostEstimate(
        flops=6 * rows * units * width,
        bytes_accessed=6 * units * width + 4 * rows * width,
        transcendentals=rows * units,
    )


def run_expert(tile_place, near, across, gain, lanes, in_rows, back_rows, extra):
    units, width = back_rows.shape
    page_rows = near.shape[2]
    rows = 4 * page_rows
    pieces = unit_pieces(units)
    out = jax.ShapeDtypeStruct((2, page_rows, width), jnp.bfloat16)
    return pl.pallas_call(
        partial(expert_kernel, pieces, extra is not None),
        out_shape=(out, out),
        in_specs=[smem_spec] + [vmem_spec] * 4 + [any_spec] * 2 + [vmem_spec] * (extra is not None),
        out_specs=(vmem_spec, vmem_spec),
        scratch_shapes=[
            pltpu.VMEM((rows, width), jnp.bfloat16),
            pltpu.VMEM((rows, 1), jnp.float32),
            pltpu.VMEM((units, width), jnp.bfloat16),
            pltpu.VMEM((units, width), jnp.bfloat16),
            pltpu.VMEM((units, width), jnp.bfloat16),
            pltpu.SemaphoreType.DMA((len(pieces), 3)),
        ],
        compiler_params=pltpu.CompilerParams(vmem_limit_bytes=28 * 2**20),
        cost_estimate=expert_cost(rows, units, width),
        name="expert_units",
    )(
        tile_place,
        near,
        across,
        gain,
        lanes,
        in_rows,
        back_rows,
        *(() if extra is None else (extra,)),
    )


def run_shared(tile_place, mine, other, gain, in_rows, back_rows):
    units, width = back_rows.shape
    rows = mine.shape[0]
    pieces = unit_pieces(units)
    return pl.pallas_call(
        partial(shared_kernel, pieces),
        out_shape=jax.ShapeDtypeStruct((rows, width), jnp.float32),
        in_specs=[smem_spec] + [vmem_spec] * 3 + [any_spec] * 2,
        out_specs=vmem_spec,
        scratch_shapes=[
            pltpu.VMEM((rows, width), jnp.bfloat16),
            pltpu.VMEM((units, width), jnp.bfloat16),
            pltpu.VMEM((units, width), jnp.bfloat16),
            pltpu.VMEM((units, width), jnp.bfloat16),
            pltpu.SemaphoreType.DMA((len(pieces), 3)),
        ],
        compiler_params=pltpu.CompilerParams(vmem_limit_bytes=28 * 2**20),
        cost_estimate=expert_cost(rows, units, width),
        name="shared_units",
    )(tile_place, mine, other, gain, in_rows, back_rows)


def project_heads(rows_ref, gain_ref, weight, bias_ref, cos_ref, sin_ref, heads):
    normed = layer_norm(rows_ref[...].astype(jnp.float32), gain_ref[...]).astype(jnp.bfloat16)
    quarter = HD // 4
    outs = []
    for which in range(3):
        mixed = (
            lax.dot_general(
                weight(which),
                normed,
                (((1,), (1,)), ((), ())),
                preferred_element_type=jnp.float32,
            )
            + bias_ref[which]
        ).reshape(heads, HD, normed.shape[0])
        if which < 2:
            parts = [mixed[:, n * quarter : (n + 1) * quarter] for n in range(4)]
            partner = jnp.concatenate([-parts[1], parts[0], -parts[3], parts[2]], axis=1)
            mixed = mixed * cos_ref[...][None] + partner * sin_ref[...][None]
        outs.append(mixed.astype(jnp.bfloat16))
    return outs


def attend_heads(query, keys, values, heads):
    turned = (((0,), (0,)), ((), ()))
    outs = []
    for head in range(heads):
        scores = lax.dot_general(
            keys[head], query[head], turned, preferred_element_type=jnp.float32
        ) * (1.0 / math.sqrt(HD))
        raised = jnp.exp(scores - jnp.max(scores, axis=0, keepdims=True))
        probs = (raised / jnp.sum(raised, axis=0, keepdims=True)).astype(jnp.bfloat16)
        outs.append(jnp.dot(values[head], probs, preferred_element_type=jnp.float32))
    return jnp.concatenate(outs, axis=0).astype(jnp.bfloat16)


def own_heads_kernel(heads, *refs):
    rows_ref, gain_ref, bias_ref, cos_ref, sin_ref, weight_hbm, out_ref, weight, arrivals = refs
    copies = [
        pltpu.make_async_copy(weight_hbm.at[which], weight.at[which], arrivals.at[which])
        for which in range(3)
    ]
    for copy in copies:
        copy.start()

    def fetched(which):
        copies[which].wait()
        return weight[which]

    outs = project_heads(rows_ref, gain_ref, fetched, bias_ref, cos_ref, sin_ref, heads)
    for which, values in enumerate(outs):
        out_ref[which] = values


def other_rows_kernel(heads, *refs):
    rows_ref, gain_ref, bias_ref, cos_ref, sin_ref, own_ref, weight_hbm, back_hbm = refs[:8]
    part_ref, keys_ref, weight, back, arrivals = refs[8:]
    copies = [
        pltpu.make_async_copy(weight_hbm.at[which], weight.at[which], arrivals.at[which])
        for which in range(3)
    ] + [pltpu.make_async_copy(back_hbm, back, arrivals.at[3])]
    for copy in copies:
        copy.start()

    def fetched(which):
        copies[which].wait()
        return weight[which]

    query, other_keys, other_values = project_heads(
        rows_ref, gain_ref, fetched, bias_ref, cos_ref, sin_ref, heads
    )
    keys = jnp.concatenate([own_ref[1], other_keys], axis=2)
    values = jnp.concatenate([own_ref[2], other_values], axis=2)
    keys_ref[0] = keys
    keys_ref[1] = values
    attended = attend_heads(query, keys, values, heads)
    copies[3].wait()
    part_ref[...] = lax.dot_general(
        attended, back[...], (((0,), (0,)), ((), ())), preferred_element_type=jnp.float32
    ).astype(jnp.bfloat16)


def own_rows_kernel(heads, *refs):
    rows_ref, own_ref, keys_ref, back_ref, bias_ref, out_ref = refs
    attended = attend_heads(own_ref[0], keys_ref[0], keys_ref[1], heads)
    out_ref[...] = (
        rows_ref[...].astype(jnp.float32)
        + bias_ref[...]
        + lax.dot_general(
            attended, back_ref[...], (((0,), (0,)), ((), ())), preferred_element_type=jnp.float32
        )
    )


def merge_kernel(columns, *refs):
    place_ref, hidden_ref, arrived_ref, gain_ref, kept_ref, given_ref, scratch = refs
    normed = layer_norm(hidden_ref[...] + arrived_ref[...].astype(jnp.float32), gain_ref[...])
    slabs = scratch.shape[0]
    for slab in range(slabs):
        scratch[slab] = normed[:, slab * 128 : (slab + 1) * 128]
    count = columns // 2
    for pair in range(normed.shape[0] // (2 * columns)):
        for parity in range(2):
            rows = [
                scratch[slab, pl.ds((2 * pair + parity) * columns + side, count, stride=2)]
                for side in range(2)
                for slab in range(slabs)
            ]
            merged = jnp.concatenate(rows, axis=1).astype(jnp.bfloat16)
            spot = pl.ds(pair * count, count)

            @pl.when(place_ref[0] == parity)
            def _keep(merged=merged, spot=spot):
                kept_ref[spot] = merged

            @pl.when(place_ref[0] != parity)
            def _give(merged=merged, spot=spot):
                given_ref[spot] = merged


def projector_kernel(spots_ref, place_ref, mine_ref, other_ref, *refs):
    weight_refs, out_ref, blocks = refs[:-2], refs[-2], refs[-1]
    count, size = mine_ref.shape[0], weight_refs[0].shape[0]
    mine_rows = pl.ds(pl.multiple_of(place_ref[0] * count, count), count)
    other_rows = pl.ds(pl.multiple_of((1 - place_ref[0]) * count, count), count)
    for number in range(len(weight_refs)):
        lanes = slice(number * size, (number + 1) * size)
        blocks[number, mine_rows] = mine_ref[:, lanes]
        blocks[number, other_rows] = other_ref[:, lanes]
    total = None
    for number, weight_ref in enumerate(weight_refs):
        part = jnp.dot(
            blocks[spots_ref[number]], weight_ref[...], preferred_element_type=jnp.float32
        )
        total = part if total is None else total + part
    out_ref[...] = total.astype(out_ref.dtype)


def run_projector(spots, place, mine, other, weights, dtype):
    rows, size, width = 2 * mine.shape[0], weights[0].shape[0], weights[0].shape[1]
    return pl.pallas_call(
        projector_kernel,
        out_shape=jax.ShapeDtypeStruct((rows, width), dtype),
        in_specs=[smem_spec] * 2 + [vmem_spec] * (2 + len(weights)),
        out_specs=vmem_spec,
        scratch_shapes=[pltpu.VMEM((len(weights), rows, size), jnp.bfloat16)],
        compiler_params=pltpu.CompilerParams(vmem_limit_bytes=28 * 2**20),
        cost_estimate=pl.CostEstimate(
            flops=2 * rows * width * size * len(weights),
            bytes_accessed=2 * width * size * len(weights),
            transcendentals=0,
        ),
        name="projector",
    )(spots, place, mine, other, *weights)


def per_device_near(
    patches,
    norm1_gain,
    qkv_weight,
    qkv_bias,
    out_weight,
    out_bias,
    norm2_gain,
    proj_weight,
    moe_gain,
    expert_in,
    expert_out,
    shared_in,
    shared_out,
    routes,
    gates,
):
    experts_count = lax.axis_size("expert")
    outer = experts_count // 4
    swap = partial(near_swap, grid=(2, outer, 2, 2))
    tile_id = lax.axis_index("tile")
    expert_id = lax.axis_index("expert")
    outer_id, inner_id, core_id = expert_id // 4, (expert_id // 2) % 2, expert_id % 2
    row_count, columns, width_vit = patches.shape[1:]
    local_rows = row_count * columns
    token_count = local_rows // 4

    def by_place(place, mine, other):
        first = place == 0
        return jnp.where(first, mine, other), jnp.where(first, other, mine)

    own_patches = patches.reshape(local_rows, width_vit)
    other_patches = swap(own_patches, flips=(1, 0, 0, 0))
    tile_place = tile_id.astype(jnp.int32).reshape(1)

    proj_blocks, proj_spots = [], []
    for low in range(outer // 2):
        for inner in range(2):
            rows = swap(proj_weight, flips=(0, low, inner, 0)) if low or inner else proj_weight
            for core, block in enumerate((rows, swap(rows, flips=(0, 0, 0, 1)))):
                proj_blocks.append(block)
                proj_spots.append(
                    ((outer_id ^ low) % (outer // 2)) * 4
                    + (inner_id ^ inner) * 2
                    + (core_id ^ core)
                )
    proj_spots = jnp.stack(proj_spots).astype(jnp.int32)

    top_count = routes.shape[-1]
    page_routes = routes.reshape(2, token_count, top_count)
    own_routes = lax.dynamic_index_in_dim(page_routes, tile_id, 0, keepdims=False)
    own_gates = gates.reshape(token_count, top_count)
    dense_gates = jnp.sum(
        jnp.where(
            own_routes[:, :, None] == jnp.arange(experts_count)[None, None, :],
            own_gates[:, :, None],
            0.0,
        ),
        axis=1,
    )
    gates_high = lax.reduce_precision(dense_gates, 8, 7)
    gate_lanes = jnp.concatenate([gates_high, dense_gates - gates_high], axis=1)
    gate_width = gate_lanes.shape[1]
    gate_lanes = jnp.pad(gate_lanes, ((0, 0), (0, 128 - gate_width))).astype(jnp.bfloat16)
    gate_rows = jnp.concatenate(
        by_place(tile_id, gate_lanes, jnp.zeros_like(gate_lanes)), axis=0
    )
    expert_lanes = jnp.arange(128) % experts_count == expert_id
    expert_lanes = (expert_lanes & (jnp.arange(128) < gate_width)).astype(jnp.float32)

    heads = qkv_weight.shape[2] // HD
    weight_rows = qkv_weight.transpose(1, 2, 0)
    bias_rows = qkv_bias[:, :, None]
    quarter = HD // 4
    feature = jnp.arange(HD)
    inverse = jnp.exp(
        (feature % quarter).astype(jnp.float32) * (-math.log(rope_base) / quarter)
    )[:, None]
    position = jnp.arange(local_rows)

    def tables(tile):
        rows = (tile * row_count + position // columns).astype(jnp.float32)[None]
        cols = (position % columns).astype(jnp.float32)[None]
        angles = jnp.where((feature < 2 * quarter)[:, None], rows, cols) * inverse
        return jnp.cos(angles), jnp.sin(angles)

    gain_first, gain_second = norm1_gain[None], norm2_gain[None]
    head_rows = (heads, HD, local_rows)
    weight_scratch = pltpu.VMEM(weight_rows.shape, jnp.bfloat16)
    params = pltpu.CompilerParams(vmem_limit_bytes=28 * 2**20)
    macs = local_rows * width_vit * heads * HD
    own_heads = pl.pallas_call(
        partial(own_heads_kernel, heads),
        out_shape=jax.ShapeDtypeStruct((3, *head_rows), jnp.bfloat16),
        in_specs=[vmem_spec] * 5 + [any_spec],
        out_specs=vmem_spec,
        scratch_shapes=[weight_scratch, pltpu.SemaphoreType.DMA((3,))],
        compiler_params=params,
        cost_estimate=pl.CostEstimate(
            flops=6 * macs, bytes_accessed=2 * weight_rows.size, transcendentals=0
        ),
        name="own_heads",
    )(own_patches, gain_first, bias_rows, *tables(tile_id), weight_rows)
    other_part, keys_values = pl.pallas_call(
        partial(other_rows_kernel, heads),
        out_shape=(
            jax.ShapeDtypeStruct((local_rows, width_vit), jnp.bfloat16),
            jax.ShapeDtypeStruct((2, heads, HD, 2 * local_rows), jnp.bfloat16),
        ),
        in_specs=[vmem_spec] * 6 + [any_spec] * 2,
        out_specs=(vmem_spec, vmem_spec),
        scratch_shapes=[
            weight_scratch,
            pltpu.VMEM(out_weight.shape, jnp.bfloat16),
            pltpu.SemaphoreType.DMA((4,)),
        ],
        compiler_params=params,
        cost_estimate=pl.CostEstimate(
            flops=10 * macs, bytes_accessed=2 * weight_rows.size, transcendentals=0
        ),
        name="other_rows",
    )(
        other_patches,
        gain_first,
        bias_rows,
        *tables(1 - tile_id),
        own_heads,
        weight_rows,
        out_weight,
    )
    arrived_part = swap(other_part, flips=(1, 0, 0, 0))
    hidden = pl.pallas_call(
        partial(own_rows_kernel, heads),
        out_shape=jax.ShapeDtypeStruct((local_rows, width_vit), jnp.float32),
        in_specs=[vmem_spec] * 5,
        out_specs=vmem_spec,
        compiler_params=params,
        cost_estimate=pl.CostEstimate(
            flops=4 * macs, bytes_accessed=2 * out_weight.size, transcendentals=0
        ),
        name="own_rows",
    )(own_patches, own_heads, keys_values, out_weight, out_bias[None])
    merged_shape = jax.ShapeDtypeStruct((token_count, 2 * width_vit), jnp.bfloat16)
    kept, given = pl.pallas_call(
        partial(merge_kernel, columns),
        out_shape=(merged_shape, merged_shape),
        in_specs=[smem_spec] + [vmem_spec] * 3,
        out_specs=(vmem_spec, vmem_spec),
        scratch_shapes=[pltpu.VMEM((width_vit // 128, local_rows, 128), jnp.float32)],
        compiler_params=params,
        name="merge_windows",
    )(
        (outer_id // (outer // 2)).astype(jnp.int32).reshape(1),
        hidden,
        arrived_part,
        gain_second,
    )

    far = outer // 2
    from_far = swap(given, flips=(0, far, 0, 0))
    from_both = swap(given, flips=(1, far, 0, 0))
    from_tile = swap(kept, flips=(1, 0, 0, 0))
    page_tokens = 2 * token_count
    project = partial(run_projector, proj_spots, tile_place, weights=proj_blocks)
    far_part = swap(project(from_far, from_both, dtype=jnp.bfloat16), flips=(0, far, 0, 0))
    tokens_half = (
        project(kept, from_tile, dtype=jnp.float32) + far_part.astype(jnp.float32)
    ).astype(jnp.bfloat16)

    width_moe = 2 * tokens_half.shape[1]
    expert_units = expert_in[0].transpose(1, 2, 0)
    shared_units = shared_in.transpose(1, 2, 0)
    gain_row, lane_row = moe_gain[None], expert_lanes[None]
    half_moe = tokens_half.shape[1]
    held = jnp.concatenate([tokens_half, gate_rows], axis=1)
    held_by_step = [held] + [swap(held, flips=(0, step, 0, 0)) for step in range(1, outer)]
    tile_flip, inner_flip, core_flip = (1, 0, 0, 0), (0, 0, 1, 0), (0, 0, 0, 1)
    contributions = []
    for step, held in enumerate(held_by_step):
        extra = None
        for flip in (inner_flip, tile_flip) if step % 2 else (tile_flip, inner_flip):
            arrived = swap(held, flips=flip)
            if step == 0 and flip == tile_flip:
                extra = run_shared(
                    tile_place, held, arrived, gain_row, shared_units, shared_out
                )
                residual = jnp.concatenate(
                    by_place(
                        tile_id,
                        *(
                            lax.dynamic_slice_in_dim(
                                rows[:, :half_moe], tile_id * token_count, token_count, 0
                            )
                            for rows in (held, arrived)
                        ),
                    ),
                    axis=1,
                )
            held = jnp.stack([held, arrived])
        if step % 2:
            held = held.transpose(1, 0, 2, 3)
        contributions.append(
            run_expert(
                tile_place,
                held,
                swap(held, flips=core_flip),
                gain_row,
                lane_row,
                expert_units,
                expert_out[0],
                extra,
            )
        )

    def add(mine, other):
        return (mine.astype(jnp.float32) + other.astype(jnp.float32)).astype(jnp.bfloat16)

    total = residual.astype(jnp.float32)
    for step, (own_sums, across_sums) in enumerate(contributions):
        summed = add(own_sums, swap(across_sums, flips=core_flip)).reshape(
            2, 2, token_count, width_moe
        )
        if step % 2:
            summed = add(summed[0], swap(summed[1], flips=inner_flip))
            stays, leaves = by_place(tile_id, summed[0], summed[1])
            summed = add(stays, swap(leaves, flips=tile_flip))
        else:
            stays, leaves = by_place(tile_id, summed[:, 0], summed[:, 1])
            summed = add(stays, swap(leaves, flips=tile_flip))
            summed = add(summed[0], swap(summed[1], flips=inner_flip))
        if step:
            summed = swap(summed, flips=(0, step, 0, 0))
        total = total + summed.astype(jnp.float32)
    return total.astype(jnp.bfloat16).reshape(1, row_count // 2, columns // 2, width_moe)


def per_device(*arguments):
    experts_count = lax.axis_size("expert")
    if lax.axis_size("tile") == 2 and experts_count % 4 == 0 and experts_count == 16:
        return per_device_near(*arguments)
    return per_device_slots(*arguments)


def solution(mesh):
    placed = (
        P("expert", "tile", None, None),
        P(),
        P(None, None, "tile"),
        P(None, "tile"),
        P("tile", None),
        P(),
        P(),
        P("expert", "tile"),
        P(),
        P("expert", None, None, "tile"),
        P("expert", "tile", None),
        P(None, None, "tile"),
        P("tile", None),
        P("expert", None, None, None),
        P("expert", "tile", None, None),
    )
    return jax.shard_map(
        per_device,
        mesh=mesh,
        in_specs=placed,
        out_specs=P("expert", "tile", None, None),
        check_vma=False,
    )
```

```python
from functools import partial
import math

import jax
import jax.numpy as jnp
from jax import lax
from jax.experimental import pallas as pl
from jax.experimental.pallas import tpu as pltpu
from jax.sharding import PartitionSpec as P

HD = 72


norm_eps = 1e-06
rope_base = 10000.0


def layer_norm(values, gain_vec):
    centre = values - jnp.mean(values, axis=-1, keepdims=True)
    spread = jnp.mean(centre * centre, axis=-1, keepdims=True)
    return centre * lax.rsqrt(spread + norm_eps) * gain_vec


def rms_norm(values, gain_vec):
    return (
        values * lax.rsqrt(jnp.mean(values * values, axis=-1, keepdims=True) + norm_eps) * gain_vec
    )


def rope_tables(positions, columns, head_size):
    quarter = head_size // 4
    inverse = jnp.exp(jnp.arange(quarter).astype(jnp.float32) * (-math.log(rope_base) / quarter))
    row_angle = (positions // columns).astype(jnp.float32)[:, None] * inverse[None, :]
    col_angle = (positions % columns).astype(jnp.float32)[:, None] * inverse[None, :]
    return (jnp.cos(row_angle), jnp.sin(row_angle), jnp.cos(col_angle), jnp.sin(col_angle))


def rotate(values, tables):
    cos_row, sin_row, cos_col, sin_col = tables
    quarter = values.shape[-1] // 4
    row_a = values[..., :quarter]
    row_b = values[..., quarter : 2 * quarter]
    col_a = values[..., 2 * quarter : 3 * quarter]
    col_b = values[..., 3 * quarter :]
    return jnp.concatenate(
        [
            row_a * cos_row[:, None] - row_b * sin_row[:, None],
            row_b * cos_row[:, None] + row_a * sin_row[:, None],
            col_a * cos_col[:, None] - col_b * sin_col[:, None],
            col_b * cos_col[:, None] + col_a * sin_col[:, None],
        ],
        axis=-1,
    )


def attend(query_rows, key_rows, value_rows, divisor):
    count = query_rows.shape[0]
    width = min(count, 512)
    blocks = query_rows.reshape(count // width, width, query_rows.shape[1], query_rows.shape[2])

    def one_block(block):
        scores = (
            jnp.einsum("qhd,khd->hqk", block, key_rows, preferred_element_type=jnp.float32)
            / divisor
        )
        weights = jax.nn.softmax(scores, axis=-1).astype(jnp.bfloat16)
        return jnp.einsum(
            "hqk,khd->qhd", weights, value_rows, preferred_element_type=jnp.float32
        ).astype(jnp.bfloat16)

    return lax.map(one_block, blocks).reshape(count, -1)


def block_slots(block_routes, experts_count, capacity):
    picks = block_routes.reshape(-1)
    onehot = (picks[:, None] == jnp.arange(experts_count)[None, :]).astype(jnp.int32)
    earlier = jnp.cumsum(onehot, axis=0) - onehot
    ranks = jnp.sum(earlier * onehot, axis=1)
    owners_flat = jnp.arange(picks.shape[0]) // block_routes.shape[1]
    table = (
        jnp.full((experts_count * capacity,), -1, dtype=jnp.int32)
        .at[picks * capacity + ranks]
        .set(owners_flat)
    )
    return (ranks.reshape(block_routes.shape), table.reshape(experts_count, capacity))


def per_device_slots(
    patches,
    norm1_gain,
    qkv_weight,
    qkv_bias,
    out_weight,
    out_bias,
    norm2_gain,
    proj_weight,
    moe_gain,
    expert_in,
    expert_out,
    shared_in,
    shared_out,
    routes,
    gates,
):
    tiles = lax.axis_size("tile")
    experts_count = lax.axis_size("expert")
    tile_id = lax.axis_index("tile")
    row_count = patches.shape[1]
    columns = patches.shape[2]
    width_vit = patches.shape[3]
    local_rows = row_count * columns
    inputs = patches.reshape(local_rows, width_vit).astype(jnp.float32)
    normed = layer_norm(inputs, norm1_gain).astype(jnp.bfloat16)
    heads_here = qkv_weight.shape[2] // HD
    qkv_flat = qkv_weight.reshape(width_vit, -1)
    bias_rows = qkv_bias.reshape(1, 3, heads_here, HD)
    piece = lax.all_gather(normed, "tile", axis=0, tiled=True)
    mixed = (
        jnp.dot(piece, qkv_flat, preferred_element_type=jnp.float32).reshape(
            piece.shape[0], 3, heads_here, HD
        )
        + bias_rows
    )
    tables = rope_tables(jnp.arange(piece.shape[0]), columns, HD)
    page_qkv = jnp.stack(
        [rotate(mixed[:, 0], tables), rotate(mixed[:, 1], tables), mixed[:, 2]], axis=1
    ).astype(jnp.bfloat16)
    attended = attend(page_qkv[:, 0], page_qkv[:, 1], page_qkv[:, 2], math.sqrt(HD))
    mixed_heads = lax.psum_scatter(
        jnp.dot(attended, out_weight, preferred_element_type=jnp.float32).astype(jnp.bfloat16),
        "tile",
        scatter_dimension=0,
        tiled=True,
    ).astype(jnp.float32)
    hidden = inputs + mixed_heads + out_bias
    normed_out = layer_norm(hidden, norm2_gain).astype(jnp.bfloat16)
    merged = (
        normed_out.reshape(row_count // 2, 2, columns // 2, 2, width_vit)
        .transpose(0, 2, 1, 3, 4)
        .reshape(-1, 4 * width_vit)
    )
    merged_count = merged.shape[0]
    group_merged = lax.all_gather(merged, "tile", axis=0, tiled=True)
    projected = jnp.dot(
        group_merged,
        lax.all_gather(proj_weight, "expert", axis=0, tiled=True),
        preferred_element_type=jnp.float32,
    ).astype(jnp.bfloat16)
    tokens_moe = lax.all_to_all(projected, "tile", split_axis=0, concat_axis=1, tiled=True)
    width_moe = tokens_moe.shape[1]
    moe_in = rms_norm(tokens_moe.astype(jnp.float32), moe_gain).astype(jnp.bfloat16)
    group_in = lax.all_gather(moe_in, "tile", axis=0, tiled=True)
    shared_gated = jnp.dot(
        group_in, shared_in.reshape(width_moe, -1), preferred_element_type=jnp.float32
    ).reshape(group_in.shape[0], 2, -1)
    shared_hidden = (jax.nn.silu(shared_gated[:, 0]) * shared_gated[:, 1]).astype(jnp.bfloat16)
    shared_part = lax.psum_scatter(
        jnp.dot(shared_hidden, shared_out, preferred_element_type=jnp.float32).astype(jnp.bfloat16),
        "tile",
        scatter_dimension=0,
        tiled=True,
    ).astype(jnp.float32)
    top_count = routes.shape[-1]
    capacity = max(2, min(merged_count, 2 * merged_count * top_count // experts_count))
    group_routes = routes.reshape(tiles, merged_count, top_count)
    group_ranks, group_owners = jax.vmap(
        partial(block_slots, experts_count=experts_count, capacity=capacity)
    )(group_routes)
    own_routes = lax.dynamic_index_in_dim(group_routes, tile_id, 0, keepdims=False)
    own_ranks = lax.dynamic_index_in_dim(group_ranks, tile_id, 0, keepdims=False)
    empty_value = jnp.zeros((), jnp.bfloat16)
    table = lax.dynamic_index_in_dim(group_owners, tile_id, 0, keepdims=False)
    used = table >= 0
    outgoing = jnp.where(used[..., None], moe_in[jnp.where(used, table, 0)], empty_value)
    received = lax.all_to_all(outgoing, "expert", split_axis=0, concat_axis=0, tiled=True)
    arrived = lax.all_gather(received[:, None], "tile", axis=1, tiled=True)
    slot_rows = arrived.reshape(-1, width_moe)
    gated = jnp.dot(
        slot_rows, expert_in.reshape(width_moe, -1), preferred_element_type=jnp.float32
    ).reshape(slot_rows.shape[0], 2, -1)
    expert_hidden = (jax.nn.silu(gated[:, 0]) * gated[:, 1]).astype(jnp.bfloat16)
    partial_out = (
        jnp.dot(
            expert_hidden,
            expert_out.reshape(expert_hidden.shape[1], width_moe),
            preferred_element_type=jnp.float32,
        )
        .astype(jnp.bfloat16)
        .reshape(arrived.shape)
    )
    came_back = lax.all_to_all(partial_out, "expert", split_axis=0, concat_axis=0, tiled=True)
    returned = lax.psum_scatter(
        came_back.astype(jnp.float32).astype(jnp.bfloat16), "tile", scatter_dimension=1, tiled=True
    )
    results_flat = returned.reshape(experts_count * capacity, width_moe)
    pick_index = own_routes * capacity + own_ranks
    gate_rows = gates.reshape(merged_count, top_count)
    routed = jnp.zeros((merged_count, width_moe), jnp.float32)
    for position in range(top_count):
        routed = routed + gate_rows[:, position : position + 1] * results_flat[
            pick_index[:, position]
        ].astype(jnp.float32)
    output = tokens_moe.astype(jnp.float32) + shared_part + routed
    return output.astype(jnp.bfloat16).reshape(1, row_count // 2, columns // 2, width_moe)


near_expert = ("half", "outer", "inner", "core")


def near_swap(values, grid, flips):
    pairs = []
    for source in range(math.prod(grid)):
        place, rest = [], source
        for size in reversed(grid):
            place.append(rest % size)
            rest //= size
        target = 0
        for spot, size, flip in zip(reversed(place), grid, flips):
            target = target * size + (spot ^ flip)
        pairs.append((source, target))
    return lax.ppermute(values, ("tile", *near_expert), pairs)


def expert_sums(normed, in_ref, back_ref):
    units = back_ref.shape[0]
    wide = (((1,), (1,)), ((), ()))
    total = None
    for begin in range(0, units, 256):
        rows = pl.ds(begin, min(256, units - begin))
        gate = lax.dot_general(normed, in_ref[0, rows], wide, preferred_element_type=jnp.float32)
        up = lax.dot_general(normed, in_ref[1, rows], wide, preferred_element_type=jnp.float32)
        hidden = (gate / (1.0 + jnp.exp(-gate)) * up).astype(jnp.bfloat16)
        part = jnp.dot(hidden, back_ref[rows], preferred_element_type=jnp.float32)
        total = part if total is None else total + part
    return total


def norm_pages(place_ref, page_refs, gain_ref, lanes_ref, normed, weights):
    half = normed.shape[1] // 2
    first = pl.multiple_of(place_ref[0] * half, half)
    second = pl.multiple_of((1 - place_ref[0]) * half, half)
    for number, (mine_ref, other_ref) in enumerate(page_refs):
        mine = mine_ref[:, :half].astype(jnp.float32)
        other = other_ref[:, :half].astype(jnp.float32)
        squares = jnp.sum(mine * mine, axis=1, keepdims=True) + jnp.sum(
            other * other, axis=1, keepdims=True
        )
        scale = lax.rsqrt(squares / (2 * half) + norm_eps)
        count = mine.shape[0]
        rows = pl.ds(number * count, count)
        normed[rows, pl.ds(first, half)] = (mine * scale * gain_ref[:, pl.ds(first, half)]).astype(
            jnp.bfloat16
        )
        normed[rows, pl.ds(second, half)] = (
            other * scale * gain_ref[:, pl.ds(second, half)]
        ).astype(jnp.bfloat16)
        if weights is not None:
            lanes = mine_ref[:, half:].astype(jnp.float32) + other_ref[:, half:].astype(jnp.float32)
            weights[rows] = jnp.sum(lanes * lanes_ref[...], axis=1, keepdims=True)


def expert_kernel(extra, *refs):
    place_ref, near_ref, across_ref, gain_ref, lanes_ref, in_ref, back_ref = refs[:7]
    extra_ref = refs[7] if extra else None
    own_out, across_out, normed, weights = refs[7 + extra :]
    page_refs = [
        (ref.at[inner, 0], ref.at[inner, 1]) for ref in (near_ref, across_ref) for inner in range(2)
    ]
    norm_pages(place_ref, page_refs, gain_ref, lanes_ref, normed, weights)
    total = expert_sums(normed[...], in_ref, back_ref) * weights[...]
    count = total.shape[0] // 4
    for page in range(4):
        rows = total[page * count : (page + 1) * count]
        if extra and page == 0:
            rows = rows + extra_ref[...]
        target = own_out if page < 2 else across_out
        target[page % 2] = rows.astype(jnp.bfloat16)


def shared_kernel(place_ref, mine_ref, other_ref, gain_ref, in_ref, back_ref, out_ref, normed):
    norm_pages(place_ref, [(mine_ref, other_ref)], gain_ref, None, normed, None)
    out_ref[...] = expert_sums(normed[...], in_ref, back_ref)


vmem_spec = pl.BlockSpec(memory_space=pltpu.VMEM)
smem_spec = pl.BlockSpec(memory_space=pltpu.SMEM)


def expert_cost(rows, units, width):
    return pl.CostEstimate(
        flops=6 * rows * units * width,
        bytes_accessed=6 * units * width + 4 * rows * width,
        transcendentals=rows * units,
    )


def run_expert(tile_place, near, across, gain, lanes, in_rows, back_rows, extra):
    units, width = back_rows.shape
    page_rows = near.shape[2]
    rows = 4 * page_rows
    out = jax.ShapeDtypeStruct((2, page_rows, width), jnp.bfloat16)
    return pl.pallas_call(
        partial(expert_kernel, extra is not None),
        out_shape=(out, out),
        in_specs=[smem_spec] + [vmem_spec] * (6 + (extra is not None)),
        out_specs=(vmem_spec, vmem_spec),
        scratch_shapes=[
            pltpu.VMEM((rows, width), jnp.bfloat16),
            pltpu.VMEM((rows, 1), jnp.float32),
        ],
        compiler_params=pltpu.CompilerParams(vmem_limit_bytes=16 * 2**20),
        cost_estimate=expert_cost(rows, units, width),
        name="expert_units",
    )(
        tile_place,
        near,
        across,
        gain,
        lanes,
        in_rows,
        back_rows,
        *(() if extra is None else (extra,)),
    )


def run_shared(tile_place, mine, other, gain, in_rows, back_rows):
    units, width = back_rows.shape
    rows = mine.shape[0]
    return pl.pallas_call(
        shared_kernel,
        out_shape=jax.ShapeDtypeStruct((rows, width), jnp.float32),
        in_specs=[smem_spec] + [vmem_spec] * 5,
        out_specs=vmem_spec,
        scratch_shapes=[
            pltpu.VMEM((rows, width), jnp.bfloat16),
        ],
        compiler_params=pltpu.CompilerParams(vmem_limit_bytes=16 * 2**20),
        cost_estimate=expert_cost(rows, units, width),
        name="shared_units",
    )(tile_place, mine, other, gain, in_rows, back_rows)


def project_heads(rows_ref, gain_ref, weight_ref, bias_ref, cos_ref, sin_ref, heads):
    normed = layer_norm(rows_ref[...].astype(jnp.float32), gain_ref[...]).astype(jnp.bfloat16)
    quarter = HD // 4
    outs = []
    for which in range(3):
        mixed = (
            lax.dot_general(
                weight_ref[which],
                normed,
                (((1,), (1,)), ((), ())),
                preferred_element_type=jnp.float32,
            )
            + bias_ref[which]
        ).reshape(heads, HD, normed.shape[0])
        if which < 2:
            parts = [mixed[:, n * quarter : (n + 1) * quarter] for n in range(4)]
            partner = jnp.concatenate([-parts[1], parts[0], -parts[3], parts[2]], axis=1)
            mixed = mixed * cos_ref[...][None] + partner * sin_ref[...][None]
        outs.append(mixed.astype(jnp.bfloat16))
    return outs


def attend_heads(query, keys, values, heads):
    turned = (((0,), (0,)), ((), ()))
    outs = []
    for head in range(heads):
        scores = lax.dot_general(
            keys[head], query[head], turned, preferred_element_type=jnp.float32
        ) * (1.0 / math.sqrt(HD))
        raised = jnp.exp(scores - jnp.max(scores, axis=0, keepdims=True))
        probs = (raised / jnp.sum(raised, axis=0, keepdims=True)).astype(jnp.bfloat16)
        outs.append(jnp.dot(values[head], probs, preferred_element_type=jnp.float32))
    return jnp.concatenate(outs, axis=0).astype(jnp.bfloat16)


def own_heads_kernel(heads, *refs):
    rows_ref, gain_ref, bias_ref, cos_ref, sin_ref, weight_ref, out_ref = refs
    outs = project_heads(rows_ref, gain_ref, weight_ref, bias_ref, cos_ref, sin_ref, heads)
    for which, values in enumerate(outs):
        out_ref[which] = values


def other_rows_kernel(heads, *refs):
    rows_ref, gain_ref, bias_ref, cos_ref, sin_ref, weight_ref, own_ref, back_ref = refs[:8]
    part_ref, keys_ref = refs[8:]
    query, other_keys, other_values = project_heads(
        rows_ref, gain_ref, weight_ref, bias_ref, cos_ref, sin_ref, heads
    )
    keys = jnp.concatenate([own_ref[1], other_keys], axis=2)
    values = jnp.concatenate([own_ref[2], other_values], axis=2)
    keys_ref[0] = keys
    keys_ref[1] = values
    attended = attend_heads(query, keys, values, heads)
    part_ref[...] = lax.dot_general(
        attended, back_ref[...], (((0,), (0,)), ((), ())), preferred_element_type=jnp.float32
    ).astype(jnp.bfloat16)


def own_rows_kernel(heads, *refs):
    rows_ref, own_ref, keys_ref, back_ref, bias_ref, out_ref = refs
    attended = attend_heads(own_ref[0], keys_ref[0], keys_ref[1], heads)
    out_ref[...] = (
        rows_ref[...].astype(jnp.float32)
        + bias_ref[...]
        + lax.dot_general(
            attended, back_ref[...], (((0,), (0,)), ((), ())), preferred_element_type=jnp.float32
        )
    )


def merge_kernel(columns, hidden_ref, arrived_ref, gain_ref, merged_ref, scratch):
    normed = layer_norm(hidden_ref[...] + arrived_ref[...].astype(jnp.float32), gain_ref[...])
    slabs = scratch.shape[0]
    for slab in range(slabs):
        scratch[slab] = normed[:, slab * 128 : (slab + 1) * 128]
    count = columns // 2
    for pair in range(normed.shape[0] // (2 * columns)):
        for parity in range(2):
            rows = [
                scratch[slab, pl.ds((2 * pair + parity) * columns + side, count, stride=2)]
                for side in range(2)
                for slab in range(slabs)
            ]
            merged = jnp.concatenate(rows, axis=1).astype(jnp.bfloat16)
            for tile in range(2):
                merged_ref[tile, parity, pl.ds(pair * count, count)] = merged


def projector_kernel(spots_ref, place_ref, rows_ref, *refs):
    weight_refs, own_out, far_out, blocks = refs[:-3], refs[-3], refs[-2], refs[-1]
    count, size = rows_ref.shape[2], weight_refs[0].shape[0]
    for tile in range(2):
        for half in range(2):
            far = place_ref[0] ^ half
            spot = pl.ds(pl.multiple_of((2 * far + tile) * count, count), count)
            for number in range(len(weight_refs)):
                blocks[number, spot] = rows_ref[tile, half, :, number * size : (number + 1) * size]
    total = None
    for number, weight_ref in enumerate(weight_refs):
        part = jnp.dot(
            blocks[spots_ref[number]], weight_ref[...], preferred_element_type=jnp.float32
        )
        total = part if total is None else total + part
    own_out[...] = total[: 2 * count]
    far_out[...] = total[2 * count :].astype(jnp.bfloat16)


def run_projector(spots, place, rows, weights):
    count, size, width = rows.shape[2], weights[0].shape[0], weights[0].shape[1]
    return pl.pallas_call(
        projector_kernel,
        out_shape=(
            jax.ShapeDtypeStruct((2 * count, width), jnp.float32),
            jax.ShapeDtypeStruct((2 * count, width), jnp.bfloat16),
        ),
        in_specs=[smem_spec] * 2 + [vmem_spec] * (1 + len(weights)),
        out_specs=(vmem_spec, vmem_spec),
        scratch_shapes=[pltpu.VMEM((len(weights), 4 * count, size), jnp.bfloat16)],
        compiler_params=pltpu.CompilerParams(vmem_limit_bytes=16 * 2**20),
        cost_estimate=pl.CostEstimate(
            flops=8 * count * width * size * len(weights),
            bytes_accessed=2 * width * size * len(weights),
            transcendentals=0,
        ),
        name="projector",
    )(spots, place, rows, *weights)


def per_device_near(
    patches,
    norm1_gain,
    qkv_weight,
    qkv_bias,
    out_weight,
    out_bias,
    norm2_gain,
    proj_weight,
    moe_gain,
    expert_in,
    expert_out,
    shared_in,
    shared_out,
    routes,
    gates,
):
    experts_count = lax.axis_size(near_expert)
    outer = experts_count // 4
    swap = partial(near_swap, grid=(2, outer, 2, 2))
    tile_id = lax.axis_index("tile")
    expert_id = lax.axis_index(near_expert)
    outer_id, inner_id, core_id = expert_id // 4, (expert_id // 2) % 2, expert_id % 2
    row_count, columns, width_vit = patches.shape[1:]
    local_rows = row_count * columns
    token_count = local_rows // 4

    def by_place(place, mine, other):
        first = place == 0
        return jnp.where(first, mine, other), jnp.where(first, other, mine)

    def after(values, earlier):
        return lax.optimization_barrier((values, earlier))[0]

    own_patches = patches.reshape(local_rows, width_vit)
    other_patches = swap(own_patches, flips=(1, 0, 0, 0))
    tile_place = tile_id.astype(jnp.int32).reshape(1)

    top_count = routes.shape[-1]
    page_routes = routes.reshape(2, token_count, top_count)
    own_routes = lax.dynamic_index_in_dim(page_routes, tile_id, 0, keepdims=False)
    own_gates = gates.reshape(token_count, top_count)
    dense_gates = jnp.sum(
        jnp.where(
            own_routes[:, :, None] == jnp.arange(experts_count)[None, None, :],
            own_gates[:, :, None],
            0.0,
        ),
        axis=1,
    )
    gates_high = lax.reduce_precision(dense_gates, 8, 7)
    gate_lanes = jnp.concatenate([gates_high, dense_gates - gates_high], axis=1)
    gate_width = gate_lanes.shape[1]
    gate_lanes = jnp.pad(gate_lanes, ((0, 0), (0, 128 - gate_width))).astype(jnp.bfloat16)
    gate_rows = jnp.concatenate(
        by_place(tile_id, gate_lanes, jnp.zeros_like(gate_lanes)), axis=0
    )
    expert_lanes = jnp.arange(128) % experts_count == expert_id
    expert_lanes = (expert_lanes & (jnp.arange(128) < gate_width)).astype(jnp.float32)

    heads = qkv_weight.shape[2] // HD
    weight_rows = qkv_weight.transpose(1, 2, 0)
    bias_rows = qkv_bias[:, :, None]
    quarter = HD // 4
    feature = jnp.arange(HD)
    inverse = jnp.exp(
        (feature % quarter).astype(jnp.float32) * (-math.log(rope_base) / quarter)
    )[:, None]
    position = jnp.arange(local_rows)

    def tables(tile):
        rows = (tile * row_count + position // columns).astype(jnp.float32)[None]
        cols = (position % columns).astype(jnp.float32)[None]
        angles = jnp.where((feature < 2 * quarter)[:, None], rows, cols) * inverse
        return jnp.cos(angles), jnp.sin(angles)

    own_tables = tables(tile_id)
    gain_first, gain_second = norm1_gain[None], norm2_gain[None]
    head_rows = (heads, HD, local_rows)
    params = pltpu.CompilerParams(vmem_limit_bytes=16 * 2**20)
    macs = local_rows * width_vit * heads * HD
    own_heads = pl.pallas_call(
        partial(own_heads_kernel, heads),
        out_shape=jax.ShapeDtypeStruct((3, *head_rows), jnp.bfloat16),
        in_specs=[vmem_spec] * 6,
        out_specs=vmem_spec,
        compiler_params=params,
        cost_estimate=pl.CostEstimate(
            flops=6 * macs, bytes_accessed=2 * weight_rows.size, transcendentals=0
        ),
        name="own_heads",
    )(own_patches, gain_first, bias_rows, *own_tables, weight_rows)
    other_part, keys_values = pl.pallas_call(
        partial(other_rows_kernel, heads),
        out_shape=(
            jax.ShapeDtypeStruct((local_rows, width_vit), jnp.bfloat16),
            jax.ShapeDtypeStruct((2, heads, HD, 2 * local_rows), jnp.bfloat16),
        ),
        in_specs=[vmem_spec] * 8,
        out_specs=(vmem_spec, vmem_spec),
        compiler_params=params,
        cost_estimate=pl.CostEstimate(
            flops=10 * macs, bytes_accessed=2 * weight_rows.size, transcendentals=0
        ),
        name="other_rows",
    )(
        other_patches,
        gain_first,
        bias_rows,
        *tables(1 - tile_id),
        weight_rows,
        own_heads,
        out_weight,
    )
    arrived_part = swap(other_part, flips=(1, 0, 0, 0))
    hidden = pl.pallas_call(
        partial(own_rows_kernel, heads),
        out_shape=jax.ShapeDtypeStruct((local_rows, width_vit), jnp.float32),
        in_specs=[vmem_spec] * 5,
        out_specs=vmem_spec,
        compiler_params=params,
        cost_estimate=pl.CostEstimate(
            flops=4 * macs, bytes_accessed=2 * out_weight.size, transcendentals=0
        ),
        name="own_rows",
    )(own_patches, own_heads, keys_values, out_weight, out_bias[None])
    merged = pl.pallas_call(
        partial(merge_kernel, columns),
        out_shape=jax.ShapeDtypeStruct((2, 2, token_count, 2 * width_vit), jnp.bfloat16),
        in_specs=[vmem_spec] * 3,
        out_specs=vmem_spec,
        scratch_shapes=[pltpu.VMEM((width_vit // 128, local_rows, 128), jnp.float32)],
        compiler_params=params,
        name="merge_windows",
    )(hidden, arrived_part, gain_second)

    proj_blocks, proj_spots = [], []
    held_rows = after(proj_weight, own_tables)
    for low in range(outer // 2):
        for inner in range(2):
            rows = swap(held_rows, flips=(0, low, inner, 0)) if low or inner else proj_weight
            for core, block in enumerate(
                (rows, swap(after(rows, merged), flips=(0, 0, 0, 1)))
            ):
                proj_blocks.append(block)
                proj_spots.append(
                    ((outer_id ^ low) % (outer // 2)) * 4
                    + (inner_id ^ inner) * 2
                    + (core_id ^ core)
                )
    proj_spots = jnp.stack(proj_spots).astype(jnp.int32)

    far = outer // 2
    merged = lax.all_to_all(
        merged.reshape(4, token_count, -1), ("tile", "half"), split_axis=0, concat_axis=0, tiled=True
    ).reshape(merged.shape)
    page_tokens = 2 * token_count
    half_place = (outer_id // far).astype(jnp.int32).reshape(1)
    own_tokens, far_tokens = run_projector(proj_spots, half_place, merged, proj_blocks)
    far_part = swap(far_tokens, flips=(0, far, 0, 0))
    tokens_half = (own_tokens + far_part.astype(jnp.float32)).astype(jnp.bfloat16)

    width_moe = 2 * tokens_half.shape[1]
    expert_units = expert_in[0].transpose(1, 2, 0)
    shared_units = shared_in.transpose(1, 2, 0)
    gain_row, lane_row = moe_gain[None], expert_lanes[None]
    half_moe = tokens_half.shape[1]
    held = jnp.concatenate([tokens_half, gate_rows], axis=1)
    held_by_step = [held] + [swap(held, flips=(0, step, 0, 0)) for step in range(1, outer)]
    tile_flip, inner_flip, core_flip = (1, 0, 0, 0), (0, 0, 1, 0), (0, 0, 0, 1)
    def add(mine, other):
        return (mine.astype(jnp.float32) + other.astype(jnp.float32)).astype(jnp.bfloat16)

    flips_of = [
        (inner_flip, tile_flip) if step % 2 else (tile_flip, inner_flip) for step in range(outer)
    ]
    near_blocks, first_sums, kept_sums = [], [], []
    for step, held in enumerate(held_by_step):
        arrived = swap(held, flips=flips_of[step][0])
        if step == 0:
            own_held, tile_held = held, arrived
        held = jnp.stack([held, arrived])
        held = jnp.stack([held, swap(held, flips=flips_of[step][1])])
        near_blocks.append(held.transpose(1, 0, 2, 3) if step % 2 else held)
    residual = jnp.concatenate(
        by_place(
            tile_id,
            *(
                lax.dynamic_slice_in_dim(
                    rows[:, :half_moe], tile_id * token_count, token_count, 0
                )
                for rows in (own_held, tile_held)
            ),
        ),
        axis=1,
    )
    shared_sums = run_shared(
        tile_place, after(own_held, near_blocks[0]), tile_held, gain_row, shared_units, shared_out
    )
    across_blocks = [swap(near, flips=core_flip) for near in near_blocks]
    for step, (near, across) in enumerate(zip(near_blocks, across_blocks)):
        if step > 1:
            near = after(near, first_sums[step - 2])
        own_sums, across_sums = run_expert(
            tile_place,
            near,
            across,
            gain_row,
            lane_row,
            expert_units,
            expert_out[0],
            None if step else shared_sums,
        )
        summed = add(own_sums, swap(across_sums, flips=core_flip)).reshape(
            2, 2, token_count, width_moe
        )
        if step % 2:
            stays, leaves = summed[0], summed[1]
        else:
            stays, leaves = by_place(tile_id, summed[:, 0], summed[:, 1])
        first_sums.append(leaves)
        kept_sums.append(stays)
    total = residual.astype(jnp.float32)
    for step, (stays, leaves) in enumerate(zip(kept_sums, first_sums)):
        summed = add(stays, swap(leaves, flips=flips_of[step][0]))
        if step % 2:
            stays, leaves = by_place(tile_id, summed[0], summed[1])
        else:
            stays, leaves = summed[0], summed[1]
        summed = add(stays, swap(leaves, flips=flips_of[step][1]))
        if step:
            summed = swap(summed, flips=(0, step, 0, 0))
        total = total + summed.astype(jnp.float32)
    return total.astype(jnp.bfloat16).reshape(1, row_count // 2, columns // 2, width_moe)


def solution(mesh):
    expert = "expert"
    near = mesh.shape["tile"] == 2 and mesh.shape["expert"] == 16
    if near:
        mesh = jax.sharding.Mesh(mesh.devices.reshape(2, 2, 2, 2, 2), ("tile", *near_expert))
        expert = near_expert
    placed = (
        P(expert, "tile", None, None),
        P(),
        P(None, None, "tile"),
        P(None, "tile"),
        P("tile", None),
        P(),
        P(),
        P(expert, "tile"),
        P(),
        P(expert, None, None, "tile"),
        P(expert, "tile", None),
        P(None, None, "tile"),
        P("tile", None),
        P(expert, None, None, None),
        P(expert, "tile", None, None),
    )
    return jax.shard_map(
        per_device_near if near else per_device_slots,
        mesh=mesh,
        in_specs=placed,
        out_specs=P(expert, "tile", None, None),
        check_vma=False,
    )
```

```python
from functools import partial
import math

import jax
import jax.numpy as jnp
from jax import lax
from jax.experimental import pallas as pl
from jax.experimental.pallas import tpu as pltpu
from jax.sharding import PartitionSpec as P

HD = 72


norm_eps = 1e-06
rope_base = 10000.0


def layer_norm(values, gain_vec):
    centre = values - jnp.mean(values, axis=-1, keepdims=True)
    spread = jnp.mean(centre * centre, axis=-1, keepdims=True)
    return centre * lax.rsqrt(spread + norm_eps) * gain_vec


def rms_norm(values, gain_vec):
    return (
        values * lax.rsqrt(jnp.mean(values * values, axis=-1, keepdims=True) + norm_eps) * gain_vec
    )


def rope_tables(positions, columns, head_size):
    quarter = head_size // 4
    inverse = jnp.exp(jnp.arange(quarter).astype(jnp.float32) * (-math.log(rope_base) / quarter))
    row_angle = (positions // columns).astype(jnp.float32)[:, None] * inverse[None, :]
    col_angle = (positions % columns).astype(jnp.float32)[:, None] * inverse[None, :]
    return (jnp.cos(row_angle), jnp.sin(row_angle), jnp.cos(col_angle), jnp.sin(col_angle))


def rotate(values, tables):
    cos_row, sin_row, cos_col, sin_col = tables
    quarter = values.shape[-1] // 4
    row_a = values[..., :quarter]
    row_b = values[..., quarter : 2 * quarter]
    col_a = values[..., 2 * quarter : 3 * quarter]
    col_b = values[..., 3 * quarter :]
    return jnp.concatenate(
        [
            row_a * cos_row[:, None] - row_b * sin_row[:, None],
            row_b * cos_row[:, None] + row_a * sin_row[:, None],
            col_a * cos_col[:, None] - col_b * sin_col[:, None],
            col_b * cos_col[:, None] + col_a * sin_col[:, None],
        ],
        axis=-1,
    )


def attend(query_rows, key_rows, value_rows, divisor):
    count = query_rows.shape[0]
    width = min(count, 512)
    blocks = query_rows.reshape(count // width, width, query_rows.shape[1], query_rows.shape[2])

    def one_block(block):
        scores = (
            jnp.einsum("qhd,khd->hqk", block, key_rows, preferred_element_type=jnp.float32)
            / divisor
        )
        weights = jax.nn.softmax(scores, axis=-1).astype(jnp.bfloat16)
        return jnp.einsum(
            "hqk,khd->qhd", weights, value_rows, preferred_element_type=jnp.float32
        ).astype(jnp.bfloat16)

    return lax.map(one_block, blocks).reshape(count, -1)


def block_slots(block_routes, experts_count, capacity):
    picks = block_routes.reshape(-1)
    onehot = (picks[:, None] == jnp.arange(experts_count)[None, :]).astype(jnp.int32)
    earlier = jnp.cumsum(onehot, axis=0) - onehot
    ranks = jnp.sum(earlier * onehot, axis=1)
    owners_flat = jnp.arange(picks.shape[0]) // block_routes.shape[1]
    table = (
        jnp.full((experts_count * capacity,), -1, dtype=jnp.int32)
        .at[picks * capacity + ranks]
        .set(owners_flat)
    )
    return (ranks.reshape(block_routes.shape), table.reshape(experts_count, capacity))


def per_device_slots(
    patches,
    norm1_gain,
    qkv_weight,
    qkv_bias,
    out_weight,
    out_bias,
    norm2_gain,
    proj_weight,
    moe_gain,
    expert_in,
    expert_out,
    shared_in,
    shared_out,
    routes,
    gates,
):
    tiles = lax.axis_size("tile")
    experts_count = lax.axis_size("expert")
    tile_id = lax.axis_index("tile")
    row_count = patches.shape[1]
    columns = patches.shape[2]
    width_vit = patches.shape[3]
    local_rows = row_count * columns
    inputs = patches.reshape(local_rows, width_vit).astype(jnp.float32)
    normed = layer_norm(inputs, norm1_gain).astype(jnp.bfloat16)
    heads_here = qkv_weight.shape[2] // HD
    qkv_flat = qkv_weight.reshape(width_vit, -1)
    bias_rows = qkv_bias.reshape(1, 3, heads_here, HD)
    piece = lax.all_gather(normed, "tile", axis=0, tiled=True)
    mixed = (
        jnp.dot(piece, qkv_flat, preferred_element_type=jnp.float32).reshape(
            piece.shape[0], 3, heads_here, HD
        )
        + bias_rows
    )
    tables = rope_tables(jnp.arange(piece.shape[0]), columns, HD)
    page_qkv = jnp.stack(
        [rotate(mixed[:, 0], tables), rotate(mixed[:, 1], tables), mixed[:, 2]], axis=1
    ).astype(jnp.bfloat16)
    attended = attend(page_qkv[:, 0], page_qkv[:, 1], page_qkv[:, 2], math.sqrt(HD))
    mixed_heads = lax.psum_scatter(
        jnp.dot(attended, out_weight, preferred_element_type=jnp.float32).astype(jnp.bfloat16),
        "tile",
        scatter_dimension=0,
        tiled=True,
    ).astype(jnp.float32)
    hidden = inputs + mixed_heads + out_bias
    normed_out = layer_norm(hidden, norm2_gain).astype(jnp.bfloat16)
    merged = (
        normed_out.reshape(row_count // 2, 2, columns // 2, 2, width_vit)
        .transpose(0, 2, 1, 3, 4)
        .reshape(-1, 4 * width_vit)
    )
    merged_count = merged.shape[0]
    group_merged = lax.all_gather(merged, "tile", axis=0, tiled=True)
    projected = jnp.dot(
        group_merged,
        lax.all_gather(proj_weight, "expert", axis=0, tiled=True),
        preferred_element_type=jnp.float32,
    ).astype(jnp.bfloat16)
    tokens_moe = lax.all_to_all(projected, "tile", split_axis=0, concat_axis=1, tiled=True)
    width_moe = tokens_moe.shape[1]
    moe_in = rms_norm(tokens_moe.astype(jnp.float32), moe_gain).astype(jnp.bfloat16)
    group_in = lax.all_gather(moe_in, "tile", axis=0, tiled=True)
    shared_gated = jnp.dot(
        group_in, shared_in.reshape(width_moe, -1), preferred_element_type=jnp.float32
    ).reshape(group_in.shape[0], 2, -1)
    shared_hidden = (jax.nn.silu(shared_gated[:, 0]) * shared_gated[:, 1]).astype(jnp.bfloat16)
    shared_part = lax.psum_scatter(
        jnp.dot(shared_hidden, shared_out, preferred_element_type=jnp.float32).astype(jnp.bfloat16),
        "tile",
        scatter_dimension=0,
        tiled=True,
    ).astype(jnp.float32)
    top_count = routes.shape[-1]
    capacity = max(2, min(merged_count, 2 * merged_count * top_count // experts_count))
    group_routes = routes.reshape(tiles, merged_count, top_count)
    group_ranks, group_owners = jax.vmap(
        partial(block_slots, experts_count=experts_count, capacity=capacity)
    )(group_routes)
    own_routes = lax.dynamic_index_in_dim(group_routes, tile_id, 0, keepdims=False)
    own_ranks = lax.dynamic_index_in_dim(group_ranks, tile_id, 0, keepdims=False)
    empty_value = jnp.zeros((), jnp.bfloat16)
    table = lax.dynamic_index_in_dim(group_owners, tile_id, 0, keepdims=False)
    used = table >= 0
    outgoing = jnp.where(used[..., None], moe_in[jnp.where(used, table, 0)], empty_value)
    received = lax.all_to_all(outgoing, "expert", split_axis=0, concat_axis=0, tiled=True)
    arrived = lax.all_gather(received[:, None], "tile", axis=1, tiled=True)
    slot_rows = arrived.reshape(-1, width_moe)
    gated = jnp.dot(
        slot_rows, expert_in.reshape(width_moe, -1), preferred_element_type=jnp.float32
    ).reshape(slot_rows.shape[0], 2, -1)
    expert_hidden = (jax.nn.silu(gated[:, 0]) * gated[:, 1]).astype(jnp.bfloat16)
    partial_out = (
        jnp.dot(
            expert_hidden,
            expert_out.reshape(expert_hidden.shape[1], width_moe),
            preferred_element_type=jnp.float32,
        )
        .astype(jnp.bfloat16)
        .reshape(arrived.shape)
    )
    came_back = lax.all_to_all(partial_out, "expert", split_axis=0, concat_axis=0, tiled=True)
    returned = lax.psum_scatter(
        came_back.astype(jnp.float32).astype(jnp.bfloat16), "tile", scatter_dimension=1, tiled=True
    )
    results_flat = returned.reshape(experts_count * capacity, width_moe)
    pick_index = own_routes * capacity + own_ranks
    gate_rows = gates.reshape(merged_count, top_count)
    routed = jnp.zeros((merged_count, width_moe), jnp.float32)
    for position in range(top_count):
        routed = routed + gate_rows[:, position : position + 1] * results_flat[
            pick_index[:, position]
        ].astype(jnp.float32)
    output = tokens_moe.astype(jnp.float32) + shared_part + routed
    return output.astype(jnp.bfloat16).reshape(1, row_count // 2, columns // 2, width_moe)


near_expert = ("half", "outer", "inner", "core")


def near_swap(values, grid, flips):
    pairs = []
    for source in range(math.prod(grid)):
        place, rest = [], source
        for size in reversed(grid):
            place.append(rest % size)
            rest //= size
        target = 0
        for spot, size, flip in zip(reversed(place), grid, flips):
            target = target * size + (spot ^ flip)
        pairs.append((source, target))
    return lax.ppermute(values, ("tile", *near_expert), pairs)


def expert_sums(normed, in_ref, back_ref):
    units = back_ref.shape[0]
    wide = (((1,), (1,)), ((), ()))
    total = None
    for begin in range(0, units, 256):
        rows = pl.ds(begin, min(256, units - begin))
        gate = lax.dot_general(normed, in_ref[0, rows], wide, preferred_element_type=jnp.float32)
        up = lax.dot_general(normed, in_ref[1, rows], wide, preferred_element_type=jnp.float32)
        hidden = (gate / (1.0 + jnp.exp(-gate)) * up).astype(jnp.bfloat16)
        part = jnp.dot(hidden, back_ref[rows], preferred_element_type=jnp.float32)
        total = part if total is None else total + part
    return total


def norm_pages(place_ref, page_refs, gain_ref, lanes_ref, normed, weights):
    half = normed.shape[1] // 2
    first = pl.multiple_of(place_ref[0] * half, half)
    second = pl.multiple_of((1 - place_ref[0]) * half, half)
    for number, (mine_ref, other_ref) in enumerate(page_refs):
        mine = mine_ref[:, :half].astype(jnp.float32)
        other = other_ref[:, :half].astype(jnp.float32)
        squares = jnp.sum(mine * mine, axis=1, keepdims=True) + jnp.sum(
            other * other, axis=1, keepdims=True
        )
        scale = lax.rsqrt(squares / (2 * half) + norm_eps)
        count = mine.shape[0]
        rows = pl.ds(number * count, count)
        normed[rows, pl.ds(first, half)] = (mine * scale * gain_ref[:, pl.ds(first, half)]).astype(
            jnp.bfloat16
        )
        normed[rows, pl.ds(second, half)] = (
            other * scale * gain_ref[:, pl.ds(second, half)]
        ).astype(jnp.bfloat16)
        if weights is not None:
            lanes = mine_ref[:, half:].astype(jnp.float32) + other_ref[:, half:].astype(jnp.float32)
            weights[rows] = jnp.sum(lanes * lanes_ref[...], axis=1, keepdims=True)


def expert_kernel(extra, *refs):
    place_ref, near_ref, across_ref, gain_ref, lanes_ref, in_ref, back_ref = refs[:7]
    extra_ref = refs[7] if extra else None
    own_out, across_out, normed, weights = refs[7 + extra :]
    page_refs = [
        (ref.at[inner, 0], ref.at[inner, 1]) for ref in (near_ref, across_ref) for inner in range(2)
    ]
    norm_pages(place_ref, page_refs, gain_ref, lanes_ref, normed, weights)
    total = expert_sums(normed[...], in_ref, back_ref) * weights[...]
    count = total.shape[0] // 4
    for page in range(4):
        rows = total[page * count : (page + 1) * count]
        if extra and page == 0:
            rows = rows + extra_ref[...]
        target = own_out if page < 2 else across_out
        target[page % 2] = rows.astype(jnp.bfloat16)


def shared_kernel(place_ref, mine_ref, other_ref, gain_ref, in_ref, back_ref, out_ref, normed):
    norm_pages(place_ref, [(mine_ref, other_ref)], gain_ref, None, normed, None)
    out_ref[...] = expert_sums(normed[...], in_ref, back_ref)


vmem_spec = pl.BlockSpec(memory_space=pltpu.VMEM)
smem_spec = pl.BlockSpec(memory_space=pltpu.SMEM)
any_spec = pl.BlockSpec(memory_space=pl.ANY)


def expert_cost(rows, units, width):
    return pl.CostEstimate(
        flops=6 * rows * units * width,
        bytes_accessed=6 * units * width + 4 * rows * width,
        transcendentals=rows * units,
    )


def run_expert(tile_place, near, across, gain, lanes, in_rows, back_rows, extra):
    units, width = back_rows.shape
    page_rows = near.shape[2]
    rows = 4 * page_rows
    out = jax.ShapeDtypeStruct((2, page_rows, width), jnp.bfloat16)
    return pl.pallas_call(
        partial(expert_kernel, extra is not None),
        out_shape=(out, out),
        in_specs=[smem_spec] + [vmem_spec] * (6 + (extra is not None)),
        out_specs=(vmem_spec, vmem_spec),
        scratch_shapes=[
            pltpu.VMEM((rows, width), jnp.bfloat16),
            pltpu.VMEM((rows, 1), jnp.float32),
        ],
        compiler_params=pltpu.CompilerParams(vmem_limit_bytes=16 * 2**20),
        cost_estimate=expert_cost(rows, units, width),
        name="expert_units",
    )(
        tile_place,
        near,
        across,
        gain,
        lanes,
        in_rows,
        back_rows,
        *(() if extra is None else (extra,)),
    )


def run_shared(tile_place, mine, other, gain, in_rows, back_rows):
    units, width = back_rows.shape
    rows = mine.shape[0]
    return pl.pallas_call(
        shared_kernel,
        out_shape=jax.ShapeDtypeStruct((rows, width), jnp.float32),
        in_specs=[smem_spec] + [vmem_spec] * 5,
        out_specs=vmem_spec,
        scratch_shapes=[
            pltpu.VMEM((rows, width), jnp.bfloat16),
        ],
        compiler_params=pltpu.CompilerParams(vmem_limit_bytes=16 * 2**20),
        cost_estimate=expert_cost(rows, units, width),
        name="shared_units",
    )(tile_place, mine, other, gain, in_rows, back_rows)


def project_heads(rows_ref, gain_ref, weight_ref, bias_ref, cos_ref, sin_ref, heads):
    normed = layer_norm(rows_ref[...].astype(jnp.float32), gain_ref[...]).astype(jnp.bfloat16)
    quarter = HD // 4
    outs = []
    for which in range(3):
        mixed = (
            lax.dot_general(
                weight_ref[which],
                normed,
                (((1,), (1,)), ((), ())),
                preferred_element_type=jnp.float32,
            )
            + bias_ref[which]
        ).reshape(heads, HD, normed.shape[0])
        if which < 2:
            parts = [mixed[:, n * quarter : (n + 1) * quarter] for n in range(4)]
            partner = jnp.concatenate([-parts[1], parts[0], -parts[3], parts[2]], axis=1)
            mixed = mixed * cos_ref[...][None] + partner * sin_ref[...][None]
        outs.append(mixed.astype(jnp.bfloat16))
    return outs


def attend_heads(query, keys, values, heads):
    turned = (((0,), (0,)), ((), ()))
    outs = []
    for head in range(heads):
        scores = lax.dot_general(
            keys[head], query[head], turned, preferred_element_type=jnp.float32
        ) * (1.0 / math.sqrt(HD))
        raised = jnp.exp(scores - jnp.max(scores, axis=0, keepdims=True))
        probs = (raised / jnp.sum(raised, axis=0, keepdims=True)).astype(jnp.bfloat16)
        outs.append(jnp.dot(values[head], probs, preferred_element_type=jnp.float32))
    return jnp.concatenate(outs, axis=0).astype(jnp.bfloat16)


def own_heads_kernel(heads, *refs):
    rows_ref, gain_ref, bias_ref, cos_ref, sin_ref, weight_ref, out_ref = refs
    outs = project_heads(rows_ref, gain_ref, weight_ref, bias_ref, cos_ref, sin_ref, heads)
    for which, values in enumerate(outs):
        out_ref[which] = values


def other_rows_kernel(heads, *refs):
    rows_ref, gain_ref, bias_ref, cos_ref, sin_ref, weight_ref, own_ref, back_ref = refs[:8]
    part_ref, keys_ref = refs[8:]
    query, other_keys, other_values = project_heads(
        rows_ref, gain_ref, weight_ref, bias_ref, cos_ref, sin_ref, heads
    )
    keys = jnp.concatenate([own_ref[1], other_keys], axis=2)
    values = jnp.concatenate([own_ref[2], other_values], axis=2)
    keys_ref[0] = keys
    keys_ref[1] = values
    attended = attend_heads(query, keys, values, heads)
    part_ref[...] = lax.dot_general(
        attended, back_ref[...], (((0,), (0,)), ((), ())), preferred_element_type=jnp.float32
    ).astype(jnp.bfloat16)


def own_rows_kernel(heads, *refs):
    rows_ref, own_ref, keys_ref, back_ref, bias_ref, out_ref = refs
    attended = attend_heads(own_ref[0], keys_ref[0], keys_ref[1], heads)
    out_ref[...] = (
        rows_ref[...].astype(jnp.float32)
        + bias_ref[...]
        + lax.dot_general(
            attended, back_ref[...], (((0,), (0,)), ((), ())), preferred_element_type=jnp.float32
        )
    )


def merge_kernel(columns, hidden_ref, arrived_ref, gain_ref, merged_ref, scratch):
    normed = layer_norm(hidden_ref[...] + arrived_ref[...].astype(jnp.float32), gain_ref[...])
    slabs = scratch.shape[0]
    for slab in range(slabs):
        scratch[slab] = normed[:, slab * 128 : (slab + 1) * 128]
    count = columns // 2
    for pair in range(normed.shape[0] // (2 * columns)):
        for parity in range(2):
            rows = [
                scratch[slab, pl.ds((2 * pair + parity) * columns + side, count, stride=2)]
                for side in range(2)
                for slab in range(slabs)
            ]
            merged = jnp.concatenate(rows, axis=1).astype(jnp.bfloat16)
            for tile in range(2):
                merged_ref[tile, parity, pl.ds(pair * count, count)] = merged


def assemble_kernel(spots_ref, *refs):
    block_refs, rows_ref, arrivals = refs[:-2], refs[-2], refs[-1]
    copies = []
    for number, block_ref in enumerate(block_refs):
        size = block_ref.shape[0]
        spot = pl.ds(pl.multiple_of(spots_ref[number] * size, size), size)
        copies.append(
            pltpu.make_async_copy(block_ref, rows_ref.at[spot], arrivals.at[number])
        )
    for copy in copies:
        copy.start()
    for copy in copies:
        copy.wait()


def assemble_rows(spots, blocks):
    size, width = blocks[0].shape
    return pl.pallas_call(
        assemble_kernel,
        out_shape=jax.ShapeDtypeStruct((len(blocks) * size, width), blocks[0].dtype),
        in_specs=[smem_spec] + [any_spec] * len(blocks),
        out_specs=vmem_spec,
        scratch_shapes=[pltpu.SemaphoreType.DMA((len(blocks),))],
        compiler_params=pltpu.CompilerParams(vmem_limit_bytes=16 * 2**20),
        cost_estimate=pl.CostEstimate(
            flops=0, bytes_accessed=4 * len(blocks) * size * width, transcendentals=0
        ),
        name="assemble_rows",
    )(spots, *blocks)


def projector_kernel(place_ref, rows_ref, weight_ref, own_out, far_out):
    mine, other = (
        jnp.concatenate([rows_ref[tile, place_ref[0] ^ half] for tile in range(2)], axis=0)
        for half in range(2)
    )
    total = jnp.dot(
        jnp.concatenate([mine, other], axis=0), weight_ref[...], preferred_element_type=jnp.float32
    )
    count = mine.shape[0]
    own_out[...] = total[:count]
    far_out[...] = total[count:].astype(jnp.bfloat16)


def run_projector(place, rows, weight):
    count, (depth, width) = rows.shape[2], weight.shape
    return pl.pallas_call(
        projector_kernel,
        out_shape=(
            jax.ShapeDtypeStruct((2 * count, width), jnp.float32),
            jax.ShapeDtypeStruct((2 * count, width), jnp.bfloat16),
        ),
        in_specs=[smem_spec] + [vmem_spec] * 2,
        out_specs=(vmem_spec, vmem_spec),
        compiler_params=pltpu.CompilerParams(vmem_limit_bytes=16 * 2**20),
        cost_estimate=pl.CostEstimate(
            flops=8 * count * width * depth, bytes_accessed=2 * width * depth, transcendentals=0
        ),
        name="projector",
    )(place, rows, weight)


def finish_kernel(own_ref, arrived_ref, gates_ref, out_ref):
    width = own_ref.shape[1]
    out_ref[:, :width] = (own_ref[...] + arrived_ref[...].astype(jnp.float32)).astype(jnp.bfloat16)
    out_ref[:, width:] = gates_ref[...]


def per_device_near(
    patches,
    norm1_gain,
    qkv_weight,
    qkv_bias,
    out_weight,
    out_bias,
    norm2_gain,
    proj_weight,
    moe_gain,
    expert_in,
    expert_out,
    shared_in,
    shared_out,
    routes,
    gates,
):
    experts_count = lax.axis_size(near_expert)
    outer = experts_count // 4
    swap = partial(near_swap, grid=(2, outer, 2, 2))
    tile_id = lax.axis_index("tile")
    expert_id = lax.axis_index(near_expert)
    outer_id, inner_id, core_id = expert_id // 4, (expert_id // 2) % 2, expert_id % 2
    row_count, columns, width_vit = patches.shape[1:]
    local_rows = row_count * columns
    token_count = local_rows // 4

    def by_place(place, mine, other):
        first = place == 0
        return jnp.where(first, mine, other), jnp.where(first, other, mine)

    def after(values, earlier):
        return lax.optimization_barrier((values, earlier))[0]

    own_patches = patches.reshape(local_rows, width_vit)
    other_patches = swap(own_patches, flips=(1, 0, 0, 0))
    tile_place = tile_id.astype(jnp.int32).reshape(1)

    top_count = routes.shape[-1]
    page_routes = routes.reshape(2, token_count, top_count)
    own_routes = lax.dynamic_index_in_dim(page_routes, tile_id, 0, keepdims=False)
    own_gates = gates.reshape(token_count, top_count)
    dense_gates = jnp.sum(
        jnp.where(
            own_routes[:, :, None] == jnp.arange(experts_count)[None, None, :],
            own_gates[:, :, None],
            0.0,
        ),
        axis=1,
    )
    gates_high = lax.reduce_precision(dense_gates, 8, 7)
    gate_lanes = jnp.concatenate([gates_high, dense_gates - gates_high], axis=1)
    gate_width = gate_lanes.shape[1]
    gate_lanes = jnp.pad(gate_lanes, ((0, 0), (0, 128 - gate_width))).astype(jnp.bfloat16)
    gate_rows = jnp.concatenate(
        by_place(tile_id, gate_lanes, jnp.zeros_like(gate_lanes)), axis=0
    )
    expert_lanes = jnp.arange(128) % experts_count == expert_id
    expert_lanes = (expert_lanes & (jnp.arange(128) < gate_width)).astype(jnp.float32)

    heads = qkv_weight.shape[2] // HD
    weight_rows = qkv_weight.transpose(1, 2, 0)
    bias_rows = qkv_bias[:, :, None]
    quarter = HD // 4
    feature = jnp.arange(HD)
    inverse = jnp.exp(
        (feature % quarter).astype(jnp.float32) * (-math.log(rope_base) / quarter)
    )[:, None]
    position = jnp.arange(local_rows)

    def tables(tile):
        rows = (tile * row_count + position // columns).astype(jnp.float32)[None]
        cols = (position % columns).astype(jnp.float32)[None]
        angles = jnp.where((feature < 2 * quarter)[:, None], rows, cols) * inverse
        return jnp.cos(angles), jnp.sin(angles)

    own_tables = tables(tile_id)
    gain_first, gain_second = norm1_gain[None], norm2_gain[None]
    head_rows = (heads, HD, local_rows)
    params = pltpu.CompilerParams(vmem_limit_bytes=16 * 2**20)
    macs = local_rows * width_vit * heads * HD
    own_heads = pl.pallas_call(
        partial(own_heads_kernel, heads),
        out_shape=jax.ShapeDtypeStruct((3, *head_rows), jnp.bfloat16),
        in_specs=[vmem_spec] * 6,
        out_specs=vmem_spec,
        compiler_params=params,
        cost_estimate=pl.CostEstimate(
            flops=6 * macs, bytes_accessed=2 * weight_rows.size, transcendentals=0
        ),
        name="own_heads",
    )(own_patches, gain_first, bias_rows, *own_tables, weight_rows)
    other_part, keys_values = pl.pallas_call(
        partial(other_rows_kernel, heads),
        out_shape=(
            jax.ShapeDtypeStruct((local_rows, width_vit), jnp.bfloat16),
            jax.ShapeDtypeStruct((2, heads, HD, 2 * local_rows), jnp.bfloat16),
        ),
        in_specs=[vmem_spec] * 8,
        out_specs=(vmem_spec, vmem_spec),
        compiler_params=params,
        cost_estimate=pl.CostEstimate(
            flops=10 * macs, bytes_accessed=2 * weight_rows.size, transcendentals=0
        ),
        name="other_rows",
    )(
        other_patches,
        gain_first,
        bias_rows,
        *tables(1 - tile_id),
        weight_rows,
        own_heads,
        out_weight,
    )
    arrived_part = swap(other_part, flips=(1, 0, 0, 0))
    hidden = pl.pallas_call(
        partial(own_rows_kernel, heads),
        out_shape=jax.ShapeDtypeStruct((local_rows, width_vit), jnp.float32),
        in_specs=[vmem_spec] * 5,
        out_specs=vmem_spec,
        compiler_params=params,
        cost_estimate=pl.CostEstimate(
            flops=4 * macs, bytes_accessed=2 * out_weight.size, transcendentals=0
        ),
        name="own_rows",
    )(own_patches, own_heads, keys_values, out_weight, out_bias[None])
    merged = pl.pallas_call(
        partial(merge_kernel, columns),
        out_shape=jax.ShapeDtypeStruct((2, 2, token_count, 2 * width_vit), jnp.bfloat16),
        in_specs=[vmem_spec] * 3,
        out_specs=vmem_spec,
        scratch_shapes=[pltpu.VMEM((width_vit // 128, local_rows, 128), jnp.float32)],
        compiler_params=params,
        name="merge_windows",
    )(hidden, arrived_part, gain_second)

    proj_blocks, proj_spots = [], []
    held_rows = after(proj_weight, own_tables)
    for low in range(outer // 2):
        for inner in range(2):
            rows = swap(held_rows, flips=(0, low, inner, 0)) if low or inner else proj_weight
            for core, block in enumerate(
                (rows, swap(after(rows, merged), flips=(0, 0, 0, 1)))
            ):
                proj_blocks.append(block)
                proj_spots.append(
                    ((outer_id ^ low) % (outer // 2)) * 4
                    + (inner_id ^ inner) * 2
                    + (core_id ^ core)
                )
    proj_spots = jnp.stack(proj_spots).astype(jnp.int32)

    far = outer // 2
    merged = lax.all_to_all(
        merged.reshape(4, token_count, -1), ("tile", "half"), split_axis=0, concat_axis=0, tiled=True
    ).reshape(merged.shape)
    page_tokens = 2 * token_count
    half_place = (outer_id // far).astype(jnp.int32).reshape(1)
    own_tokens, far_tokens = run_projector(
        half_place, merged, assemble_rows(proj_spots, proj_blocks)
    )
    far_part = swap(far_tokens, flips=(0, far, 0, 0))
    tokens_half = (own_tokens + far_part.astype(jnp.float32)).astype(jnp.bfloat16)

    width_moe = 2 * tokens_half.shape[1]
    expert_units = expert_in[0].transpose(1, 2, 0)
    shared_units = shared_in.transpose(1, 2, 0)
    gain_row, lane_row = moe_gain[None], expert_lanes[None]
    half_moe = tokens_half.shape[1]
    held = jnp.concatenate([tokens_half, gate_rows], axis=1)
    held_by_step = [held] + [swap(held, flips=(0, step, 0, 0)) for step in range(1, outer)]
    tile_flip, inner_flip, core_flip = (1, 0, 0, 0), (0, 0, 1, 0), (0, 0, 0, 1)
    def add(mine, other):
        return (mine.astype(jnp.float32) + other.astype(jnp.float32)).astype(jnp.bfloat16)

    flips_of = [
        (inner_flip, tile_flip) if step % 2 else (tile_flip, inner_flip) for step in range(outer)
    ]
    near_blocks, first_sums, kept_sums = [], [], []
    for step, held in enumerate(held_by_step):
        if step in ():
            over_tile, over_inner, over_both = (
                swap(held, flips=flip) for flip in (tile_flip, inner_flip, (1, 0, 1, 0))
            )
            near_blocks.append(
                jnp.stack([held, over_tile, over_inner, over_both]).reshape(2, 2, *held.shape)
            )
            continue
        arrived = swap(held, flips=flips_of[step][0])
        if step == 0:
            own_held, tile_held = held, arrived
        held = jnp.stack([held, arrived])
        held = jnp.stack([held, swap(held, flips=flips_of[step][1])])
        near_blocks.append(held.transpose(1, 0, 2, 3) if step % 2 else held)
    residual = jnp.concatenate(
        by_place(
            tile_id,
            *(
                lax.dynamic_slice_in_dim(
                    rows[:, :half_moe], tile_id * token_count, token_count, 0
                )
                for rows in (own_held, tile_held)
            ),
        ),
        axis=1,
    )
    shared_sums = run_shared(
        tile_place, after(own_held, near_blocks[0]), tile_held, gain_row, shared_units, shared_out
    )
    across_blocks = [swap(near, flips=core_flip) for near in near_blocks]
    for step, (near, across) in enumerate(zip(near_blocks, across_blocks)):
        if step > 1:
            near = after(near, first_sums[step - 2])
        own_sums, across_sums = run_expert(
            tile_place,
            near,
            across,
            gain_row,
            lane_row,
            expert_units,
            expert_out[0],
            None if step else shared_sums,
        )
        summed = add(own_sums, swap(across_sums, flips=core_flip)).reshape(
            2, 2, token_count, width_moe
        )
        if step % 2 and step not in (2, 3):
            stays, leaves = summed[0], summed[1]
        else:
            stays, leaves = by_place(tile_id, summed[:, 0], summed[:, 1])
        first_sums.append(leaves)
        kept_sums.append(stays)
    total = residual.astype(jnp.float32)
    for step, (stays, leaves) in enumerate(zip(kept_sums, first_sums)):
        if step in (2, 3):
            summed = (
                stays[0].astype(jnp.float32)
                + swap(leaves[0], flips=tile_flip).astype(jnp.float32)
                + swap(stays[1], flips=inner_flip).astype(jnp.float32)
                + swap(leaves[1], flips=(1, 0, 1, 0)).astype(jnp.float32)
            ).astype(jnp.bfloat16)
        else:
            summed = add(stays, swap(leaves, flips=flips_of[step][0]))
            if step % 2:
                stays, leaves = by_place(tile_id, summed[0], summed[1])
            else:
                stays, leaves = summed[0], summed[1]
            summed = add(stays, swap(leaves, flips=flips_of[step][1]))
        if step:
            summed = swap(summed, flips=(0, step, 0, 0))
        total = total + summed.astype(jnp.float32)
    return total.astype(jnp.bfloat16).reshape(1, row_count // 2, columns // 2, width_moe)


def solution(mesh):
    expert = "expert"
    near = mesh.shape["tile"] == 2 and mesh.shape["expert"] == 16
    if near:
        mesh = jax.sharding.Mesh(mesh.devices.reshape(2, 2, 2, 2, 2), ("tile", *near_expert))
        expert = near_expert
    placed = (
        P(expert, "tile", None, None),
        P(),
        P(None, None, "tile"),
        P(None, "tile"),
        P("tile", None),
        P(),
        P(),
        P(expert, "tile"),
        P(),
        P(expert, None, None, "tile"),
        P(expert, "tile", None),
        P(None, None, "tile"),
        P("tile", None),
        P(expert, None, None, None),
        P(expert, "tile", None, None),
    )
    return jax.shard_map(
        per_device_near if near else per_device_slots,
        mesh=mesh,
        in_specs=placed,
        out_specs=P(expert, "tile", None, None),
        check_vma=False,
    )
```

```python
from functools import partial
import math

import jax
import jax.numpy as jnp
from jax import lax
from jax.experimental import pallas as pl
from jax.experimental.pallas import tpu as pltpu
from jax.sharding import PartitionSpec as P

HD = 72


norm_eps = 1e-06
rope_base = 10000.0


def layer_norm(values, gain_vec):
    centre = values - jnp.mean(values, axis=-1, keepdims=True)
    spread = jnp.mean(centre * centre, axis=-1, keepdims=True)
    return centre * lax.rsqrt(spread + norm_eps) * gain_vec


def rms_norm(values, gain_vec):
    return (
        values * lax.rsqrt(jnp.mean(values * values, axis=-1, keepdims=True) + norm_eps) * gain_vec
    )


def rope_tables(positions, columns, head_size):
    quarter = head_size // 4
    inverse = jnp.exp(jnp.arange(quarter).astype(jnp.float32) * (-math.log(rope_base) / quarter))
    row_angle = (positions // columns).astype(jnp.float32)[:, None] * inverse[None, :]
    col_angle = (positions % columns).astype(jnp.float32)[:, None] * inverse[None, :]
    return (jnp.cos(row_angle), jnp.sin(row_angle), jnp.cos(col_angle), jnp.sin(col_angle))


def rotate(values, tables):
    cos_row, sin_row, cos_col, sin_col = tables
    quarter = values.shape[-1] // 4
    row_a = values[..., :quarter]
    row_b = values[..., quarter : 2 * quarter]
    col_a = values[..., 2 * quarter : 3 * quarter]
    col_b = values[..., 3 * quarter :]
    return jnp.concatenate(
        [
            row_a * cos_row[:, None] - row_b * sin_row[:, None],
            row_b * cos_row[:, None] + row_a * sin_row[:, None],
            col_a * cos_col[:, None] - col_b * sin_col[:, None],
            col_b * cos_col[:, None] + col_a * sin_col[:, None],
        ],
        axis=-1,
    )


def attend(query_rows, key_rows, value_rows, divisor):
    count = query_rows.shape[0]
    width = min(count, 512)
    blocks = query_rows.reshape(count // width, width, query_rows.shape[1], query_rows.shape[2])

    def one_block(block):
        scores = (
            jnp.einsum("qhd,khd->hqk", block, key_rows, preferred_element_type=jnp.float32)
            / divisor
        )
        weights = jax.nn.softmax(scores, axis=-1).astype(jnp.bfloat16)
        return jnp.einsum(
            "hqk,khd->qhd", weights, value_rows, preferred_element_type=jnp.float32
        ).astype(jnp.bfloat16)

    return lax.map(one_block, blocks).reshape(count, -1)


def block_slots(block_routes, experts_count, capacity):
    picks = block_routes.reshape(-1)
    onehot = (picks[:, None] == jnp.arange(experts_count)[None, :]).astype(jnp.int32)
    earlier = jnp.cumsum(onehot, axis=0) - onehot
    ranks = jnp.sum(earlier * onehot, axis=1)
    owners_flat = jnp.arange(picks.shape[0]) // block_routes.shape[1]
    table = (
        jnp.full((experts_count * capacity,), -1, dtype=jnp.int32)
        .at[picks * capacity + ranks]
        .set(owners_flat)
    )
    return (ranks.reshape(block_routes.shape), table.reshape(experts_count, capacity))


def per_device_slots(
    patches,
    norm1_gain,
    qkv_weight,
    qkv_bias,
    out_weight,
    out_bias,
    norm2_gain,
    proj_weight,
    moe_gain,
    expert_in,
    expert_out,
    shared_in,
    shared_out,
    routes,
    gates,
):
    tiles = lax.axis_size("tile")
    experts_count = lax.axis_size("expert")
    tile_id = lax.axis_index("tile")
    row_count = patches.shape[1]
    columns = patches.shape[2]
    width_vit = patches.shape[3]
    local_rows = row_count * columns
    inputs = patches.reshape(local_rows, width_vit).astype(jnp.float32)
    normed = layer_norm(inputs, norm1_gain).astype(jnp.bfloat16)
    heads_here = qkv_weight.shape[2] // HD
    qkv_flat = qkv_weight.reshape(width_vit, -1)
    bias_rows = qkv_bias.reshape(1, 3, heads_here, HD)
    piece = lax.all_gather(normed, "tile", axis=0, tiled=True)
    mixed = (
        jnp.dot(piece, qkv_flat, preferred_element_type=jnp.float32).reshape(
            piece.shape[0], 3, heads_here, HD
        )
        + bias_rows
    )
    tables = rope_tables(jnp.arange(piece.shape[0]), columns, HD)
    page_qkv = jnp.stack(
        [rotate(mixed[:, 0], tables), rotate(mixed[:, 1], tables), mixed[:, 2]], axis=1
    ).astype(jnp.bfloat16)
    attended = attend(page_qkv[:, 0], page_qkv[:, 1], page_qkv[:, 2], math.sqrt(HD))
    mixed_heads = lax.psum_scatter(
        jnp.dot(attended, out_weight, preferred_element_type=jnp.float32).astype(jnp.bfloat16),
        "tile",
        scatter_dimension=0,
        tiled=True,
    ).astype(jnp.float32)
    hidden = inputs + mixed_heads + out_bias
    normed_out = layer_norm(hidden, norm2_gain).astype(jnp.bfloat16)
    merged = (
        normed_out.reshape(row_count // 2, 2, columns // 2, 2, width_vit)
        .transpose(0, 2, 1, 3, 4)
        .reshape(-1, 4 * width_vit)
    )
    merged_count = merged.shape[0]
    group_merged = lax.all_gather(merged, "tile", axis=0, tiled=True)
    projected = jnp.dot(
        group_merged,
        lax.all_gather(proj_weight, "expert", axis=0, tiled=True),
        preferred_element_type=jnp.float32,
    ).astype(jnp.bfloat16)
    tokens_moe = lax.all_to_all(projected, "tile", split_axis=0, concat_axis=1, tiled=True)
    width_moe = tokens_moe.shape[1]
    moe_in = rms_norm(tokens_moe.astype(jnp.float32), moe_gain).astype(jnp.bfloat16)
    group_in = lax.all_gather(moe_in, "tile", axis=0, tiled=True)
    shared_gated = jnp.dot(
        group_in, shared_in.reshape(width_moe, -1), preferred_element_type=jnp.float32
    ).reshape(group_in.shape[0], 2, -1)
    shared_hidden = (jax.nn.silu(shared_gated[:, 0]) * shared_gated[:, 1]).astype(jnp.bfloat16)
    shared_part = lax.psum_scatter(
        jnp.dot(shared_hidden, shared_out, preferred_element_type=jnp.float32).astype(jnp.bfloat16),
        "tile",
        scatter_dimension=0,
        tiled=True,
    ).astype(jnp.float32)
    top_count = routes.shape[-1]
    capacity = max(2, min(merged_count, 2 * merged_count * top_count // experts_count))
    group_routes = routes.reshape(tiles, merged_count, top_count)
    group_ranks, group_owners = jax.vmap(
        partial(block_slots, experts_count=experts_count, capacity=capacity)
    )(group_routes)
    own_routes = lax.dynamic_index_in_dim(group_routes, tile_id, 0, keepdims=False)
    own_ranks = lax.dynamic_index_in_dim(group_ranks, tile_id, 0, keepdims=False)
    empty_value = jnp.zeros((), jnp.bfloat16)
    table = lax.dynamic_index_in_dim(group_owners, tile_id, 0, keepdims=False)
    used = table >= 0
    outgoing = jnp.where(used[..., None], moe_in[jnp.where(used, table, 0)], empty_value)
    received = lax.all_to_all(outgoing, "expert", split_axis=0, concat_axis=0, tiled=True)
    arrived = lax.all_gather(received[:, None], "tile", axis=1, tiled=True)
    slot_rows = arrived.reshape(-1, width_moe)
    gated = jnp.dot(
        slot_rows, expert_in.reshape(width_moe, -1), preferred_element_type=jnp.float32
    ).reshape(slot_rows.shape[0], 2, -1)
    expert_hidden = (jax.nn.silu(gated[:, 0]) * gated[:, 1]).astype(jnp.bfloat16)
    partial_out = (
        jnp.dot(
            expert_hidden,
            expert_out.reshape(expert_hidden.shape[1], width_moe),
            preferred_element_type=jnp.float32,
        )
        .astype(jnp.bfloat16)
        .reshape(arrived.shape)
    )
    came_back = lax.all_to_all(partial_out, "expert", split_axis=0, concat_axis=0, tiled=True)
    returned = lax.psum_scatter(
        came_back.astype(jnp.float32).astype(jnp.bfloat16), "tile", scatter_dimension=1, tiled=True
    )
    results_flat = returned.reshape(experts_count * capacity, width_moe)
    pick_index = own_routes * capacity + own_ranks
    gate_rows = gates.reshape(merged_count, top_count)
    routed = jnp.zeros((merged_count, width_moe), jnp.float32)
    for position in range(top_count):
        routed = routed + gate_rows[:, position : position + 1] * results_flat[
            pick_index[:, position]
        ].astype(jnp.float32)
    output = tokens_moe.astype(jnp.float32) + shared_part + routed
    return output.astype(jnp.bfloat16).reshape(1, row_count // 2, columns // 2, width_moe)


near_expert = ("half", "outer", "inner", "core")


def near_swap(values, grid, flips):
    pairs = []
    for source in range(math.prod(grid)):
        place, rest = [], source
        for size in reversed(grid):
            place.append(rest % size)
            rest //= size
        target = 0
        for spot, size, flip in zip(reversed(place), grid, flips):
            target = target * size + (spot ^ flip)
        pairs.append((source, target))
    return lax.ppermute(values, ("tile", *near_expert), pairs)


def expert_sums(normed, in_ref, back_ref):
    units = back_ref.shape[0]
    wide = (((1,), (1,)), ((), ()))
    total = None
    for begin in range(0, units, 256):
        rows = pl.ds(begin, min(256, units - begin))
        gate = lax.dot_general(normed, in_ref[0, rows], wide, preferred_element_type=jnp.float32)
        up = lax.dot_general(normed, in_ref[1, rows], wide, preferred_element_type=jnp.float32)
        hidden = (gate / (1.0 + jnp.exp(-gate)) * up).astype(jnp.bfloat16)
        part = jnp.dot(hidden, back_ref[rows], preferred_element_type=jnp.float32)
        total = part if total is None else total + part
    return total


def norm_pages(place_ref, page_refs, gain_ref, lanes_ref, normed, weights):
    half = normed.shape[1] // 2
    first = pl.multiple_of(place_ref[0] * half, half)
    second = pl.multiple_of((1 - place_ref[0]) * half, half)
    for number, (mine_ref, other_ref) in enumerate(page_refs):
        mine = mine_ref[:, :half].astype(jnp.float32)
        other = other_ref[:, :half].astype(jnp.float32)
        squares = jnp.sum(mine * mine, axis=1, keepdims=True) + jnp.sum(
            other * other, axis=1, keepdims=True
        )
        scale = lax.rsqrt(squares / (2 * half) + norm_eps)
        count = mine.shape[0]
        rows = pl.ds(number * count, count)
        normed[rows, pl.ds(first, half)] = (mine * scale * gain_ref[:, pl.ds(first, half)]).astype(
            jnp.bfloat16
        )
        normed[rows, pl.ds(second, half)] = (
            other * scale * gain_ref[:, pl.ds(second, half)]
        ).astype(jnp.bfloat16)
        if weights is not None:
            lanes = mine_ref[:, half:].astype(jnp.float32) + other_ref[:, half:].astype(jnp.float32)
            weights[rows] = jnp.sum(lanes * lanes_ref[...], axis=1, keepdims=True)


def expert_kernel(extra, *refs):
    place_ref, near_ref, across_ref, gain_ref, lanes_ref, in_ref, back_ref = refs[:7]
    extra_ref = refs[7] if extra else None
    own_out, across_out, normed, weights = refs[7 + extra :]
    page_refs = [
        (ref.at[inner, 0], ref.at[inner, 1]) for ref in (near_ref, across_ref) for inner in range(2)
    ]
    norm_pages(place_ref, page_refs, gain_ref, lanes_ref, normed, weights)
    total = expert_sums(normed[...], in_ref, back_ref) * weights[...]
    count = total.shape[0] // 4
    for page in range(4):
        rows = total[page * count : (page + 1) * count]
        if extra and page == 0:
            rows = rows + extra_ref[...]
        target = own_out if page < 2 else across_out
        target[page % 2] = rows.astype(jnp.bfloat16)


def shared_kernel(place_ref, mine_ref, other_ref, gain_ref, in_ref, back_ref, out_ref, normed):
    norm_pages(place_ref, [(mine_ref, other_ref)], gain_ref, None, normed, None)
    out_ref[...] = expert_sums(normed[...], in_ref, back_ref)


vmem_spec = pl.BlockSpec(memory_space=pltpu.VMEM)
smem_spec = pl.BlockSpec(memory_space=pltpu.SMEM)
any_spec = pl.BlockSpec(memory_space=pl.ANY)


def expert_cost(rows, units, width):
    return pl.CostEstimate(
        flops=6 * rows * units * width,
        bytes_accessed=6 * units * width + 4 * rows * width,
        transcendentals=rows * units,
    )


def run_expert(tile_place, near, across, gain, lanes, in_rows, back_rows, extra):
    units, width = back_rows.shape
    page_rows = near.shape[2]
    rows = 4 * page_rows
    out = jax.ShapeDtypeStruct((2, page_rows, width), jnp.bfloat16)
    return pl.pallas_call(
        partial(expert_kernel, extra is not None),
        out_shape=(out, out),
        in_specs=[smem_spec] + [vmem_spec] * (6 + (extra is not None)),
        out_specs=(vmem_spec, vmem_spec),
        scratch_shapes=[
            pltpu.VMEM((rows, width), jnp.bfloat16),
            pltpu.VMEM((rows, 1), jnp.float32),
        ],
        compiler_params=pltpu.CompilerParams(vmem_limit_bytes=16 * 2**20),
        cost_estimate=expert_cost(rows, units, width),
        name="expert_units",
    )(
        tile_place,
        near,
        across,
        gain,
        lanes,
        in_rows,
        back_rows,
        *(() if extra is None else (extra,)),
    )


def run_shared(tile_place, mine, other, gain, in_rows, back_rows):
    units, width = back_rows.shape
    rows = mine.shape[0]
    return pl.pallas_call(
        shared_kernel,
        out_shape=jax.ShapeDtypeStruct((rows, width), jnp.float32),
        in_specs=[smem_spec] + [vmem_spec] * 5,
        out_specs=vmem_spec,
        scratch_shapes=[
            pltpu.VMEM((rows, width), jnp.bfloat16),
        ],
        compiler_params=pltpu.CompilerParams(vmem_limit_bytes=16 * 2**20),
        cost_estimate=expert_cost(rows, units, width),
        name="shared_units",
    )(tile_place, mine, other, gain, in_rows, back_rows)


def project_heads(rows_ref, gain_ref, weight_ref, bias_ref, cos_ref, sin_ref, heads):
    normed = layer_norm(rows_ref[...].astype(jnp.float32), gain_ref[...]).astype(jnp.bfloat16)
    quarter = HD // 4
    outs = []
    for which in range(3):
        mixed = (
            lax.dot_general(
                weight_ref[which],
                normed,
                (((1,), (1,)), ((), ())),
                preferred_element_type=jnp.float32,
            )
            + bias_ref[which]
        ).reshape(heads, HD, normed.shape[0])
        if which < 2:
            parts = [mixed[:, n * quarter : (n + 1) * quarter] for n in range(4)]
            partner = jnp.concatenate([-parts[1], parts[0], -parts[3], parts[2]], axis=1)
            mixed = mixed * cos_ref[...][None] + partner * sin_ref[...][None]
        outs.append(mixed.astype(jnp.bfloat16))
    return outs


def attend_heads(query, keys, values, heads):
    turned = (((0,), (0,)), ((), ()))
    outs = []
    for head in range(heads):
        scores = lax.dot_general(
            keys[head], query[head], turned, preferred_element_type=jnp.float32
        ) * (1.0 / math.sqrt(HD))
        raised = jnp.exp(scores - jnp.max(scores, axis=0, keepdims=True))
        probs = (raised / jnp.sum(raised, axis=0, keepdims=True)).astype(jnp.bfloat16)
        outs.append(jnp.dot(values[head], probs, preferred_element_type=jnp.float32))
    return jnp.concatenate(outs, axis=0).astype(jnp.bfloat16)


def own_heads_kernel(heads, *refs):
    rows_ref, gain_ref, bias_ref, cos_ref, sin_ref, weight_ref, out_ref = refs
    outs = project_heads(rows_ref, gain_ref, weight_ref, bias_ref, cos_ref, sin_ref, heads)
    for which, values in enumerate(outs):
        out_ref[which] = values


def other_rows_kernel(heads, *refs):
    rows_ref, gain_ref, bias_ref, cos_ref, sin_ref, weight_ref, own_ref, back_ref = refs[:8]
    part_ref, keys_ref = refs[8:]
    query, other_keys, other_values = project_heads(
        rows_ref, gain_ref, weight_ref, bias_ref, cos_ref, sin_ref, heads
    )
    keys = jnp.concatenate([own_ref[1], other_keys], axis=2)
    values = jnp.concatenate([own_ref[2], other_values], axis=2)
    keys_ref[0] = keys
    keys_ref[1] = values
    attended = attend_heads(query, keys, values, heads)
    part_ref[...] = lax.dot_general(
        attended, back_ref[...], (((0,), (0,)), ((), ())), preferred_element_type=jnp.float32
    ).astype(jnp.bfloat16)


def own_rows_kernel(heads, *refs):
    rows_ref, own_ref, keys_ref, back_ref, bias_ref, out_ref = refs
    attended = attend_heads(own_ref[0], keys_ref[0], keys_ref[1], heads)
    out_ref[...] = (
        rows_ref[...].astype(jnp.float32)
        + bias_ref[...]
        + lax.dot_general(
            attended, back_ref[...], (((0,), (0,)), ((), ())), preferred_element_type=jnp.float32
        )
    )


def merge_kernel(columns, hidden_ref, arrived_ref, gain_ref, merged_ref, scratch):
    normed = layer_norm(hidden_ref[...] + arrived_ref[...].astype(jnp.float32), gain_ref[...])
    slabs = scratch.shape[0]
    for slab in range(slabs):
        scratch[slab] = normed[:, slab * 128 : (slab + 1) * 128]
    count = columns // 2
    for pair in range(normed.shape[0] // (2 * columns)):
        for parity in range(2):
            rows = [
                scratch[slab, pl.ds((2 * pair + parity) * columns + side, count, stride=2)]
                for side in range(2)
                for slab in range(slabs)
            ]
            merged = jnp.concatenate(rows, axis=1).astype(jnp.bfloat16)
            for tile in range(2):
                merged_ref[tile, parity, pl.ds(pair * count, count)] = merged


def assemble_kernel(spots_ref, *refs):
    block_refs, rows_ref, arrivals = refs[:-2], refs[-2], refs[-1]
    copies = []
    for number, block_ref in enumerate(block_refs):
        size = block_ref.shape[0]
        spot = pl.ds(pl.multiple_of(spots_ref[number] * size, size), size)
        copies.append(
            pltpu.make_async_copy(block_ref, rows_ref.at[spot], arrivals.at[number])
        )
    for copy in copies:
        copy.start()
    for copy in copies:
        copy.wait()


def assemble_rows(spots, blocks):
    size, width = blocks[0].shape
    return pl.pallas_call(
        assemble_kernel,
        out_shape=jax.ShapeDtypeStruct((len(blocks) * size, width), blocks[0].dtype),
        in_specs=[smem_spec] + [any_spec] * len(blocks),
        out_specs=vmem_spec,
        scratch_shapes=[pltpu.SemaphoreType.DMA((len(blocks),))],
        compiler_params=pltpu.CompilerParams(vmem_limit_bytes=16 * 2**20),
        cost_estimate=pl.CostEstimate(
            flops=0, bytes_accessed=4 * len(blocks) * size * width, transcendentals=0
        ),
        name="assemble_rows",
    )(spots, *blocks)


def projector_kernel(place_ref, rows_ref, weight_ref, own_out, far_out):
    mine, other = (
        jnp.concatenate([rows_ref[tile, place_ref[0] ^ half] for tile in range(2)], axis=0)
        for half in range(2)
    )
    total = jnp.dot(
        jnp.concatenate([mine, other], axis=0), weight_ref[...], preferred_element_type=jnp.float32
    )
    count = mine.shape[0]
    own_out[...] = total[:count]
    far_out[...] = total[count:].astype(jnp.bfloat16)


def run_projector(place, rows, weight):
    count, (depth, width) = rows.shape[2], weight.shape
    return pl.pallas_call(
        projector_kernel,
        out_shape=(
            jax.ShapeDtypeStruct((2 * count, width), jnp.float32),
            jax.ShapeDtypeStruct((2 * count, width), jnp.bfloat16),
        ),
        in_specs=[smem_spec] + [vmem_spec] * 2,
        out_specs=(vmem_spec, vmem_spec),
        compiler_params=pltpu.CompilerParams(vmem_limit_bytes=16 * 2**20),
        cost_estimate=pl.CostEstimate(
            flops=8 * count * width * depth, bytes_accessed=2 * width * depth, transcendentals=0
        ),
        name="projector",
    )(place, rows, weight)


def finish_kernel(own_ref, arrived_ref, gates_ref, out_ref):
    width = own_ref.shape[1]
    out_ref[:, :width] = (own_ref[...] + arrived_ref[...].astype(jnp.float32)).astype(jnp.bfloat16)
    out_ref[:, width:] = gates_ref[...]


def per_device_near(
    patches,
    norm1_gain,
    qkv_weight,
    qkv_bias,
    out_weight,
    out_bias,
    norm2_gain,
    proj_weight,
    moe_gain,
    expert_in,
    expert_out,
    shared_in,
    shared_out,
    routes,
    gates,
):
    experts_count = lax.axis_size(near_expert)
    outer = experts_count // 4
    swap = partial(near_swap, grid=(2, outer, 2, 2))
    tile_id = lax.axis_index("tile")
    expert_id = lax.axis_index(near_expert)
    outer_id, inner_id, core_id = expert_id // 4, (expert_id // 2) % 2, expert_id % 2
    row_count, columns, width_vit = patches.shape[1:]
    local_rows = row_count * columns
    token_count = local_rows // 4

    def by_place(place, mine, other):
        first = place == 0
        return jnp.where(first, mine, other), jnp.where(first, other, mine)

    def after(values, earlier):
        return lax.optimization_barrier((values, earlier))[0]

    own_patches = patches.reshape(local_rows, width_vit)
    other_patches = swap(own_patches, flips=(1, 0, 0, 0))
    tile_place = tile_id.astype(jnp.int32).reshape(1)

    top_count = routes.shape[-1]
    page_routes = routes.reshape(2, token_count, top_count)
    own_routes = lax.dynamic_index_in_dim(page_routes, tile_id, 0, keepdims=False)
    own_gates = gates.reshape(token_count, top_count)
    dense_gates = jnp.sum(
        jnp.where(
            own_routes[:, :, None] == jnp.arange(experts_count)[None, None, :],
            own_gates[:, :, None],
            0.0,
        ),
        axis=1,
    )
    gates_high = lax.reduce_precision(dense_gates, 8, 7)
    gate_lanes = jnp.concatenate([gates_high, dense_gates - gates_high], axis=1)
    gate_width = gate_lanes.shape[1]
    gate_lanes = jnp.pad(gate_lanes, ((0, 0), (0, 128 - gate_width))).astype(jnp.bfloat16)
    gate_rows = jnp.concatenate(
        by_place(tile_id, gate_lanes, jnp.zeros_like(gate_lanes)), axis=0
    )
    expert_lanes = jnp.arange(128) % experts_count == expert_id
    expert_lanes = (expert_lanes & (jnp.arange(128) < gate_width)).astype(jnp.float32)

    heads = qkv_weight.shape[2] // HD
    weight_rows = qkv_weight.transpose(1, 2, 0)
    bias_rows = qkv_bias[:, :, None]
    quarter = HD // 4
    feature = jnp.arange(HD)
    inverse = jnp.exp(
        (feature % quarter).astype(jnp.float32) * (-math.log(rope_base) / quarter)
    )[:, None]
    position = jnp.arange(local_rows)

    def tables(tile):
        rows = (tile * row_count + position // columns).astype(jnp.float32)[None]
        cols = (position % columns).astype(jnp.float32)[None]
        angles = jnp.where((feature < 2 * quarter)[:, None], rows, cols) * inverse
        return jnp.cos(angles), jnp.sin(angles)

    own_tables = tables(tile_id)
    gain_first, gain_second = norm1_gain[None], norm2_gain[None]
    head_rows = (heads, HD, local_rows)
    params = pltpu.CompilerParams(vmem_limit_bytes=16 * 2**20)
    macs = local_rows * width_vit * heads * HD
    own_heads = pl.pallas_call(
        partial(own_heads_kernel, heads),
        out_shape=jax.ShapeDtypeStruct((3, *head_rows), jnp.bfloat16),
        in_specs=[vmem_spec] * 6,
        out_specs=vmem_spec,
        compiler_params=params,
        cost_estimate=pl.CostEstimate(
            flops=6 * macs, bytes_accessed=2 * weight_rows.size, transcendentals=0
        ),
        name="own_heads",
    )(own_patches, gain_first, bias_rows, *own_tables, weight_rows)
    other_part, keys_values = pl.pallas_call(
        partial(other_rows_kernel, heads),
        out_shape=(
            jax.ShapeDtypeStruct((local_rows, width_vit), jnp.bfloat16),
            jax.ShapeDtypeStruct((2, heads, HD, 2 * local_rows), jnp.bfloat16),
        ),
        in_specs=[vmem_spec] * 8,
        out_specs=(vmem_spec, vmem_spec),
        compiler_params=params,
        cost_estimate=pl.CostEstimate(
            flops=10 * macs, bytes_accessed=2 * weight_rows.size, transcendentals=0
        ),
        name="other_rows",
    )(
        other_patches,
        gain_first,
        bias_rows,
        *tables(1 - tile_id),
        weight_rows,
        own_heads,
        out_weight,
    )
    arrived_part = swap(other_part, flips=(1, 0, 0, 0))
    hidden = pl.pallas_call(
        partial(own_rows_kernel, heads),
        out_shape=jax.ShapeDtypeStruct((local_rows, width_vit), jnp.float32),
        in_specs=[vmem_spec] * 5,
        out_specs=vmem_spec,
        compiler_params=params,
        cost_estimate=pl.CostEstimate(
            flops=4 * macs, bytes_accessed=2 * out_weight.size, transcendentals=0
        ),
        name="own_rows",
    )(own_patches, own_heads, keys_values, out_weight, out_bias[None])
    merged = pl.pallas_call(
        partial(merge_kernel, columns),
        out_shape=jax.ShapeDtypeStruct((2, 2, token_count, 2 * width_vit), jnp.bfloat16),
        in_specs=[vmem_spec] * 3,
        out_specs=vmem_spec,
        scratch_shapes=[pltpu.VMEM((width_vit // 128, local_rows, 128), jnp.float32)],
        compiler_params=params,
        name="merge_windows",
    )(hidden, arrived_part, gain_second)

    proj_blocks, proj_spots = [], []
    held_rows = after(proj_weight, own_tables)
    for low in range(outer // 2):
        for inner in range(2):
            rows = swap(held_rows, flips=(0, low, inner, 0)) if low or inner else proj_weight
            for core, block in enumerate(
                (rows, swap(after(rows, merged), flips=(0, 0, 0, 1)))
            ):
                proj_blocks.append(block)
                proj_spots.append(
                    ((outer_id ^ low) % (outer // 2)) * 4
                    + (inner_id ^ inner) * 2
                    + (core_id ^ core)
                )
    proj_spots = jnp.stack(proj_spots).astype(jnp.int32)

    far = outer // 2
    merged = lax.all_to_all(
        merged.reshape(4, token_count, -1), ("tile", "half"), split_axis=0, concat_axis=0, tiled=True
    ).reshape(merged.shape)
    page_tokens = 2 * token_count
    half_place = (outer_id // far).astype(jnp.int32).reshape(1)
    own_tokens, far_tokens = run_projector(
        half_place, merged, assemble_rows(proj_spots, proj_blocks)
    )
    far_part = swap(far_tokens, flips=(0, far, 0, 0))
    tokens_half = (own_tokens + far_part.astype(jnp.float32)).astype(jnp.bfloat16)

    width_moe = 2 * tokens_half.shape[1]
    expert_units = expert_in[0].transpose(1, 2, 0)
    shared_units = shared_in.transpose(1, 2, 0)
    gain_row, lane_row = moe_gain[None], expert_lanes[None]
    half_moe = tokens_half.shape[1]
    held = jnp.concatenate([tokens_half, gate_rows], axis=1)
    held_by_step = [held] + [swap(held, flips=(0, step, 0, 0)) for step in range(1, outer)]
    tile_flip, inner_flip, core_flip = (1, 0, 0, 0), (0, 0, 1, 0), (0, 0, 0, 1)
    def add(mine, other):
        return (mine.astype(jnp.float32) + other.astype(jnp.float32)).astype(jnp.bfloat16)

    flips_of = [
        (inner_flip, tile_flip) if step % 2 else (tile_flip, inner_flip) for step in range(outer)
    ]
    near_blocks, first_sums, kept_sums = [], [], []
    for step, held in enumerate(held_by_step):
        if step in ():
            over_tile, over_inner, over_both = (
                swap(held, flips=flip) for flip in (tile_flip, inner_flip, (1, 0, 1, 0))
            )
            near_blocks.append(
                jnp.stack([held, over_tile, over_inner, over_both]).reshape(2, 2, *held.shape)
            )
            continue
        arrived = swap(held, flips=flips_of[step][0])
        if step == 0:
            own_held, tile_held = held, arrived
        held = jnp.stack([held, arrived])
        held = jnp.stack([held, swap(held, flips=flips_of[step][1])])
        near_blocks.append(held.transpose(1, 0, 2, 3) if step % 2 else held)
    residual = jnp.concatenate(
        by_place(
            tile_id,
            *(
                lax.dynamic_slice_in_dim(
                    rows[:, :half_moe], tile_id * token_count, token_count, 0
                )
                for rows in (own_held, tile_held)
            ),
        ),
        axis=1,
    )
    shared_sums = run_shared(
        tile_place, after(own_held, near_blocks[0]), tile_held, gain_row, shared_units, shared_out
    )
    across_blocks = [swap(near, flips=core_flip) for near in near_blocks]
    for step, (near, across) in enumerate(zip(near_blocks, across_blocks)):
        if step == 3:
            near = after(near, first_sums[1])
        own_sums, across_sums = run_expert(
            tile_place,
            near,
            across,
            gain_row,
            lane_row,
            expert_units,
            expert_out[0],
            None if step else shared_sums,
        )
        summed = add(own_sums, swap(across_sums, flips=core_flip)).reshape(
            2, 2, token_count, width_moe
        )
        if step % 2 and step not in (2, 3):
            stays, leaves = summed[0], summed[1]
        else:
            stays, leaves = by_place(tile_id, summed[:, 0], summed[:, 1])
        first_sums.append(leaves)
        kept_sums.append(stays)
    total = residual.astype(jnp.float32)
    for step, (stays, leaves) in enumerate(zip(kept_sums, first_sums)):
        if step in (2, 3):
            summed = (
                stays[0].astype(jnp.float32)
                + swap(leaves[0], flips=tile_flip).astype(jnp.float32)
                + swap(stays[1], flips=inner_flip).astype(jnp.float32)
                + swap(leaves[1], flips=(1, 0, 1, 0)).astype(jnp.float32)
            ).astype(jnp.bfloat16)
        else:
            summed = add(stays, swap(leaves, flips=flips_of[step][0]))
            if step % 2:
                stays, leaves = by_place(tile_id, summed[0], summed[1])
            else:
                stays, leaves = summed[0], summed[1]
            summed = add(stays, swap(leaves, flips=flips_of[step][1]))
        if step:
            summed = swap(summed, flips=(0, step, 0, 0))
        total = total + summed.astype(jnp.float32)
    return total.astype(jnp.bfloat16).reshape(1, row_count // 2, columns // 2, width_moe)


def solution(mesh):
    expert = "expert"
    near = mesh.shape["tile"] == 2 and mesh.shape["expert"] == 16
    if near:
        mesh = jax.sharding.Mesh(mesh.devices.reshape(2, 2, 2, 2, 2), ("tile", *near_expert))
        expert = near_expert
    placed = (
        P(expert, "tile", None, None),
        P(),
        P(None, None, "tile"),
        P(None, "tile"),
        P("tile", None),
        P(),
        P(),
        P(expert, "tile"),
        P(),
        P(expert, None, None, "tile"),
        P(expert, "tile", None),
        P(None, None, "tile"),
        P("tile", None),
        P(expert, None, None, None),
        P(expert, "tile", None, None),
    )
    return jax.shard_map(
        per_device_near if near else per_device_slots,
        mesh=mesh,
        in_specs=placed,
        out_specs=P(expert, "tile", None, None),
        check_vma=False,
    )
```

```python
from functools import partial
import math

import jax
import jax.numpy as jnp
from jax import lax
from jax.experimental import pallas as pl
from jax.experimental.pallas import tpu as pltpu
from jax.sharding import PartitionSpec as P

HD = 72


norm_eps = 1e-06
rope_base = 10000.0


def layer_norm(values, gain_vec):
    centre = values - jnp.mean(values, axis=-1, keepdims=True)
    spread = jnp.mean(centre * centre, axis=-1, keepdims=True)
    return centre * lax.rsqrt(spread + norm_eps) * gain_vec


def rms_norm(values, gain_vec):
    return (
        values * lax.rsqrt(jnp.mean(values * values, axis=-1, keepdims=True) + norm_eps) * gain_vec
    )


def rope_tables(positions, columns, head_size):
    quarter = head_size // 4
    inverse = jnp.exp(jnp.arange(quarter).astype(jnp.float32) * (-math.log(rope_base) / quarter))
    row_angle = (positions // columns).astype(jnp.float32)[:, None] * inverse[None, :]
    col_angle = (positions % columns).astype(jnp.float32)[:, None] * inverse[None, :]
    return (jnp.cos(row_angle), jnp.sin(row_angle), jnp.cos(col_angle), jnp.sin(col_angle))


def rotate(values, tables):
    cos_row, sin_row, cos_col, sin_col = tables
    quarter = values.shape[-1] // 4
    row_a = values[..., :quarter]
    row_b = values[..., quarter : 2 * quarter]
    col_a = values[..., 2 * quarter : 3 * quarter]
    col_b = values[..., 3 * quarter :]
    return jnp.concatenate(
        [
            row_a * cos_row[:, None] - row_b * sin_row[:, None],
            row_b * cos_row[:, None] + row_a * sin_row[:, None],
            col_a * cos_col[:, None] - col_b * sin_col[:, None],
            col_b * cos_col[:, None] + col_a * sin_col[:, None],
        ],
        axis=-1,
    )


def attend(query_rows, key_rows, value_rows, divisor):
    count = query_rows.shape[0]
    width = min(count, 512)
    blocks = query_rows.reshape(count // width, width, query_rows.shape[1], query_rows.shape[2])

    def one_block(block):
        scores = (
            jnp.einsum("qhd,khd->hqk", block, key_rows, preferred_element_type=jnp.float32)
            / divisor
        )
        weights = jax.nn.softmax(scores, axis=-1).astype(jnp.bfloat16)
        return jnp.einsum(
            "hqk,khd->qhd", weights, value_rows, preferred_element_type=jnp.float32
        ).astype(jnp.bfloat16)

    return lax.map(one_block, blocks).reshape(count, -1)


def block_slots(block_routes, experts_count, capacity):
    picks = block_routes.reshape(-1)
    onehot = (picks[:, None] == jnp.arange(experts_count)[None, :]).astype(jnp.int32)
    earlier = jnp.cumsum(onehot, axis=0) - onehot
    ranks = jnp.sum(earlier * onehot, axis=1)
    owners_flat = jnp.arange(picks.shape[0]) // block_routes.shape[1]
    table = (
        jnp.full((experts_count * capacity,), -1, dtype=jnp.int32)
        .at[picks * capacity + ranks]
        .set(owners_flat)
    )
    return (ranks.reshape(block_routes.shape), table.reshape(experts_count, capacity))


def per_device_slots(
    patches,
    norm1_gain,
    qkv_weight,
    qkv_bias,
    out_weight,
    out_bias,
    norm2_gain,
    proj_weight,
    moe_gain,
    expert_in,
    expert_out,
    shared_in,
    shared_out,
    routes,
    gates,
):
    tiles = lax.axis_size("tile")
    experts_count = lax.axis_size("expert")
    tile_id = lax.axis_index("tile")
    row_count = patches.shape[1]
    columns = patches.shape[2]
    width_vit = patches.shape[3]
    local_rows = row_count * columns
    inputs = patches.reshape(local_rows, width_vit).astype(jnp.float32)
    normed = layer_norm(inputs, norm1_gain).astype(jnp.bfloat16)
    heads_here = qkv_weight.shape[2] // HD
    qkv_flat = qkv_weight.reshape(width_vit, -1)
    bias_rows = qkv_bias.reshape(1, 3, heads_here, HD)
    piece = lax.all_gather(normed, "tile", axis=0, tiled=True)
    mixed = (
        jnp.dot(piece, qkv_flat, preferred_element_type=jnp.float32).reshape(
            piece.shape[0], 3, heads_here, HD
        )
        + bias_rows
    )
    tables = rope_tables(jnp.arange(piece.shape[0]), columns, HD)
    page_qkv = jnp.stack(
        [rotate(mixed[:, 0], tables), rotate(mixed[:, 1], tables), mixed[:, 2]], axis=1
    ).astype(jnp.bfloat16)
    attended = attend(page_qkv[:, 0], page_qkv[:, 1], page_qkv[:, 2], math.sqrt(HD))
    mixed_heads = lax.psum_scatter(
        jnp.dot(attended, out_weight, preferred_element_type=jnp.float32).astype(jnp.bfloat16),
        "tile",
        scatter_dimension=0,
        tiled=True,
    ).astype(jnp.float32)
    hidden = inputs + mixed_heads + out_bias
    normed_out = layer_norm(hidden, norm2_gain).astype(jnp.bfloat16)
    merged = (
        normed_out.reshape(row_count // 2, 2, columns // 2, 2, width_vit)
        .transpose(0, 2, 1, 3, 4)
        .reshape(-1, 4 * width_vit)
    )
    merged_count = merged.shape[0]
    group_merged = lax.all_gather(merged, "tile", axis=0, tiled=True)
    projected = jnp.dot(
        group_merged,
        lax.all_gather(proj_weight, "expert", axis=0, tiled=True),
        preferred_element_type=jnp.float32,
    ).astype(jnp.bfloat16)
    tokens_moe = lax.all_to_all(projected, "tile", split_axis=0, concat_axis=1, tiled=True)
    width_moe = tokens_moe.shape[1]
    moe_in = rms_norm(tokens_moe.astype(jnp.float32), moe_gain).astype(jnp.bfloat16)
    group_in = lax.all_gather(moe_in, "tile", axis=0, tiled=True)
    shared_gated = jnp.dot(
        group_in, shared_in.reshape(width_moe, -1), preferred_element_type=jnp.float32
    ).reshape(group_in.shape[0], 2, -1)
    shared_hidden = (jax.nn.silu(shared_gated[:, 0]) * shared_gated[:, 1]).astype(jnp.bfloat16)
    shared_part = lax.psum_scatter(
        jnp.dot(shared_hidden, shared_out, preferred_element_type=jnp.float32).astype(jnp.bfloat16),
        "tile",
        scatter_dimension=0,
        tiled=True,
    ).astype(jnp.float32)
    top_count = routes.shape[-1]
    capacity = max(2, min(merged_count, 2 * merged_count * top_count // experts_count))
    group_routes = routes.reshape(tiles, merged_count, top_count)
    group_ranks, group_owners = jax.vmap(
        partial(block_slots, experts_count=experts_count, capacity=capacity)
    )(group_routes)
    own_routes = lax.dynamic_index_in_dim(group_routes, tile_id, 0, keepdims=False)
    own_ranks = lax.dynamic_index_in_dim(group_ranks, tile_id, 0, keepdims=False)
    empty_value = jnp.zeros((), jnp.bfloat16)
    table = lax.dynamic_index_in_dim(group_owners, tile_id, 0, keepdims=False)
    used = table >= 0
    outgoing = jnp.where(used[..., None], moe_in[jnp.where(used, table, 0)], empty_value)
    received = lax.all_to_all(outgoing, "expert", split_axis=0, concat_axis=0, tiled=True)
    arrived = lax.all_gather(received[:, None], "tile", axis=1, tiled=True)
    slot_rows = arrived.reshape(-1, width_moe)
    gated = jnp.dot(
        slot_rows, expert_in.reshape(width_moe, -1), preferred_element_type=jnp.float32
    ).reshape(slot_rows.shape[0], 2, -1)
    expert_hidden = (jax.nn.silu(gated[:, 0]) * gated[:, 1]).astype(jnp.bfloat16)
    partial_out = (
        jnp.dot(
            expert_hidden,
            expert_out.reshape(expert_hidden.shape[1], width_moe),
            preferred_element_type=jnp.float32,
        )
        .astype(jnp.bfloat16)
        .reshape(arrived.shape)
    )
    came_back = lax.all_to_all(partial_out, "expert", split_axis=0, concat_axis=0, tiled=True)
    returned = lax.psum_scatter(
        came_back.astype(jnp.float32).astype(jnp.bfloat16), "tile", scatter_dimension=1, tiled=True
    )
    results_flat = returned.reshape(experts_count * capacity, width_moe)
    pick_index = own_routes * capacity + own_ranks
    gate_rows = gates.reshape(merged_count, top_count)
    routed = jnp.zeros((merged_count, width_moe), jnp.float32)
    for position in range(top_count):
        routed = routed + gate_rows[:, position : position + 1] * results_flat[
            pick_index[:, position]
        ].astype(jnp.float32)
    output = tokens_moe.astype(jnp.float32) + shared_part + routed
    return output.astype(jnp.bfloat16).reshape(1, row_count // 2, columns // 2, width_moe)


near_expert = ("half", "outer", "inner", "core")


def near_swap(values, grid, flips):
    pairs = []
    for source in range(math.prod(grid)):
        place, rest = [], source
        for size in reversed(grid):
            place.append(rest % size)
            rest //= size
        target = 0
        for spot, size, flip in zip(reversed(place), grid, flips):
            target = target * size + (spot ^ flip)
        pairs.append((source, target))
    return lax.ppermute(values, ("tile", *near_expert), pairs)


def expert_sums(normed, in_ref, back_ref):
    units = back_ref.shape[0]
    wide = (((1,), (1,)), ((), ()))
    total = None
    for begin in range(0, units, 256):
        rows = pl.ds(begin, min(256, units - begin))
        gate = lax.dot_general(normed, in_ref[0, rows], wide, preferred_element_type=jnp.float32)
        up = lax.dot_general(normed, in_ref[1, rows], wide, preferred_element_type=jnp.float32)
        hidden = (gate / (1.0 + jnp.exp(-gate)) * up).astype(jnp.bfloat16)
        part = jnp.dot(hidden, back_ref[rows], preferred_element_type=jnp.float32)
        total = part if total is None else total + part
    return total


def norm_pages(place_ref, page_refs, gain_ref, lanes_ref, normed, weights):
    half = normed.shape[1] // 2
    first = pl.multiple_of(place_ref[0] * half, half)
    second = pl.multiple_of((1 - place_ref[0]) * half, half)
    for number, (mine_ref, other_ref) in enumerate(page_refs):
        mine = mine_ref[:, :half].astype(jnp.float32)
        other = other_ref[:, :half].astype(jnp.float32)
        squares = jnp.sum(mine * mine, axis=1, keepdims=True) + jnp.sum(
            other * other, axis=1, keepdims=True
        )
        scale = lax.rsqrt(squares / (2 * half) + norm_eps)
        count = mine.shape[0]
        rows = pl.ds(number * count, count)
        normed[rows, pl.ds(first, half)] = (mine * scale * gain_ref[:, pl.ds(first, half)]).astype(
            jnp.bfloat16
        )
        normed[rows, pl.ds(second, half)] = (
            other * scale * gain_ref[:, pl.ds(second, half)]
        ).astype(jnp.bfloat16)
        if weights is not None:
            lanes = mine_ref[:, half:].astype(jnp.float32) + other_ref[:, half:].astype(jnp.float32)
            weights[rows] = jnp.sum(lanes * lanes_ref[...], axis=1, keepdims=True)


def expert_kernel(extra, *refs):
    place_ref, near_ref, across_ref, gain_ref, lanes_ref, in_ref, back_ref = refs[:7]
    extra_ref = refs[7] if extra else None
    own_out, across_out, normed, weights = refs[7 + extra :]
    page_refs = [
        (ref.at[inner, 0], ref.at[inner, 1]) for ref in (near_ref, across_ref) for inner in range(2)
    ]
    norm_pages(place_ref, page_refs, gain_ref, lanes_ref, normed, weights)
    total = expert_sums(normed[...], in_ref, back_ref) * weights[...]
    count = total.shape[0] // 4
    for page in range(4):
        rows = total[page * count : (page + 1) * count]
        if extra and page == 0:
            rows = rows + extra_ref[...]
        target = own_out if page < 2 else across_out
        target[page % 2] = rows.astype(jnp.bfloat16)


def shared_kernel(place_ref, mine_ref, other_ref, gain_ref, in_ref, back_ref, out_ref, normed):
    norm_pages(place_ref, [(mine_ref, other_ref)], gain_ref, None, normed, None)
    out_ref[...] = expert_sums(normed[...], in_ref, back_ref)


vmem_spec = pl.BlockSpec(memory_space=pltpu.VMEM)
smem_spec = pl.BlockSpec(memory_space=pltpu.SMEM)
any_spec = pl.BlockSpec(memory_space=pl.ANY)


def expert_cost(rows, units, width):
    return pl.CostEstimate(
        flops=6 * rows * units * width,
        bytes_accessed=6 * units * width + 4 * rows * width,
        transcendentals=rows * units,
    )


def run_expert(tile_place, near, across, gain, lanes, in_rows, back_rows, extra):
    units, width = back_rows.shape
    page_rows = near.shape[2]
    rows = 4 * page_rows
    out = jax.ShapeDtypeStruct((2, page_rows, width), jnp.bfloat16)
    return pl.pallas_call(
        partial(expert_kernel, extra is not None),
        out_shape=(out, out),
        in_specs=[smem_spec] + [vmem_spec] * (6 + (extra is not None)),
        out_specs=(vmem_spec, vmem_spec),
        scratch_shapes=[
            pltpu.VMEM((rows, width), jnp.bfloat16),
            pltpu.VMEM((rows, 1), jnp.float32),
        ],
        compiler_params=pltpu.CompilerParams(vmem_limit_bytes=16 * 2**20),
        cost_estimate=expert_cost(rows, units, width),
        name="expert_units",
    )(
        tile_place,
        near,
        across,
        gain,
        lanes,
        in_rows,
        back_rows,
        *(() if extra is None else (extra,)),
    )


def run_shared(tile_place, mine, other, gain, in_rows, back_rows):
    units, width = back_rows.shape
    rows = mine.shape[0]
    return pl.pallas_call(
        shared_kernel,
        out_shape=jax.ShapeDtypeStruct((rows, width), jnp.float32),
        in_specs=[smem_spec] + [vmem_spec] * 5,
        out_specs=vmem_spec,
        scratch_shapes=[
            pltpu.VMEM((rows, width), jnp.bfloat16),
        ],
        compiler_params=pltpu.CompilerParams(vmem_limit_bytes=16 * 2**20),
        cost_estimate=expert_cost(rows, units, width),
        name="shared_units",
    )(tile_place, mine, other, gain, in_rows, back_rows)


def project_heads(rows_ref, gain_ref, weight_ref, bias_ref, cos_ref, sin_ref, heads):
    normed = layer_norm(rows_ref[...].astype(jnp.float32), gain_ref[...]).astype(jnp.bfloat16)
    quarter = HD // 4
    outs = []
    for which in range(3):
        mixed = (
            lax.dot_general(
                weight_ref[which],
                normed,
                (((1,), (1,)), ((), ())),
                preferred_element_type=jnp.float32,
            )
            + jnp.broadcast_to(bias_ref[which : which + 1], (normed.shape[0], heads * HD)).T
        ).reshape(heads, HD, normed.shape[0])
        if which < 2:
            parts = [mixed[:, n * quarter : (n + 1) * quarter] for n in range(4)]
            partner = jnp.concatenate([-parts[1], parts[0], -parts[3], parts[2]], axis=1)
            mixed = mixed * cos_ref[...][None] + partner * sin_ref[...][None]
        outs.append(mixed.astype(jnp.bfloat16))
    return outs


def attend_heads(query, keys, values, heads):
    turned = (((0,), (0,)), ((), ()))
    outs = []
    for head in range(heads):
        scores = lax.dot_general(
            keys[head], query[head], turned, preferred_element_type=jnp.float32
        ) * (1.0 / math.sqrt(HD))
        raised = jnp.exp(scores - jnp.max(scores, axis=0, keepdims=True))
        probs = (raised / jnp.sum(raised, axis=0, keepdims=True)).astype(jnp.bfloat16)
        outs.append(jnp.dot(values[head], probs, preferred_element_type=jnp.float32))
    return jnp.concatenate(outs, axis=0).astype(jnp.bfloat16)


def own_heads_kernel(heads, *refs):
    rows_ref, gain_ref, bias_ref, cos_ref, sin_ref, weight_ref, out_ref = refs
    outs = project_heads(rows_ref, gain_ref, weight_ref, bias_ref, cos_ref, sin_ref, heads)
    for which, values in enumerate(outs):
        out_ref[which] = values


def other_rows_kernel(heads, *refs):
    rows_ref, gain_ref, bias_ref, cos_ref, sin_ref, weight_ref, own_ref, back_ref = refs[:8]
    part_ref, keys_ref = refs[8:]
    query, other_keys, other_values = project_heads(
        rows_ref, gain_ref, weight_ref, bias_ref, cos_ref, sin_ref, heads
    )
    keys = jnp.concatenate([own_ref[1], other_keys], axis=2)
    values = jnp.concatenate([own_ref[2], other_values], axis=2)
    keys_ref[0] = keys
    keys_ref[1] = values
    attended = attend_heads(query, keys, values, heads)
    part_ref[...] = lax.dot_general(
        attended, back_ref[...], (((0,), (0,)), ((), ())), preferred_element_type=jnp.float32
    ).astype(jnp.bfloat16)


def own_rows_kernel(heads, *refs):
    rows_ref, own_ref, keys_ref, back_ref, bias_ref, out_ref = refs
    attended = attend_heads(own_ref[0], keys_ref[0], keys_ref[1], heads)
    out_ref[...] = (
        rows_ref[...].astype(jnp.float32)
        + bias_ref[...]
        + lax.dot_general(
            attended, back_ref[...], (((0,), (0,)), ((), ())), preferred_element_type=jnp.float32
        )
    )


def merge_kernel(columns, hidden_ref, arrived_ref, gain_ref, merged_ref, scratch):
    normed = layer_norm(hidden_ref[...] + arrived_ref[...].astype(jnp.float32), gain_ref[...])
    slabs = scratch.shape[0]
    for slab in range(slabs):
        scratch[slab] = normed[:, slab * 128 : (slab + 1) * 128]
    count = columns // 2
    for pair in range(normed.shape[0] // (2 * columns)):
        for parity in range(2):
            rows = [
                scratch[slab, pl.ds((2 * pair + parity) * columns + side, count, stride=2)]
                for side in range(2)
                for slab in range(slabs)
            ]
            merged = jnp.concatenate(rows, axis=1).astype(jnp.bfloat16)
            for tile in range(2):
                merged_ref[tile, parity, pl.ds(pair * count, count)] = merged


def assemble_kernel(spots_ref, *refs):
    block_refs, rows_ref, arrivals = refs[:-2], refs[-2], refs[-1]
    copies = []
    for number, block_ref in enumerate(block_refs):
        size = block_ref.shape[0]
        spot = pl.ds(pl.multiple_of(spots_ref[number] * size, size), size)
        copies.append(
            pltpu.make_async_copy(block_ref, rows_ref.at[spot], arrivals.at[number])
        )
    for copy in copies:
        copy.start()
    for copy in copies:
        copy.wait()


def assemble_rows(spots, blocks):
    size, width = blocks[0].shape
    return pl.pallas_call(
        assemble_kernel,
        out_shape=jax.ShapeDtypeStruct((len(blocks) * size, width), blocks[0].dtype),
        in_specs=[smem_spec] + [any_spec] * len(blocks),
        out_specs=vmem_spec,
        scratch_shapes=[pltpu.SemaphoreType.DMA((len(blocks),))],
        compiler_params=pltpu.CompilerParams(vmem_limit_bytes=16 * 2**20),
        cost_estimate=pl.CostEstimate(
            flops=0, bytes_accessed=4 * len(blocks) * size * width, transcendentals=0
        ),
        name="assemble_rows",
    )(spots, *blocks)


def projector_kernel(place_ref, rows_ref, weight_ref, own_out, far_out):
    mine, other = (
        jnp.concatenate([rows_ref[tile, place_ref[0] ^ half] for tile in range(2)], axis=0)
        for half in range(2)
    )
    total = jnp.dot(
        jnp.concatenate([mine, other], axis=0), weight_ref[...], preferred_element_type=jnp.float32
    )
    count = mine.shape[0]
    own_out[...] = total[:count]
    far_out[...] = total[count:].astype(jnp.bfloat16)


def run_projector(place, rows, weight):
    count, (depth, width) = rows.shape[2], weight.shape
    return pl.pallas_call(
        projector_kernel,
        out_shape=(
            jax.ShapeDtypeStruct((2 * count, width), jnp.float32),
            jax.ShapeDtypeStruct((2 * count, width), jnp.bfloat16),
        ),
        in_specs=[smem_spec] + [vmem_spec] * 2,
        out_specs=(vmem_spec, vmem_spec),
        compiler_params=pltpu.CompilerParams(vmem_limit_bytes=16 * 2**20),
        cost_estimate=pl.CostEstimate(
            flops=8 * count * width * depth, bytes_accessed=2 * width * depth, transcendentals=0
        ),
        name="projector",
    )(place, rows, weight)


def finish_kernel(own_ref, arrived_ref, gates_ref, out_ref):
    width = own_ref.shape[1]
    out_ref[:, :width] = (own_ref[...] + arrived_ref[...].astype(jnp.float32)).astype(jnp.bfloat16)
    out_ref[:, width:] = gates_ref[...]


def per_device_near(
    patches,
    norm1_gain,
    qkv_weight,
    qkv_bias,
    out_weight,
    out_bias,
    norm2_gain,
    proj_weight,
    moe_gain,
    expert_in,
    expert_out,
    shared_in,
    shared_out,
    routes,
    gates,
):
    experts_count = lax.axis_size(near_expert)
    outer = experts_count // 4
    swap = partial(near_swap, grid=(2, outer, 2, 2))
    tile_id = lax.axis_index("tile")
    expert_id = lax.axis_index(near_expert)
    outer_id, inner_id, core_id = expert_id // 4, (expert_id // 2) % 2, expert_id % 2
    row_count, columns, width_vit = patches.shape[1:]
    local_rows = row_count * columns
    token_count = local_rows // 4

    def by_place(place, mine, other):
        first = place == 0
        return jnp.where(first, mine, other), jnp.where(first, other, mine)

    def after(values, earlier):
        return lax.optimization_barrier((values, earlier))[0]

    own_patches = patches.reshape(local_rows, width_vit)
    other_patches = swap(own_patches, flips=(1, 0, 0, 0))
    tile_place = tile_id.astype(jnp.int32).reshape(1)

    top_count = routes.shape[-1]
    page_routes = routes.reshape(2, token_count, top_count)
    own_routes = lax.dynamic_index_in_dim(page_routes, tile_id, 0, keepdims=False)
    own_gates = gates.reshape(token_count, top_count)
    dense_gates = jnp.sum(
        jnp.where(
            own_routes[:, :, None] == jnp.arange(experts_count)[None, None, :],
            own_gates[:, :, None],
            0.0,
        ),
        axis=1,
    )
    gates_high = lax.reduce_precision(dense_gates, 8, 7)
    gate_lanes = jnp.concatenate([gates_high, dense_gates - gates_high], axis=1)
    gate_width = gate_lanes.shape[1]
    gate_lanes = jnp.pad(gate_lanes, ((0, 0), (0, 128 - gate_width))).astype(jnp.bfloat16)
    gate_rows = jnp.concatenate(
        by_place(tile_id, gate_lanes, jnp.zeros_like(gate_lanes)), axis=0
    )
    expert_lanes = jnp.arange(128) % experts_count == expert_id
    expert_lanes = (expert_lanes & (jnp.arange(128) < gate_width)).astype(jnp.float32)

    heads = qkv_weight.shape[2] // HD
    weight_rows = qkv_weight.transpose(1, 2, 0)
    bias_rows = qkv_bias
    quarter = HD // 4
    feature = jnp.arange(HD)
    inverse = jnp.exp(
        (feature % quarter).astype(jnp.float32) * (-math.log(rope_base) / quarter)
    )[:, None]
    position = jnp.arange(local_rows)

    def tables(tile):
        rows = (tile * row_count + position // columns).astype(jnp.float32)[None]
        cols = (position % columns).astype(jnp.float32)[None]
        angles = jnp.where((feature < 2 * quarter)[:, None], rows, cols) * inverse
        return jnp.cos(angles), jnp.sin(angles)

    own_tables = tables(tile_id)
    gain_first, gain_second = norm1_gain[None], norm2_gain[None]
    head_rows = (heads, HD, local_rows)
    params = pltpu.CompilerParams(vmem_limit_bytes=16 * 2**20)
    macs = local_rows * width_vit * heads * HD
    own_heads = pl.pallas_call(
        partial(own_heads_kernel, heads),
        out_shape=jax.ShapeDtypeStruct((3, *head_rows), jnp.bfloat16),
        in_specs=[vmem_spec] * 6,
        out_specs=vmem_spec,
        compiler_params=params,
        cost_estimate=pl.CostEstimate(
            flops=6 * macs, bytes_accessed=2 * weight_rows.size, transcendentals=0
        ),
        name="own_heads",
    )(own_patches, gain_first, bias_rows, *own_tables, weight_rows)
    other_part, keys_values = pl.pallas_call(
        partial(other_rows_kernel, heads),
        out_shape=(
            jax.ShapeDtypeStruct((local_rows, width_vit), jnp.bfloat16),
            jax.ShapeDtypeStruct((2, heads, HD, 2 * local_rows), jnp.bfloat16),
        ),
        in_specs=[vmem_spec] * 8,
        out_specs=(vmem_spec, vmem_spec),
        compiler_params=params,
        cost_estimate=pl.CostEstimate(
            flops=10 * macs, bytes_accessed=2 * weight_rows.size, transcendentals=0
        ),
        name="other_rows",
    )(
        other_patches,
        gain_first,
        bias_rows,
        *tables(1 - tile_id),
        weight_rows,
        own_heads,
        out_weight,
    )
    arrived_part = swap(other_part, flips=(1, 0, 0, 0))
    hidden = pl.pallas_call(
        partial(own_rows_kernel, heads),
        out_shape=jax.ShapeDtypeStruct((local_rows, width_vit), jnp.float32),
        in_specs=[vmem_spec] * 5,
        out_specs=vmem_spec,
        compiler_params=params,
        cost_estimate=pl.CostEstimate(
            flops=4 * macs, bytes_accessed=2 * out_weight.size, transcendentals=0
        ),
        name="own_rows",
    )(own_patches, own_heads, keys_values, out_weight, out_bias[None])
    merged = pl.pallas_call(
        partial(merge_kernel, columns),
        out_shape=jax.ShapeDtypeStruct((2, 2, token_count, 2 * width_vit), jnp.bfloat16),
        in_specs=[vmem_spec] * 3,
        out_specs=vmem_spec,
        scratch_shapes=[pltpu.VMEM((width_vit // 128, local_rows, 128), jnp.float32)],
        compiler_params=params,
        name="merge_windows",
    )(hidden, arrived_part, gain_second)

    proj_blocks, proj_spots = [], []
    held_rows = after(proj_weight, own_tables)
    for low in range(outer // 2):
        for inner in range(2):
            rows = swap(held_rows, flips=(0, low, inner, 0)) if low or inner else proj_weight
            for core, block in enumerate(
                (rows, swap(after(rows, merged), flips=(0, 0, 0, 1)))
            ):
                proj_blocks.append(block)
                proj_spots.append(
                    ((outer_id ^ low) % (outer // 2)) * 4
                    + (inner_id ^ inner) * 2
                    + (core_id ^ core)
                )
    proj_spots = jnp.stack(proj_spots).astype(jnp.int32)

    far = outer // 2
    merged = lax.all_to_all(
        merged.reshape(4, token_count, -1), ("tile", "half"), split_axis=0, concat_axis=0, tiled=True
    ).reshape(merged.shape)
    page_tokens = 2 * token_count
    half_place = (outer_id // far).astype(jnp.int32).reshape(1)
    own_tokens, far_tokens = run_projector(
        half_place, merged, assemble_rows(proj_spots, proj_blocks)
    )
    far_part = swap(far_tokens, flips=(0, far, 0, 0))
    tokens_half = (own_tokens + far_part.astype(jnp.float32)).astype(jnp.bfloat16)

    width_moe = 2 * tokens_half.shape[1]
    expert_units = expert_in[0].transpose(1, 2, 0)
    shared_units = shared_in.transpose(1, 2, 0)
    gain_row, lane_row = moe_gain[None], expert_lanes[None]
    half_moe = tokens_half.shape[1]
    held = jnp.concatenate([tokens_half, gate_rows], axis=1)
    held_by_step = [held] + [swap(held, flips=(0, step, 0, 0)) for step in range(1, outer)]
    tile_flip, inner_flip, core_flip = (1, 0, 0, 0), (0, 0, 1, 0), (0, 0, 0, 1)
    def add(mine, other):
        return (mine.astype(jnp.float32) + other.astype(jnp.float32)).astype(jnp.bfloat16)

    flips_of = [
        (inner_flip, tile_flip) if step % 2 else (tile_flip, inner_flip) for step in range(outer)
    ]
    near_blocks, first_sums, kept_sums = [], [], []
    for step, held in enumerate(held_by_step):
        if step in ():
            over_tile, over_inner, over_both = (
                swap(held, flips=flip) for flip in (tile_flip, inner_flip, (1, 0, 1, 0))
            )
            near_blocks.append(
                jnp.stack([held, over_tile, over_inner, over_both]).reshape(2, 2, *held.shape)
            )
            continue
        arrived = swap(held, flips=flips_of[step][0])
        if step == 0:
            own_held, tile_held = held, arrived
        held = jnp.stack([held, arrived])
        held = jnp.stack([held, swap(held, flips=flips_of[step][1])])
        near_blocks.append(held.transpose(1, 0, 2, 3) if step % 2 else held)
    residual = jnp.concatenate(
        by_place(
            tile_id,
            *(
                lax.dynamic_slice_in_dim(
                    rows[:, :half_moe], tile_id * token_count, token_count, 0
                )
                for rows in (own_held, tile_held)
            ),
        ),
        axis=1,
    )
    shared_sums = run_shared(
        tile_place, after(own_held, near_blocks[0]), tile_held, gain_row, shared_units, shared_out
    )
    across_blocks = [swap(near, flips=core_flip) for near in near_blocks]
    for step, (near, across) in enumerate(zip(near_blocks, across_blocks)):
        if step == 3:
            near = after(near, first_sums[1])
        own_sums, across_sums = run_expert(
            tile_place,
            near,
            across,
            gain_row,
            lane_row,
            expert_units,
            expert_out[0],
            None if step else shared_sums,
        )
        summed = add(own_sums, swap(across_sums, flips=core_flip)).reshape(
            2, 2, token_count, width_moe
        )
        if step % 2 and step not in (2, 3):
            stays, leaves = summed[0], summed[1]
        else:
            stays, leaves = by_place(tile_id, summed[:, 0], summed[:, 1])
        first_sums.append(leaves)
        kept_sums.append(stays)
    total = residual.astype(jnp.float32)
    for step, (stays, leaves) in enumerate(zip(kept_sums, first_sums)):
        if step in (2, 3):
            summed = (
                stays[0].astype(jnp.float32)
                + swap(leaves[0], flips=tile_flip).astype(jnp.float32)
                + swap(stays[1], flips=inner_flip).astype(jnp.float32)
                + swap(leaves[1], flips=(1, 0, 1, 0)).astype(jnp.float32)
            ).astype(jnp.bfloat16)
        else:
            summed = add(stays, swap(leaves, flips=flips_of[step][0]))
            if step % 2:
                stays, leaves = by_place(tile_id, summed[0], summed[1])
            else:
                stays, leaves = summed[0], summed[1]
            summed = add(stays, swap(leaves, flips=flips_of[step][1]))
        if step:
            summed = swap(summed, flips=(0, step, 0, 0))
        total = total + summed.astype(jnp.float32)
    return total.astype(jnp.bfloat16).reshape(1, row_count // 2, columns // 2, width_moe)


def solution(mesh):
    expert = "expert"
    near = mesh.shape["tile"] == 2 and mesh.shape["expert"] == 16
    if near:
        mesh = jax.sharding.Mesh(mesh.devices.reshape(2, 2, 2, 2, 2), ("tile", *near_expert))
        expert = near_expert
    placed = (
        P(expert, "tile", None, None),
        P(),
        P(None, None, "tile"),
        P(None, "tile"),
        P("tile", None),
        P(),
        P(),
        P(expert, "tile"),
        P(),
        P(expert, None, None, "tile"),
        P(expert, "tile", None),
        P(None, None, "tile"),
        P("tile", None),
        P(expert, None, None, None),
        P(expert, "tile", None, None),
    )
    return jax.shard_map(
        per_device_near if near else per_device_slots,
        mesh=mesh,
        in_specs=placed,
        out_specs=P(expert, "tile", None, None),
        check_vma=False,
    )
```
